128 devices in a mesh: gx: 8 (over y, x_lo), gz: 16 (over x_hi, z, core).
Axes of the slice: x: 4 (x_hi: 2, x_lo: 2; x = x_hi * 2 + x_lo), y: 4, z: 4, core: 2. Of those that a mesh axis runs over, the one named last changes fastest.
Arguments:
- flow: float32 [4, 512, 1024, 128], P(None, 'gx', 'gz'), may hold values from -16 to 16
- dy_matrix: float32 [128, 128], replicated, may hold values from -0.5 to 0.5
Outputs:
- moments: float32 [40, 512, 128], P(None, 'gx')
The draws below stay inside these ranges and needn't reach their ends.
All inputs are finite; a program needn't handle non-finite values.
Results may differ from the reference program's by a relative error of at most 0.00012.
Values sent between devices are 32-bit elements; how exact they have to be, the bound alone decides.
No kernel may reach another device: no remote copies, remote signals or barrier semaphores. Data moves between devices by JAX's collectives and lax.ppermute only.
A program may use at most 128 MiB of HBM per device.

```python
import jax
import jax.numpy as jnp
from jax import lax

NY = 128
NX = 512
NZ = 1024


def draw_flow(key, part):
    key = jax.random.fold_in(key, 7)
    key_base = jax.random.fold_in(key, 1)
    key_scale = jax.random.fold_in(key, 2)
    key_noise = jax.random.fold_in(key, 3)
    offsets = jax.random.truncated_normal(key_base, -4.0, 4.0, (4, NX, 1, NY), jnp.float32)
    spread = jnp.exp(jax.random.uniform(key_scale, (4, NX, 1, NY), jnp.float32, jnp.log(0.3), jnp.log(3.0)))
    noise = jax.random.truncated_normal(key_noise, -4.0, 4.0, (4, NX, NZ, NY), jnp.float32)
    return offsets + spread * noise


def normal_values(own_key, shape, scale, bound, kind=jnp.bfloat16):
    entries = jax.random.normal(own_key, shape, jnp.float32) * scale
    return jnp.minimum(jnp.maximum(entries, -bound), bound).astype(kind)


def setup_inputs(seed: int = 0) -> dict:
    splits = jax.random.split(jax.random.key(seed), 3)
    return {
        "flow": draw_flow(jax.random.fold_in(splits[2], 71), 0),
        "dy_matrix": normal_values(splits[1], (NY, NY), NY ** -0.5, 0.5, jnp.float32),
    }


coeffs = (0.8, -0.2, 4.0 / 105.0, -1.0 / 280.0)
pair_list = ((0, 0), (0, 1), (0, 2), (1, 1), (1, 2), (2, 2))
triple_list = ((0, 0, 0), (0, 0, 1), (0, 0, 2), (0, 1, 1), (0, 1, 2), (0, 2, 2), (1, 1, 1), (1, 1, 2), (1, 2, 2), (2, 2, 2))


def centered(padded, along, length):
    result = jnp.zeros_like(lax.slice_in_dim(padded, 4, 4 + length, axis=along))
    for offset in range(1, 5):
        upper = lax.slice_in_dim(padded, 4 + offset, 4 + offset + length, axis=along)
        lower = lax.slice_in_dim(padded, 4 - offset, 4 - offset + length, axis=along)
        result = result + coeffs[offset - 1] * (upper - lower)
    return result


def moment_sums(fluct, slopes):
    term_list = []
    for left_c, right_c in pair_list:
        term_list.append(fluct[left_c] * fluct[right_c])
    for first_c, second_c, third_c in triple_list:
        term_list.append(fluct[first_c] * fluct[second_c] * fluct[third_c])
    for comp_c in range(3):
        term_list.append(fluct[3] * fluct[comp_c])
    for left_c, right_c in pair_list:
        term_list.append(fluct[3] * (slopes[left_c][right_c] + slopes[right_c][left_c]))
    for left_c, right_c in pair_list:
        term_list.append(slopes[left_c][0] * slopes[right_c][0] + slopes[left_c][1] * slopes[right_c][1] + slopes[left_c][2] * slopes[right_c][2])
    for left_c, right_c in pair_list:
        term_list.append(-(fluct[left_c] * slopes[3][right_c] + fluct[right_c] * slopes[3][left_c]))
    return jnp.stack([jnp.sum(entry_term, axis=1) for entry_term in term_list])


def reference(flow, dy_matrix):
    averages = jnp.sum(flow, axis=2) / NZ
    fluct = flow - averages[:, :, None, :]
    x_padded = jnp.pad(fluct, ((0, 0), (4, 4), (0, 0), (0, 0)), mode="symmetric")
    z_padded = jnp.pad(fluct, ((0, 0), (0, 0), (4, 4), (0, 0)), mode="wrap")
    slope_x = centered(x_padded, 1, NX)
    slope_z = centered(z_padded, 2, NZ)
    slope_y = jnp.dot(fluct, dy_matrix.T, precision=lax.Precision.HIGHEST)
    slopes = [(slope_x[comp_c], slope_y[comp_c], slope_z[comp_c]) for comp_c in range(4)]
    totals = moment_sums(fluct, slopes)
    return jnp.concatenate([averages[:3], totals / NZ], axis=0)
```

```python
import functools

import jax
import jax.numpy as jnp
from jax import lax
from jax.experimental import pallas as pl
from jax.experimental.pallas import tpu as pltpu
from jax.sharding import Mesh, PartitionSpec as P

F32 = jnp.float32
BF16 = jnp.bfloat16
lead = 4.0 / 5.0
ratios = (1.0, -0.25, 1.0 / 21.0, -1.0 / 224.0)
pairs = ((0, 0), (0, 1), (0, 2), (1, 1), (1, 2), (2, 2))
triples = (
    (0, 0, 0), (0, 0, 1), (0, 0, 2), (0, 1, 1), (0, 1, 2),
    (0, 2, 2), (1, 1, 1), (1, 1, 2), (1, 2, 2), (2, 2, 2),
)
MEAN, DXM, ZSUM, UU, UUU, PU, PG, GG, UG = 0, 4, 8, 11, 17, 27, 30, 36, 42
STATE = 47
OUT = 40
NBASE = 19
NSLOPE = 22
GXA, ZA, CA = "gx", ("xh", "z", "c"), "c"


def combine(left, right, count, dmat, put):
    half = [0.5 * (left(MEAN + c) - right(MEAN + c)) for c in range(4)]
    gx = [0.5 * (left(DXM + c) - right(DXM + c)) for c in range(4)]
    gy = [
        jnp.dot(h, dmat, precision=lax.Precision.HIGHEST, preferred_element_type=F32) for h in half
    ]
    dz = [half[3] * (left(ZSUM + c) - right(ZSUM + c)) for c in range(3)]
    both = float(2 * count)
    nh = [both * h for h in half]
    for c in range(4):
        put(MEAN + c, 0.5 * (left(MEAN + c) + right(MEAN + c)))
        put(DXM + c, 0.5 * (left(DXM + c) + right(DXM + c)))
    for c in range(3):
        put(ZSUM + c, left(ZSUM + c) + right(ZSUM + c))
    gap = {}
    for k, (i, j) in enumerate(pairs):
        a, b = left(UU + k), right(UU + k)
        gap[i, j] = gap[j, i] = a - b
        put(UU + k, (a + b) + nh[i] * half[j])
    for k, (i, j, l) in enumerate(triples):
        fix = half[i] * gap[j, l] + half[j] * gap[i, l] + half[l] * gap[i, j]
        put(UUU + k, (left(UUU + k) + right(UUU + k)) + fix)
    for c in range(3):
        put(PU + c, (left(PU + c) + right(PU + c)) + nh[3] * half[c])
    fixes = (
        2.0 * nh[3] * gx[0],
        nh[3] * (gy[0] + gx[1]),
        dz[0] + nh[3] * gx[2],
        2.0 * nh[3] * gy[1],
        dz[1] + nh[3] * gy[2],
        2.0 * dz[2],
    )
    for k in range(6):
        put(PG + k, (left(PG + k) + right(PG + k)) + fixes[k])
    for k, (i, j) in enumerate(pairs):
        fix = both * (gx[i] * gx[j] + gy[i] * gy[j])
        put(GG + k, (left(GG + k) + right(GG + k)) + fix)
    fixes = (
        -2.0 * nh[0] * gx[3],
        -(nh[0] * gy[3] + nh[1] * gx[3]),
        dz[0] - nh[2] * gx[3],
        -2.0 * nh[1] * gy[3],
        dz[1] - nh[2] * gy[3],
    )
    for k in range(5):
        put(UG + k, (left(UG + k) + right(UG + k)) + fixes[k])


def base_kernel(flow, mean, base, acc):
    rows, depth = flow.shape[1], flow.shape[2]

    def one(x, _):
        centre = []
        for c in range(4):
            m = jnp.sum(flow[c, x], axis=0, keepdims=True) * (1.0 / depth)
            mean[c, pl.ds(x, 1), :] = m
            centre.append(m)
        total = [None] * NBASE

        def add(k, v):
            total[k] = v if total[k] is None else total[k] + v

        for b in range(depth // 8):
            f = [flow[c, x, pl.ds(8 * b, 8), :] - centre[c] for c in range(4)]
            prod = {}
            for k, (i, j) in enumerate(pairs):
                prod[i, j] = f[i] * f[j]
                add(k, prod[i, j])
            for k, (i, j, l) in enumerate(triples):
                add(6 + k, prod[i, j] * f[l])
            for c in range(3):
                add(16 + c, f[3] * f[c])
        for k in range(NBASE):
            acc[pl.ds(pl.multiple_of(k * 8 * rows + 8 * x, 8), 8), :] = total[k]
        return 0

    lax.fori_loop(0, rows, one, 0)
    for k in range(NBASE):
        base[k] = sum(acc[pl.ds(k * 8 * rows + s, rows, stride=8), :] for s in range(8))


def base_moments(flow):
    _, lx, lz, ny = flow.shape
    step = 8
    return pl.pallas_call(
        base_kernel,
        grid=(lx // step,),
        in_specs=[pl.BlockSpec((4, step, lz, ny), lambda i: (0, i, 0, 0))],
        out_specs=[
            pl.BlockSpec((4, step, ny), lambda i: (0, i, 0)),
            pl.BlockSpec((NBASE, step, ny), lambda i: (0, i, 0)),
        ],
        out_shape=[
            jax.ShapeDtypeStruct((4, lx, ny), F32),
            jax.ShapeDtypeStruct((NBASE, lx, ny), F32),
        ],
        scratch_shapes=[pltpu.VMEM((NBASE * 8 * step, ny), F32)],
        compiler_params=pltpu.CompilerParams(vmem_limit_bytes=24 * 2**20),
        cost_estimate=pl.CostEstimate(
            flops=50 * flow.size, bytes_accessed=4 * flow.size, transcendentals=0
        ),
        name="base_moments",
    )(flow)


def slope_kernel(
    flow, xl, xr, zl, zr, mean, base, dy, keep, send, raw, acc, mpad, dxm, weights, ysl, sems
):
    _, lx, lz, ny = flow.shape
    half = lx // 2
    core = lax.axis_index(CA)
    gi = lax.axis_index(GXA)
    gn = lax.axis_size(GXA)
    parts = 8
    piece = lx // parts
    first = half * (1 - core)

    def body_copy(k):
        at = lax.rem(first + piece * k, lx)
        return pltpu.make_async_copy(
            flow.at[:, pl.ds(at, piece)],
            raw.at[:, pl.ds(4 + at, piece), pl.ds(8, lz)],
            sems.at[k],
        )

    def rim_copies(side):
        if side == 0:
            plain = pltpu.make_async_copy(
                xl, raw.at[:, pl.ds(0, 4), pl.ds(8, lz)], sems.at[parts]
            )
            mirror = [
                pltpu.make_async_copy(
                    flow.at[:, pl.ds(3 - j, 1)],
                    raw.at[:, pl.ds(j, 1), pl.ds(8, lz)],
                    sems.at[parts + 2 + j],
                )
                for j in range(4)
            ]
        else:
            plain = pltpu.make_async_copy(
                xr, raw.at[:, pl.ds(4 + lx, 4), pl.ds(8, lz)], sems.at[parts + 1]
            )
            mirror = [
                pltpu.make_async_copy(
                    flow.at[:, pl.ds(lx - 1 - j, 1)],
                    raw.at[:, pl.ds(4 + lx + j, 1), pl.ds(8, lz)],
                    sems.at[parts + 6 + j],
                )
                for j in range(4)
            ]
        return plain, mirror

    ends = (gi == 0, gi == gn - 1)
    for side in range(2):
        plain, mirror = rim_copies(side)

        @pl.when(ends[side])
        def _():
            for c in mirror:
                c.start()

        @pl.when(jnp.logical_not(ends[side]))
        def _():
            plain.start()

    for k in range(parts):
        body_copy(k).start()

    d = dy[...].T * (1.0 / lead)
    dhi = d.astype(BF16)
    dlo = (d - dhi.astype(F32)).astype(BF16)
    weights[pl.ds(0, ny), pl.ds(0, ny)] = dhi
    weights[pl.ds(0, ny), pl.ds(ny, ny)] = dlo
    weights[pl.ds(ny, ny), pl.ds(0, ny)] = dhi
    weights[pl.ds(ny, ny), pl.ds(ny, ny)] = jnp.zeros_like(dlo)

    for side in range(2):
        plain, mirror = rim_copies(side)

        @pl.when(ends[side])
        def _():
            for c in mirror:
                c.wait()

        @pl.when(jnp.logical_not(ends[side]))
        def _():
            plain.wait()

    for c in range(4):
        mpad[c, pl.ds(8, lx), :] = mean[c]
        for j in range(4):
            for src, dst in ((j, 4 + j), (4 + lx + j, 8 + lx + j)):
                mpad[c, pl.ds(dst, 1), :] = jnp.sum(
                    raw[c, src, pl.ds(8, lz), :], axis=0, keepdims=True
                ) * (1.0 / lz)
    for c in range(4):
        out = None
        for k in range(4):
            diff = mpad[c, pl.ds(9 + k, lx), :] - mpad[c, pl.ds(7 - k, lx), :]
            out = diff if out is None else out + ratios[k] * diff
        dxm[c] = out

    for k in range(parts):
        body_copy(k).wait()

    def one(i, _):
        x = lax.rem(i + first, lx)
        for c in range(3):
            raw[c, x + 4, pl.ds(4, 4), :] = zl[c, x]
            raw[c, x + 4, pl.ds(8 + lz, 4), :] = zr[c, x]
        centre = [mean[c, pl.ds(x, 1), :] for c in range(4)]
        shift = [dxm[c, pl.ds(x, 1), :] for c in range(4)]
        for c in range(4):
            a = raw[c, x + 4, pl.ds(8, lz), :] - centre[c]
            hi = a.astype(BF16)
            lo = (a - hi.astype(F32)).astype(BF16)
            y = jnp.dot(
                jnp.concatenate([hi, lo], axis=1), weights[...], preferred_element_type=F32
            )
            ysl[c] = y[:, :ny] + y[:, ny:]
        total = [None] * NSLOPE

        def add(k, v):
            total[k] = v if total[k] is None else total[k] + v

        for b in range(lz // 8):
            at = 8 + 8 * b
            g = [[None] * 3 for _ in range(4)]
            for c in range(4):
                out = None
                for k in range(4):
                    diff = raw[c, x + 5 + k, pl.ds(at, 8), :] - raw[c, x + 3 - k, pl.ds(at, 8), :]
                    out = diff if out is None else out + ratios[k] * diff
                g[c][0] = out - shift[c]
                g[c][1] = ysl[c, pl.ds(8 * b, 8), :]
            for c in range(3):
                out = None
                for k in range(4):
                    diff = (
                        raw[c, x + 4, pl.ds(at + 1 + k, 8), :]
                        - raw[c, x + 4, pl.ds(at - 1 - k, 8), :]
                    )
                    out = diff if out is None else out + ratios[k] * diff
                g[c][2] = out
            u = [raw[c, x + 4, pl.ds(at, 8), :] - centre[c] for c in range(4)]
            p = u[3]
            for c in range(3):
                add(c, g[c][2])
            add(3, p * g[0][0])
            add(4, p * (g[0][1] + g[1][0]))
            add(5, p * g[0][2])
            add(6, p * g[2][0])
            add(7, p * g[1][1])
            add(8, p * g[1][2])
            add(9, p * g[2][1])
            add(10, p * g[2][2])
            for k, (i2, j2) in enumerate(pairs):
                for dim in range(3):
                    add(11 + k, g[i2][dim] * g[j2][dim])
            add(17, u[0] * g[3][0])
            add(18, u[0] * g[3][1] + u[1] * g[3][0])
            add(19, u[1] * g[3][1])
            add(20, u[2] * g[3][0])
            add(21, u[2] * g[3][1])
        for k in range(NSLOPE):
            acc[pl.ds(pl.multiple_of(k * 8 * lx + 8 * i, 8), 8), :] = total[k]
        return 0

    lax.fori_loop(0, lx, one, 0)

    for part, out in ((0, send), (1, keep)):
        src = half * (1 - core) if part == 0 else half * core
        src = pl.multiple_of(src, 8)

        def total(k):
            at = k * 8 * lx + 8 * half * part
            return sum(acc[pl.ds(at + s, half, stride=8), :] for s in range(8))

        for c in range(4):
            out[MEAN + c] = mean[c, pl.ds(src, half), :]
            out[DXM + c] = dxm[c, pl.ds(src, half), :]
        for k in range(NBASE):
            out[UU + k] = base[k, pl.ds(src, half), :]
        for c in range(3):
            out[ZSUM + c] = total(c)
        s02, s12 = total(5), total(8)
        out[PG + 0] = 2.0 * total(3)
        out[PG + 1] = total(4)
        out[PG + 2] = s02 + total(6)
        out[PG + 3] = 2.0 * total(7)
        out[PG + 4] = s12 + total(9)
        out[PG + 5] = 2.0 * total(10)
        for k in range(6):
            out[GG + k] = total(11 + k)
        out[UG + 0] = -2.0 * total(17)
        out[UG + 1] = -total(18)
        out[UG + 2] = s02 - total(20)
        out[UG + 3] = -2.0 * total(19)
        out[UG + 4] = s12 - total(21)


def slope_moments(flow, xl, xr, zl, zr, mean, base, dy):
    _, lx, lz, ny = flow.shape
    vm = pl.BlockSpec(memory_space=pltpu.VMEM)
    hb = pl.BlockSpec(memory_space=pl.ANY)
    shape = jax.ShapeDtypeStruct((STATE, lx // 2, ny), F32)
    return pl.pallas_call(
        slope_kernel,
        in_specs=[hb, hb, hb, vm, vm, vm, vm, vm],
        out_specs=[vm, vm],
        out_shape=[shape, shape],
        scratch_shapes=[
            pltpu.VMEM((4, lx + 8, lz + 16, ny), F32),
            pltpu.VMEM((NSLOPE * 8 * lx, ny), F32),
            pltpu.VMEM((4, lx + 16, ny), F32),
            pltpu.VMEM((4, lx, ny), F32),
            pltpu.VMEM((2 * ny, 2 * ny), BF16),
            pltpu.VMEM((4, lz, ny), F32),
            pltpu.SemaphoreType.DMA((18,)),
        ],
        compiler_params=pltpu.CompilerParams(vmem_limit_bytes=40 * 2**20),
        cost_estimate=pl.CostEstimate(
            flops=200 * flow.size, bytes_accessed=4 * flow.size, transcendentals=0
        ),
        name="slope_moments",
    )(flow, xl, xr, zl, zr, mean, base, dy)


def core_kernel(count, keep, got, dy, own, up, down, far):
    d = dy[...].T * (1.0 / lead)
    rows = own.shape[1]
    zi = lax.axis_index("z")
    zn = lax.axis_size("z")
    for k, out in ((0, own), (1, up), (zn - 1, down), (2, far)):
        at = pl.multiple_of(rows * lax.rem(zi + k, zn), 8)

        def put(f, v, out=out):
            out[f] = v

        combine(
            lambda f, at=at: keep[f, pl.ds(at, rows), :],
            lambda f, at=at: got[f, pl.ds(at, rows), :],
            count, d, put,
        )


def span_kernel(count, own, one, two, three, dy, out, left, right):
    d = dy[...].T * (1.0 / lead)

    def put_to(ref):
        def put(f, v):
            ref[f] = v
        return put

    combine(lambda f: own[f], lambda f: one[f], count, d, put_to(left))
    combine(lambda f: two[f], lambda f: three[f], count, d, put_to(right))
    combine(lambda f: left[f], lambda f: right[f], 2 * count, d, put_to(out))


def last_kernel(count, mine, other, dy, out, state):
    d = dy[...].T * (1.0 / lead)

    def put(f, v):
        state[f] = v

    combine(lambda f: mine[f], lambda f: other[f], count, d, put)
    scale = 1.0 / (2 * count)
    for c in range(3):
        out[c] = state[MEAN + c]
    for k in range(NBASE):
        out[3 + k] = state[UU + k] * scale
    for k in range(6):
        out[22 + k] = state[PG + k] * (scale * lead)
        out[28 + k] = state[GG + k] * (scale * lead * lead)
    for k in range(5):
        out[34 + k] = state[UG + k] * (scale * lead)
    out[39] = state[PG + 5] * (scale * lead)


def place_kernel(*refs):
    ins, out = refs[:-1], refs[-1]
    rows = ins[0].shape[1]
    zi = lax.axis_index("z")
    zn = lax.axis_size("z")
    core = lax.axis_index(CA)
    for k, ref in enumerate(ins):
        side, step = divmod(k, zn)
        c = core if side == 0 else 1 - core
        at = pl.multiple_of(rows * (zn * c + lax.rem(zi + zn - step, zn)), 8)
        out[:, pl.ds(at, rows), :] = ref[...]


def small_call(kernel, outs, scratch, name, *args):
    vm = pl.BlockSpec(memory_space=pltpu.VMEM)
    return pl.pallas_call(
        kernel,
        in_specs=[vm] * len(args),
        out_specs=[vm] * len(outs),
        out_shape=[jax.ShapeDtypeStruct(s, F32) for s in outs],
        scratch_shapes=[pltpu.VMEM(s, F32) for s in scratch],
        compiler_params=pltpu.CompilerParams(vmem_limit_bytes=24 * 2**20),
        name=name,
    )(*args)


def send(value, axis, step):
    size = lax.axis_size(axis)
    return lax.ppermute(value, axis, [(i, (i + step) % size) for i in range(size)])


def shards(flow, dy):
    _, lx, lz, ny = flow.shape
    gn = lax.axis_size(GXA)
    zn = lax.axis_size("z")
    up = [(i, i + 1) for i in range(gn - 1)]
    down = [(i + 1, i) for i in range(gn - 1)]
    with jax.named_scope("rims"):
        xl = lax.ppermute(flow[:, lx - 4 :], GXA, up)
        xr = lax.ppermute(flow[:, :4], GXA, down)
        zl = send(flow[:, :, lz - 4 :], ZA, 1)
        zr = send(flow[:, :, :4], ZA, -1)
    mean, base = base_moments(flow)
    keep, give = slope_moments(flow, xl, xr, zl, zr, mean, base, dy)
    with jax.named_scope("core_exchange"):
        got = send(give, CA, 1)
    rows = lx // 2 // zn
    piece = (STATE, rows, ny)
    own, up1, down1, far = small_call(
        functools.partial(core_kernel, lz), [piece] * 4, [], "core_merge", keep, got, dy
    )
    with jax.named_scope("span_exchange"):
        one = send(up1, "z", 1)
        three = send(down1, "z", -1)
        two = send(far, "z", 2)
    (part,) = small_call(
        functools.partial(span_kernel, 2 * lz),
        [piece], [piece, piece], "span_merge", own, one, two, three, dy,
    )
    with jax.named_scope("x_exchange"):
        other = send(part, "xh", 1)
    (done,) = small_call(
        functools.partial(last_kernel, 2 * zn * lz),
        [(OUT, rows, ny)], [piece], "last_merge", part, other, dy,
    )
    with jax.named_scope("spread"):
        mine = [done] + [send(done, "z", k) for k in (1, 2, 3)]
        theirs = [send(v, CA, 1) for v in mine]
    (out,) = small_call(place_kernel, [(OUT, lx, ny)], [], "place", *mine, *theirs)
    return out


def solution(mesh):
    gx, gz = mesh.shape["gx"], mesh.shape["gz"]
    fine = Mesh(mesh.devices.reshape(gx, 2, gz // 4, 2), (GXA,) + ZA)
    return jax.shard_map(
        shards,
        mesh=fine,
        in_specs=(P(None, GXA, ZA, None), P()),
        out_specs=P(None, GXA, None),
        check_vma=False,
    )
```

```python
import functools

import jax
import jax.numpy as jnp
from jax import lax
from jax.experimental import pallas as pl
from jax.experimental.pallas import tpu as pltpu
from jax.sharding import Mesh, PartitionSpec as P

F32 = jnp.float32
BF16 = jnp.bfloat16
lead = 4.0 / 5.0
ratios = (1.0, -0.25, 1.0 / 21.0, -1.0 / 224.0)
pairs = ((0, 0), (0, 1), (0, 2), (1, 1), (1, 2), (2, 2))
triples = (
    (0, 0, 0), (0, 0, 1), (0, 0, 2), (0, 1, 1), (0, 1, 2),
    (0, 2, 2), (1, 1, 1), (1, 1, 2), (1, 2, 2), (2, 2, 2),
)
MEAN, DXM, ZSUM, UU, UUU, PU, PG, GG, UG = 0, 4, 8, 11, 17, 27, 30, 36, 42
STATE = 47
OUT = 40
NBASE = 19
NSLOPE = 22
GXA, ZA, CA = "gx", ("xh", "z", "c"), "c"


def combine(left, right, count, dmat, put):
    half = [0.5 * (left(MEAN + c) - right(MEAN + c)) for c in range(4)]
    gx = [0.5 * (left(DXM + c) - right(DXM + c)) for c in range(4)]
    gy = [
        jnp.dot(h, dmat, precision=lax.Precision.HIGHEST, preferred_element_type=F32) for h in half
    ]
    dz = [half[3] * (left(ZSUM + c) - right(ZSUM + c)) for c in range(3)]
    both = float(2 * count)
    nh = [both * h for h in half]
    for c in range(4):
        put(MEAN + c, 0.5 * (left(MEAN + c) + right(MEAN + c)))
        put(DXM + c, 0.5 * (left(DXM + c) + right(DXM + c)))
    for c in range(3):
        put(ZSUM + c, left(ZSUM + c) + right(ZSUM + c))
    gap = {}
    for k, (i, j) in enumerate(pairs):
        a, b = left(UU + k), right(UU + k)
        gap[i, j] = gap[j, i] = a - b
        put(UU + k, (a + b) + nh[i] * half[j])
    for k, (i, j, l) in enumerate(triples):
        fix = half[i] * gap[j, l] + half[j] * gap[i, l] + half[l] * gap[i, j]
        put(UUU + k, (left(UUU + k) + right(UUU + k)) + fix)
    for c in range(3):
        put(PU + c, (left(PU + c) + right(PU + c)) + nh[3] * half[c])
    fixes = (
        2.0 * nh[3] * gx[0],
        nh[3] * (gy[0] + gx[1]),
        dz[0] + nh[3] * gx[2],
        2.0 * nh[3] * gy[1],
        dz[1] + nh[3] * gy[2],
        2.0 * dz[2],
    )
    for k in range(6):
        put(PG + k, (left(PG + k) + right(PG + k)) + fixes[k])
    for k, (i, j) in enumerate(pairs):
        fix = both * (gx[i] * gx[j] + gy[i] * gy[j])
        put(GG + k, (left(GG + k) + right(GG + k)) + fix)
    fixes = (
        -2.0 * nh[0] * gx[3],
        -(nh[0] * gy[3] + nh[1] * gx[3]),
        dz[0] - nh[2] * gx[3],
        -2.0 * nh[1] * gy[3],
        dz[1] - nh[2] * gy[3],
    )
    for k in range(5):
        put(UG + k, (left(UG + k) + right(UG + k)) + fixes[k])


def row_sum(k, rows, acc, first=0, count=None):
    count = rows if count is None else count
    return sum(acc[pl.ds(8 * (k * rows + first) + s, count, stride=8), :] for s in range(8))


def copy_all(copies):
    for c in copies:
        c.start()
    for c in copies:
        c.wait()


def z_rim_kernel(flow, zl, zr, sems):
    lz = flow.shape[2]
    copy_all([
        pltpu.make_async_copy(flow.at[pl.ds(0, 3), :, pl.ds(lz - 4, 4)], zl, sems.at[0]),
        pltpu.make_async_copy(flow.at[pl.ds(0, 3), :, pl.ds(0, 4)], zr, sems.at[1]),
    ])


def x_rim_kernel(flow, after, xl, xr, sems):
    lx = flow.shape[1]
    copy_all([
        pltpu.make_async_copy(flow.at[:, pl.ds(lx - 4, 4)], xl, sems.at[0]),
        pltpu.make_async_copy(flow.at[:, pl.ds(0, 4)], xr, sems.at[1]),
    ])


def pad_kernel(flow, after, pad, sems):
    _, lx, lz, _ = flow.shape
    copy_all([
        pltpu.make_async_copy(flow.at[c], pad.at[c, pl.ds(4, lx), pl.ds(8, lz)], sems.at[c])
        for c in range(4)
    ])


def cut(kernel, shapes, copies, name, flow, *after):
    flow = pltpu.with_memory_space_constraint(flow, pltpu.HBM)
    return pl.pallas_call(
        kernel,
        in_specs=[pl.BlockSpec(memory_space=pltpu.HBM)]
        + [pl.BlockSpec(memory_space=pl.ANY)] * len(after),
        out_specs=[pl.BlockSpec(memory_space=pltpu.VMEM)] * len(shapes),
        out_shape=[pltpu.VMEM(s, F32) for s in shapes],
        scratch_shapes=[pltpu.SemaphoreType.DMA((copies,))],
        compiler_params=pltpu.CompilerParams(vmem_limit_bytes=4 * 2**20),
        name=name,
    )(flow, *after)


def base_kernel(pad_in, dy, pad, ysl, mean, base, acc, weights):
    _, lx, lz, ny = ysl.shape
    step = 8
    parts = lx // step

    d = dy[...].T * (1.0 / lead)
    dhi = d.astype(BF16)
    dlo = (d - dhi.astype(F32)).astype(BF16)
    weights[pl.ds(0, ny), pl.ds(0, ny)] = dhi
    weights[pl.ds(0, ny), pl.ds(ny, ny)] = dlo
    weights[pl.ds(ny, ny), pl.ds(0, ny)] = dhi
    weights[pl.ds(ny, ny), pl.ds(ny, ny)] = jnp.zeros_like(dlo)

    def one(x, _):
        centre = []
        for c in range(4):
            m = jnp.sum(pad[c, x + 4, pl.ds(8, lz), :], axis=0, keepdims=True) * (1.0 / lz)
            mean[c, pl.ds(x, 1), :] = m
            centre.append(m)
        total = [None] * NBASE

        def add(k, v):
            total[k] = v if total[k] is None else total[k] + v

        for b in range(lz // 8):
            f = [pad[c, x + 4, pl.ds(8 + 8 * b, 8), :] - centre[c] for c in range(4)]
            for c in range(4):
                pad[c, x + 4, pl.ds(8 + 8 * b, 8), :] = f[c]
            prod = {}
            for k, (i, j) in enumerate(pairs):
                prod[i, j] = f[i] * f[j]
                add(k, prod[i, j])
            for k, (i, j, l) in enumerate(triples):
                add(6 + k, prod[i, j] * f[l])
            for c in range(3):
                add(16 + c, f[3] * f[c])
        for k in range(NBASE):
            acc[pl.ds(pl.multiple_of(k * 8 * lx + 8 * x, 8), 8), :] = total[k]
        return 0

    def part(k, _):
        lax.fori_loop(step * k, step * k + step, one, 0)
        left = []
        for r in range(step):
            for c in range(4):
                a = pad[c, step * k + r + 4, pl.ds(8, lz), :]
                hi = a.astype(BF16)
                lo = (a - hi.astype(F32)).astype(BF16)
                left.append(jnp.concatenate([hi, lo], axis=1))
        y = jnp.dot(jnp.concatenate(left, axis=0), weights[...], preferred_element_type=F32)
        y = y[:, :ny] + y[:, ny:]
        for r in range(step):
            for c in range(4):
                at = (4 * r + c) * lz
                ysl[c, step * k + r] = y[at : at + lz]
        return 0

    lax.fori_loop(0, parts, part, 0)
    for k in range(NBASE):
        base[k] = row_sum(k, lx, acc)


def base_moments(pad, dy):
    ny = dy.shape[0]
    lx, lz = pad.shape[1] - 8, pad.shape[2] - 16
    vm = pl.BlockSpec(memory_space=pltpu.VMEM)
    shapes = [pad.shape, (4, lx, lz, ny), (4, lx, ny), (NBASE, lx, ny)]
    return pl.pallas_call(
        base_kernel,
        in_specs=[vm, vm],
        out_specs=[vm] * 4,
        out_shape=[pltpu.VMEM(s, F32) for s in shapes],
        input_output_aliases={0: 0},
        scratch_shapes=[
            pltpu.VMEM((NBASE * 8 * lx, ny), F32),
            pltpu.VMEM((2 * ny, 2 * ny), BF16),
        ],
        compiler_params=pltpu.CompilerParams(vmem_limit_bytes=16 * 2**20),
        cost_estimate=pl.CostEstimate(
            flops=1000, bytes_accessed=1000, transcendentals=0
        ),
        name="base_moments",
    )(pad, dy)


def difference(upper, lower):
    out = None
    for k in range(4):
        diff = upper(k) - lower(k)
        out = diff if out is None else out + ratios[k] * diff
    return out


def slope_row(pad, ysl, x):
    lz = ysl.shape[2]
    total = [None] * NSLOPE

    def add(k, v):
        total[k] = v if total[k] is None else total[k] + v

    for b in range(lz // 8):
        at = 8 + 8 * b
        u = [pad[c, x + 4, pl.ds(at, 8), :] for c in range(4)]
        p = u[3]
        g = [[None] * 3 for _ in range(4)]
        for c in range(4):
            g[c][0] = difference(
                lambda k: pad[c, x + 5 + k, pl.ds(at, 8), :],
                lambda k: pad[c, x + 3 - k, pl.ds(at, 8), :],
            )
            g[c][1] = ysl[c, x, pl.ds(8 * b, 8), :]
        for c in range(3):
            g[c][2] = difference(
                lambda k: pad[c, x + 4, pl.ds(at + 1 + k, 8), :],
                lambda k: pad[c, x + 4, pl.ds(at - 1 - k, 8), :],
            )
        for c in range(3):
            add(c, g[c][2])
        add(3, p * g[0][0])
        add(4, p * (g[0][1] + g[1][0]))
        add(5, p * g[0][2])
        add(6, p * g[2][0])
        add(7, p * g[1][1])
        add(8, p * g[1][2])
        add(9, p * g[2][1])
        add(10, p * g[2][2])
        for k, (i, j) in enumerate(pairs):
            for dim in range(3):
                add(11 + k, g[i][dim] * g[j][dim])
        add(17, u[0] * g[3][0])
        add(18, u[0] * g[3][1] + u[1] * g[3][0])
        add(19, u[1] * g[3][1])
        add(20, u[2] * g[3][0])
        add(21, u[2] * g[3][1])
    return total


def slope_fields(total):
    s02, s12 = total(5), total(8)
    yield PG + 0, 2.0 * total(3)
    yield PG + 1, total(4)
    yield PG + 2, s02 + total(6)
    yield PG + 3, 2.0 * total(7)
    yield PG + 4, s12 + total(9)
    yield PG + 5, 2.0 * total(10)
    for c in range(3):
        yield ZSUM + c, total(c)
    for k in range(6):
        yield GG + k, total(11 + k)
    yield UG + 0, -2.0 * total(17)
    yield UG + 1, -total(18)
    yield UG + 2, s02 - total(20)
    yield UG + 3, -2.0 * total(19)
    yield UG + 4, s12 - total(21)


def inner_kernel(pad_in, ysl, zl, zr, mean, base, pad, keep, send, acc):
    _, lx, lz, ny = ysl.shape
    half = lx // 2
    core = lax.axis_index(CA)

    def rim(x, _):
        for c in range(3):
            m = mean[c, pl.ds(x, 1), :]
            pad[c, x + 4, pl.ds(4, 4), :] = zl[c, x] - m
            pad[c, x + 4, pl.ds(8 + lz, 4), :] = zr[c, x] - m
        return 0

    lax.fori_loop(0, lx, rim, 0, unroll=4)

    def one(x, _):
        total = slope_row(pad, ysl, x)
        for k in range(NSLOPE):
            acc[pl.ds(pl.multiple_of(k * 8 * lx + 8 * x, 8), 8), :] = total[k]
        return 0

    lax.fori_loop(4, lx - 4, one, 0)

    for out, side in ((send, 1 - core), (keep, core)):
        at = pl.multiple_of(half * side, 8)

        def total(k, at=at):
            where = pl.multiple_of(8 * (k * lx + at), 8)
            return sum(acc[pl.ds(where + s, half, stride=8), :] for s in range(8))

        for c in range(4):
            out[MEAN + c] = mean[c, pl.ds(at, half), :]
        for k in range(NBASE):
            out[UU + k] = base[k, pl.ds(at, half), :]
        for f, v in slope_fields(total):
            out[f] = v


def inner_moments(pad, ysl, zl, zr, mean, base):
    _, lx, lz, ny = ysl.shape
    vm = pl.BlockSpec(memory_space=pltpu.VMEM)
    shape = pltpu.VMEM((STATE, lx // 2, ny), F32)
    return pl.pallas_call(
        inner_kernel,
        in_specs=[vm] * 6,
        out_specs=[vm] * 3,
        out_shape=[pltpu.VMEM(pad.shape, F32), shape, shape],
        input_output_aliases={0: 0},
        scratch_shapes=[pltpu.VMEM((NSLOPE * 8 * lx, ny), F32)],
        compiler_params=pltpu.CompilerParams(vmem_limit_bytes=16 * 2**20),
        cost_estimate=pl.CostEstimate(
            flops=5000 * ysl.size, bytes_accessed=40 * ysl.size, transcendentals=0
        ),
        name="inner_moments",
    )(pad, ysl, zl, zr, mean, base)


def edge_kernel(
    pad_in, keep_in, send_in, ysl, xl, xr, mean, pad, keep, send, acc, mpad, dxm
):
    _, lx, lz, ny = ysl.shape
    half = lx // 2
    core = lax.axis_index(CA)
    gi = lax.axis_index(GXA)
    at_ends = (gi == 0, gi == lax.axis_size(GXA) - 1)

    for c in range(4):
        mpad[c, pl.ds(8, lx), :] = mean[c]
        for j in range(4):
            for halo, at_end, src, dst in (
                (xl, at_ends[0], 3 - j, j), (xr, at_ends[1], lx - 1 - j, lx + 4 + j)
            ):
                own = pad[c, src + 4, pl.ds(8, lz), :]
                m = jnp.sum(halo[c, j], axis=0, keepdims=True) * (1.0 / lz)
                pad[c, dst, pl.ds(8, lz), :] = jnp.where(at_end, own, halo[c, j] - m)
                mpad[c, pl.ds(dst + 4, 1), :] = jnp.where(at_end, mean[c, pl.ds(src, 1), :], m)
        dxm[c] = difference(
            lambda k: mpad[c, pl.ds(9 + k, lx), :], lambda k: mpad[c, pl.ds(7 - k, lx), :]
        )

    for out, side in ((send, 1 - core), (keep, core)):
        for c in range(4):
            out[DXM + c] = dxm[c, pl.ds(pl.multiple_of(half * side, 8), half), :]

    def one(i, _):
        x = jnp.where(i < 4, i, lx - 8 + i)
        total = slope_row(pad, ysl, x)
        for k in range(NSLOPE):
            acc[pl.ds(pl.multiple_of(k * 64 + 8 * i, 8), 8), :] = total[k]
        return 0

    lax.fori_loop(0, 8, one, 0)

    fields = list(slope_fields(lambda k: row_sum(k, 8, acc)))
    for side, rows in ((0, slice(0, 4)), (1, slice(4, 8))):
        at = 0 if side == 0 else half - 4

        @pl.when(core == side)
        def _():
            for f, v in fields:
                keep[f, pl.ds(at, 4), :] = v[rows]

        @pl.when(core != side)
        def _():
            for f, v in fields:
                send[f, pl.ds(at, 4), :] = v[rows]


def edge_moments(pad, keep, send, ysl, xl, xr, mean):
    _, lx, lz, ny = ysl.shape
    vm = pl.BlockSpec(memory_space=pltpu.VMEM)
    out = pl.pallas_call(
        edge_kernel,
        in_specs=[vm] * 7,
        out_specs=[vm] * 3,
        out_shape=[pltpu.VMEM(v.shape, F32) for v in (pad, keep, send)],
        input_output_aliases={0: 0, 1: 1, 2: 2},
        scratch_shapes=[
            pltpu.VMEM((NSLOPE * 64, ny), F32),
            pltpu.VMEM((4, lx + 16, ny), F32),
            pltpu.VMEM((4, lx, ny), F32),
        ],
        compiler_params=pltpu.CompilerParams(vmem_limit_bytes=16 * 2**20),
        cost_estimate=pl.CostEstimate(
            flops=25 * ysl.size, bytes_accessed=ysl.size // 2, transcendentals=0
        ),
        name="edge_moments",
    )(pad, keep, send, ysl, xl, xr, mean)
    return out[1:]


def core_kernel(count, keep, got, dy, own, up, down, far):
    d = dy[...].T * (1.0 / lead)
    rows = own.shape[1]
    zi = lax.axis_index("z")
    zn = lax.axis_size("z")
    for k, out in ((0, own), (1, up), (zn - 1, down), (2, far)):
        at = pl.multiple_of(rows * lax.rem(zi + k, zn), 8)

        def put(f, v, out=out):
            out[f] = v

        combine(
            lambda f, at=at: keep[f, pl.ds(at, rows), :],
            lambda f, at=at: got[f, pl.ds(at, rows), :],
            count, d, put,
        )


def span_kernel(count, own, one, two, three, dy, out, left, right):
    d = dy[...].T * (1.0 / lead)

    def put_to(ref):
        def put(f, v):
            ref[f] = v
        return put

    combine(lambda f: own[f], lambda f: one[f], count, d, put_to(left))
    combine(lambda f: two[f], lambda f: three[f], count, d, put_to(right))
    combine(lambda f: left[f], lambda f: right[f], 2 * count, d, put_to(out))


def last_kernel(count, mine, other, dy, out, state):
    d = dy[...].T * (1.0 / lead)

    def put(f, v):
        state[f] = v

    combine(lambda f: mine[f], lambda f: other[f], count, d, put)
    scale = 1.0 / (2 * count)
    for c in range(3):
        out[c] = state[MEAN + c]
    for k in range(NBASE):
        out[3 + k] = state[UU + k] * scale
    for k in range(6):
        out[22 + k] = state[PG + k] * (scale * lead)
        out[28 + k] = state[GG + k] * (scale * lead * lead)
    for k in range(5):
        out[34 + k] = state[UG + k] * (scale * lead)
    out[39] = state[PG + 5] * (scale * lead)


def place_kernel(*refs):
    ins, out = refs[:-1], refs[-1]
    rows = ins[0].shape[1]
    zi = lax.axis_index("z")
    zn = lax.axis_size("z")
    core = lax.axis_index(CA)
    for k, ref in enumerate(ins):
        side, step = divmod(k, zn)
        c = core if side == 0 else 1 - core
        at = pl.multiple_of(rows * (zn * c + lax.rem(zi + zn - step, zn)), 8)
        out[:, pl.ds(at, rows), :] = ref[...]


def small_call(kernel, outs, scratch, name, *args):
    vm = pl.BlockSpec(memory_space=pltpu.VMEM)
    return pl.pallas_call(
        kernel,
        in_specs=[vm] * len(args),
        out_specs=[vm] * len(outs),
        out_shape=[jax.ShapeDtypeStruct(s, F32) for s in outs],
        scratch_shapes=[pltpu.VMEM(s, F32) for s in scratch],
        compiler_params=pltpu.CompilerParams(vmem_limit_bytes=24 * 2**20),
        name=name,
    )(*args)


def send(value, axis, step):
    size = lax.axis_size(axis)
    return lax.ppermute(value, axis, [(i, (i + step) % size) for i in range(size)])


def shards(flow, dy):
    _, lx, lz, ny = flow.shape
    gn = lax.axis_size(GXA)
    zn = lax.axis_size("z")
    up = [(i, i + 1) for i in range(gn - 1)]
    down = [(i + 1, i) for i in range(gn - 1)]
    zs, xs = (3, lx, 4, ny), (4, 4, lz, ny)
    zl, zr = cut(z_rim_kernel, [zs, zs], 2, "z_rims", flow)
    xl, xr = cut(x_rim_kernel, [xs, xs], 2, "x_rims", flow, zl)
    (pad,) = cut(pad_kernel, [(4, lx + 8, lz + 16, ny)], 4, "load", flow, xl)
    with jax.named_scope("rim_exchange"):
        zl = send(zl, ZA, 1)
        zr = send(zr, ZA, -1)
        xl = lax.ppermute(xl, GXA, up)
        xr = lax.ppermute(xr, GXA, down)
    pad, ysl, mean, base = base_moments(pad, dy)
    pad, keep, give = inner_moments(pad, ysl, zl, zr, mean, base)
    keep, give = edge_moments(pad, keep, give, ysl, xl, xr, mean)
    with jax.named_scope("core_exchange"):
        got = send(give, CA, 1)
    rows = lx // 2 // zn
    piece = (STATE, rows, ny)
    own, up1, down1, far = small_call(
        functools.partial(core_kernel, lz), [piece] * 4, [], "core_merge", keep, got, dy
    )
    with jax.named_scope("span_exchange"):
        one = send(up1, "z", 1)
        three = send(down1, "z", -1)
        two = send(far, "z", 2)
    (part,) = small_call(
        functools.partial(span_kernel, 2 * lz),
        [piece], [piece, piece], "span_merge", own, one, two, three, dy,
    )
    with jax.named_scope("x_exchange"):
        other = send(part, "xh", 1)
    (done,) = small_call(
        functools.partial(last_kernel, 2 * zn * lz),
        [(OUT, rows, ny)], [piece], "last_merge", part, other, dy,
    )
    with jax.named_scope("spread"):
        mine = [done] + [send(done, "z", k) for k in (1, 2, 3)]
        theirs = [send(v, CA, 1) for v in mine]
    (out,) = small_call(place_kernel, [(OUT, lx, ny)], [], "place", *mine, *theirs)
    return out


def solution(mesh):
    gx, gz = mesh.shape["gx"], mesh.shape["gz"]
    fine = Mesh(mesh.devices.reshape(gx, 2, gz // 4, 2), (GXA,) + ZA)
    return jax.shard_map(
        shards,
        mesh=fine,
        in_specs=(P(None, GXA, ZA, None), P()),
        out_specs=P(None, GXA, None),
        check_vma=False,
    )
```

```python
import functools

import jax
import jax.numpy as jnp
from jax import lax
from jax.experimental import pallas as pl
from jax.experimental.pallas import tpu as pltpu
from jax.sharding import Mesh, PartitionSpec as P

F32 = jnp.float32
BF16 = jnp.bfloat16
lead = 4.0 / 5.0
ratios = (1.0, -0.25, 1.0 / 21.0, -1.0 / 224.0)
pairs = ((0, 0), (0, 1), (0, 2), (1, 1), (1, 2), (2, 2))
triples = (
    (0, 0, 0), (0, 0, 1), (0, 0, 2), (0, 1, 1), (0, 1, 2),
    (0, 2, 2), (1, 1, 1), (1, 1, 2), (1, 2, 2), (2, 2, 2),
)
MEAN, UU, UUU, PU, DXM, PG, GG, UG = 0, 4, 10, 20, 23, 27, 33, 39
FIRST = 23
STATE = 44
OUT = 40
NBASE = 19
NSLOPE = 22
GXA, ZA, CA = "gx", ("xh", "z", "c"), "c"


def combine_base(left, right, count, put):
    half = [0.5 * (left(MEAN + c) - right(MEAN + c)) for c in range(4)]
    nh = [float(2 * count) * h for h in half]
    for c in range(4):
        put(MEAN + c, 0.5 * (left(MEAN + c) + right(MEAN + c)))
    gap = {}
    for k, (i, j) in enumerate(pairs):
        a, b = left(UU + k), right(UU + k)
        gap[i, j] = gap[j, i] = a - b
        put(UU + k, (a + b) + nh[i] * half[j])
    for k, (i, j, l) in enumerate(triples):
        fix = half[i] * gap[j, l] + half[j] * gap[i, l] + half[l] * gap[i, j]
        put(UUU + k, (left(UUU + k) + right(UUU + k)) + fix)
    for c in range(3):
        put(PU + c, (left(PU + c) + right(PU + c)) + nh[3] * half[c])


def combine_slopes(left, right, count, dmat, put):
    half = [0.5 * (left(MEAN + c) - right(MEAN + c)) for c in range(4)]
    gx = [0.5 * (left(DXM + c) - right(DXM + c)) for c in range(4)]
    rows = half[0].shape[0]
    turned = jnp.dot(
        jnp.concatenate(half, axis=0), dmat,
        precision=lax.Precision.HIGHEST, preferred_element_type=F32,
    )
    gy = [turned[c * rows : (c + 1) * rows] for c in range(4)]
    both = float(2 * count)
    nh = [both * h for h in half]
    for c in range(4):
        put(DXM + c, 0.5 * (left(DXM + c) + right(DXM + c)))
    fixes = (
        2.0 * nh[3] * gx[0],
        nh[3] * (gy[0] + gx[1]),
        nh[3] * gx[2],
        2.0 * nh[3] * gy[1],
        nh[3] * gy[2],
    )
    for k in range(5):
        put(PG + k, (left(PG + k) + right(PG + k)) + fixes[k])
    put(PG + 5, left(PG + 5) + right(PG + 5))
    for k, (i, j) in enumerate(pairs):
        fix = both * (gx[i] * gx[j] + gy[i] * gy[j])
        put(GG + k, (left(GG + k) + right(GG + k)) + fix)
    fixes = (
        2.0 * nh[0] * gx[3],
        nh[0] * gy[3] + nh[1] * gx[3],
        nh[2] * gx[3],
        2.0 * nh[1] * gy[3],
        nh[2] * gy[3],
    )
    for k in range(5):
        put(UG + k, (left(UG + k) + right(UG + k)) - fixes[k])


def copy_all(copies):
    for c in copies:
        c.start()
    for c in copies:
        c.wait()


def rim_kernel(flow, zl, zr, xl, xr, sems):
    _, lx, lz, _ = flow.shape
    copy_all([
        pltpu.make_async_copy(flow.at[pl.ds(0, 3), :, pl.ds(lz - 4, 4)], zl, sems.at[0]),
        pltpu.make_async_copy(flow.at[pl.ds(0, 3), :, pl.ds(0, 4)], zr, sems.at[1]),
        pltpu.make_async_copy(flow.at[:, pl.ds(lx - 4, 4)], xl, sems.at[2]),
        pltpu.make_async_copy(flow.at[:, pl.ds(0, 4)], xr, sems.at[3]),
    ])


def cut(kernel, shapes, copies, name, flow, *after):
    flow = pltpu.with_memory_space_constraint(flow, pltpu.HBM)
    return pl.pallas_call(
        kernel,
        in_specs=[pl.BlockSpec(memory_space=pltpu.HBM)]
        + [pl.BlockSpec(memory_space=pl.ANY)] * len(after),
        out_specs=[pl.BlockSpec(memory_space=pltpu.VMEM)] * len(shapes),
        out_shape=[pltpu.VMEM(s, F32) for s in shapes],
        scratch_shapes=[pltpu.SemaphoreType.DMA((copies,))],
        compiler_params=pltpu.CompilerParams(vmem_limit_bytes=4 * 2**20),
        name=name,
    )(flow, *after)


def base_kernel(flow, dy, pad, ysl, mean, keep, send, dmat, acc, weights, sems):
    _, lx, lz, ny = ysl.shape
    half = lx // 2
    core = lax.axis_index(CA)
    step = 8
    parts = lx // step

    def fetch(k):
        return pltpu.make_async_copy(
            flow.at[:, pl.ds(step * k, step)],
            pad.at[:, pl.ds(step * k + 4, step), pl.ds(8, lz)],
            sems.at[k],
        )

    for k in range(parts):
        fetch(k).start()

    d = dy[...].T * (1.0 / lead)
    dmat[...] = d
    dhi = d.astype(BF16)
    dlo = (d - dhi.astype(F32)).astype(BF16)
    weights[pl.ds(0, ny), pl.ds(0, ny)] = dhi
    weights[pl.ds(0, ny), pl.ds(ny, ny)] = dlo
    weights[pl.ds(ny, ny), pl.ds(0, ny)] = dhi
    weights[pl.ds(ny, ny), pl.ds(ny, ny)] = jnp.zeros_like(dlo)

    def part(k, _):
        fetch(k).wait()
        left = []
        for r in range(step):
            x = step * k + r
            for c in range(4):
                f = pad[c, x + 4, pl.ds(8, lz), :]
                m = jnp.sum(f, axis=0, keepdims=True) * (1.0 / lz)
                mean[c, pl.ds(x, 1), :] = m
                a = f - m
                pad[c, x + 4, pl.ds(8, lz), :] = a
                hi = a.astype(BF16)
                lo = (a - hi.astype(F32)).astype(BF16)
                left.append(jnp.concatenate([hi, lo], axis=1))
        y = jnp.dot(jnp.concatenate(left, axis=0), weights[...], preferred_element_type=F32)
        for r in range(step):
            x = step * k + r
            total = [None] * NBASE

            def add(n, v):
                total[n] = v if total[n] is None else total[n] + v

            for b in range(lz // 8):
                f = [pad[c, x + 4, pl.ds(8 + 8 * b, 8), :] for c in range(4)]
                prod = {}
                for n, (i, j) in enumerate(pairs):
                    prod[i, j] = f[i] * f[j]
                    add(n, prod[i, j])
                for n, (i, j, l) in enumerate(triples):
                    add(6 + n, prod[i, j] * f[l])
                for c in range(3):
                    add(16 + c, f[3] * f[c])
            for n in range(NBASE):
                acc[pl.ds(pl.multiple_of(n * 8 * lx + 8 * x, 8), 8), :] = total[n]
        y = y[:, :ny] + y[:, ny:]
        for r in range(step):
            for c in range(4):
                at = (4 * r + c) * lz
                ysl[c, step * k + r] = y[at : at + lz]
        return 0

    lax.fori_loop(0, parts, part, 0)
    for out, side in ((send, 1 - core), (keep, core)):
        at = pl.multiple_of(half * side, 8)
        for c in range(4):
            out[MEAN + c] = mean[c, pl.ds(at, half), :]
        for k in range(NBASE):
            out[UU + k] = half_sum(k, acc, lx, at)


def row_sum(k, rows, acc):
    return sum(acc[pl.ds(8 * k * rows + s, rows, stride=8), :] for s in range(8))


def half_sum(k, acc, rows, at):
    where = pl.multiple_of(8 * (k * rows + at), 8)
    return sum(acc[pl.ds(where + s, rows // 2, stride=8), :] for s in range(8))


def base_moments(flow, dy):
    _, lx, lz, ny = flow.shape
    vm = pl.BlockSpec(memory_space=pltpu.VMEM)
    half = (FIRST, lx // 2, ny)
    shapes = [
        (4, lx + 8, lz + 16, ny), (4, lx, lz, ny), (4, lx, ny), half, half, (ny, ny),
    ]
    return pl.pallas_call(
        base_kernel,
        in_specs=[pl.BlockSpec(memory_space=pltpu.HBM), vm],
        out_specs=[vm] * 6,
        out_shape=[pltpu.VMEM(s, F32) for s in shapes],
        scratch_shapes=[
            pltpu.VMEM((NBASE * 8 * lx, ny), F32),
            pltpu.VMEM((2 * ny, 2 * ny), BF16),
            pltpu.SemaphoreType.DMA((lx // 8,)),
        ],
        compiler_params=pltpu.CompilerParams(vmem_limit_bytes=16 * 2**20),
        cost_estimate=pl.CostEstimate(flops=1000, bytes_accessed=1000, transcendentals=0),
        name="base_moments",
    )(pltpu.with_memory_space_constraint(flow, pltpu.HBM), dy)


def difference(upper, lower):
    out = None
    for k in range(4):
        diff = upper(k) - lower(k)
        out = diff if out is None else out + ratios[k] * diff
    return out


def slope_row(pad, ysl, x):
    lz, ny = ysl.shape[2:]
    total = [None] * NSLOPE
    row = lax.broadcasted_iota(jnp.int32, (8, ny), 0)
    row = jnp.minimum(row, 7 - row)
    weight = jnp.full((8, ny), sum(ratios), F32)
    for k in range(3):
        weight = jnp.where(row == k, sum(ratios[3 - k :]), weight)
    for c in range(3):
        total[c] = weight * (
            pad[c, x + 4, pl.ds(4 + lz, 8), :] - pad[c, x + 4, pl.ds(4, 8), :]
        )

    def add(k, v):
        total[k] = v if total[k] is None else total[k] + v

    for b in range(lz // 8):
        at = 8 + 8 * b
        u = [pad[c, x + 4, pl.ds(at, 8), :] for c in range(4)]
        p = u[3]
        g = [[None] * 3 for _ in range(4)]
        for c in range(4):
            g[c][0] = difference(
                lambda k: pad[c, x + 5 + k, pl.ds(at, 8), :],
                lambda k: pad[c, x + 3 - k, pl.ds(at, 8), :],
            )
            g[c][1] = ysl[c, x, pl.ds(8 * b, 8), :]
        for c in range(3):
            g[c][2] = difference(
                lambda k: pad[c, x + 4, pl.ds(at + 1 + k, 8), :],
                lambda k: pad[c, x + 4, pl.ds(at - 1 - k, 8), :],
            )
        add(3, p * g[0][0])
        add(4, p * (g[0][1] + g[1][0]))
        add(5, p * g[0][2])
        add(6, p * g[2][0])
        add(7, p * g[1][1])
        add(8, p * g[1][2])
        add(9, p * g[2][1])
        add(10, p * g[2][2])
        for k, (i, j) in enumerate(pairs):
            for dim in range(3):
                add(11 + k, g[i][dim] * g[j][dim])
        add(17, u[0] * g[3][0])
        add(18, u[0] * g[3][1] + u[1] * g[3][0])
        add(19, u[1] * g[3][1])
        add(20, u[2] * g[3][0])
        add(21, u[2] * g[3][1])
    return total


def slope_fields(total, pressure):
    s02, s12, s22 = (total(n) + pressure * total(c) for c, n in enumerate((5, 8, 10)))
    yield PG + 0, 2.0 * total(3)
    yield PG + 1, total(4)
    yield PG + 2, s02 + total(6)
    yield PG + 3, 2.0 * total(7)
    yield PG + 4, s12 + total(9)
    yield PG + 5, 2.0 * s22
    for k in range(6):
        yield GG + k, total(11 + k)
    yield UG + 0, -2.0 * total(17)
    yield UG + 1, -total(18)
    yield UG + 2, s02 - total(20)
    yield UG + 3, -2.0 * total(19)
    yield UG + 4, s12 - total(21)


def inner_kernel(pad_in, ysl, zl, zr, mean, after, pad, keep, send, acc):
    _, lx, lz, ny = ysl.shape
    half = lx // 2
    core = lax.axis_index(CA)

    def rim(x, _):
        for c in range(3):
            m = mean[c, pl.ds(x, 1), :]
            pad[c, x + 4, pl.ds(4, 4), :] = zl[c, x] - m
            pad[c, x + 4, pl.ds(8 + lz, 4), :] = zr[c, x] - m
        return 0

    lax.fori_loop(0, lx, rim, 0, unroll=4)

    def one(x, _):
        total = slope_row(pad, ysl, x)
        for k in range(NSLOPE):
            acc[pl.ds(pl.multiple_of(k * 8 * lx + 8 * x, 8), 8), :] = total[k]
        return 0

    lax.fori_loop(4, lx - 4, one, 0)

    for out, side in ((send, 1 - core), (keep, core)):
        at = pl.multiple_of(half * side, 8)

        fields = slope_fields(
            lambda k, at=at: half_sum(k, acc, lx, at), mean[3, pl.ds(at, half), :]
        )
        for f, v in fields:
            out[f - FIRST] = v


def inner_moments(pad, ysl, zl, zr, mean, after):
    _, lx, lz, ny = ysl.shape
    vm = pl.BlockSpec(memory_space=pltpu.VMEM)
    shape = pltpu.VMEM((STATE - FIRST, lx // 2, ny), F32)
    return pl.pallas_call(
        inner_kernel,
        in_specs=[vm] * 5 + [pl.BlockSpec(memory_space=pl.ANY)],
        out_specs=[vm] * 3,
        out_shape=[pltpu.VMEM(pad.shape, F32), shape, shape],
        input_output_aliases={0: 0},
        scratch_shapes=[pltpu.VMEM((NSLOPE * 8 * lx, ny), F32)],
        compiler_params=pltpu.CompilerParams(vmem_limit_bytes=16 * 2**20),
        cost_estimate=pl.CostEstimate(
            flops=1500000000, bytes_accessed=84_000_000, transcendentals=0
        ),
        name="inner_moments",
    )(pad, ysl, zl, zr, mean, after)


def edge_kernel(
    pad_in, keep_in, send_in, ysl, xl, xr, mean, after, pad, keep, send, acc, mpad, dxm
):
    _, lx, lz, ny = ysl.shape
    half = lx // 2
    core = lax.axis_index(CA)
    gi = lax.axis_index(GXA)
    at_ends = (gi == 0, gi == lax.axis_size(GXA) - 1)

    for c in range(4):
        mpad[c, pl.ds(8, lx), :] = mean[c]
        for j in range(4):
            for halo, at_end, src, dst in (
                (xl, at_ends[0], 3 - j, j), (xr, at_ends[1], lx - 1 - j, lx + 4 + j)
            ):
                own = pad[c, src + 4, pl.ds(8, lz), :]
                m = jnp.sum(halo[c, j], axis=0, keepdims=True) * (1.0 / lz)
                pad[c, dst, pl.ds(8, lz), :] = jnp.where(at_end, own, halo[c, j] - m)
                mpad[c, pl.ds(dst + 4, 1), :] = jnp.where(at_end, mean[c, pl.ds(src, 1), :], m)
        dxm[c] = difference(
            lambda k: mpad[c, pl.ds(9 + k, lx), :], lambda k: mpad[c, pl.ds(7 - k, lx), :]
        )

    for out, side in ((send, 1 - core), (keep, core)):
        for c in range(4):
            out[DXM - FIRST + c] = dxm[c, pl.ds(pl.multiple_of(half * side, 8), half), :]

    def one(i, _):
        x = jnp.where(i < 4, i, lx - 8 + i)
        total = slope_row(pad, ysl, x)
        for k in range(NSLOPE):
            acc[pl.ds(pl.multiple_of(k * 64 + 8 * i, 8), 8), :] = total[k]
        return 0

    lax.fori_loop(0, 8, one, 0)

    pressure = jnp.concatenate([mean[3, pl.ds(0, 4), :], mean[3, pl.ds(lx - 4, 4), :]], axis=0)
    fields = list(slope_fields(lambda k: row_sum(k, 8, acc), pressure))
    for side, rows in ((0, slice(0, 4)), (1, slice(4, 8))):
        at = 0 if side == 0 else half - 4

        @pl.when(core == side)
        def _():
            for f, v in fields:
                keep[f - FIRST, pl.ds(at, 4), :] = v[rows]

        @pl.when(core != side)
        def _():
            for f, v in fields:
                send[f - FIRST, pl.ds(at, 4), :] = v[rows]


def edge_moments(pad, keep, send, ysl, xl, xr, mean, after):
    _, lx, lz, ny = ysl.shape
    vm = pl.BlockSpec(memory_space=pltpu.VMEM)
    out = pl.pallas_call(
        edge_kernel,
        in_specs=[vm] * 7 + [pl.BlockSpec(memory_space=pl.ANY)],
        out_specs=[vm] * 3,
        out_shape=[pltpu.VMEM(v.shape, F32) for v in (pad, keep, send)],
        input_output_aliases={0: 0, 1: 1, 2: 2},
        scratch_shapes=[
            pltpu.VMEM((NSLOPE * 64, ny), F32),
            pltpu.VMEM((4, lx + 16, ny), F32),
            pltpu.VMEM((4, lx, ny), F32),
        ],
        compiler_params=pltpu.CompilerParams(vmem_limit_bytes=16 * 2**20),
        cost_estimate=pl.CostEstimate(
            flops=25 * ysl.size, bytes_accessed=ysl.size // 2, transcendentals=0
        ),
        name="edge_moments",
    )(pad, keep, send, ysl, xl, xr, mean, after)
    return out[1:]


def picker(one, two=None):
    return lambda f: one[f] if f < FIRST else two[f - FIRST]


def storer(one, two=None):
    def put(f, v):
        if f < FIRST:
            one[f] = v
        else:
            two[f - FIRST] = v
    return put


def z_places(rows):
    zi = lax.axis_index("z")
    zn = lax.axis_size("z")
    return [pl.multiple_of(rows * lax.rem(zi + k, zn), 8) for k in (0, 1, zn - 1, 2)]


def core_base_kernel(count, keep, got, *outs):
    rows = outs[0].shape[1]
    for out, at in zip(outs, z_places(rows)):
        combine_base(
            lambda f, at=at: keep[f, pl.ds(at, rows), :],
            lambda f, at=at: got[f, pl.ds(at, rows), :],
            count, storer(out),
        )


def core_slope_kernel(count, keep1, got1, keep2, got2, dmat, *outs):
    rows = outs[0].shape[1]
    places = z_places(rows)

    def pick(one, two):
        def field(f):
            ref, k = (one, f) if f < FIRST else (two, f - FIRST)
            return jnp.concatenate([ref[k, pl.ds(at, rows), :] for at in places], axis=0)
        return field

    def put(f, v):
        for n, ref in enumerate(outs):
            ref[f - FIRST] = v[rows * n : rows * (n + 1)]

    combine_slopes(pick(keep1, keep2), pick(got1, got2), count, dmat[...], put)


def span_base_kernel(count, own, one, two, three, out, left, right):
    combine_base(picker(own), picker(one), count, storer(left))
    combine_base(picker(two), picker(three), count, storer(right))
    combine_base(picker(left), picker(right), 2 * count, storer(out))


def span_slope_kernel(count, *refs):
    base, (own, one, two, three) = refs[:4], refs[4:8]
    left1, right1, dmat, out, left, right = refs[8:]
    d = dmat[...]
    combine_slopes(picker(base[0], own), picker(base[1], one), count, d, storer(None, left))
    combine_slopes(picker(base[2], two), picker(base[3], three), count, d, storer(None, right))
    combine_slopes(
        picker(left1, left), picker(right1, right), 2 * count, d, storer(None, out)
    )


def last_base_kernel(count, mine, other, out, state):
    combine_base(picker(mine), picker(other), count, storer(state))
    scale = 1.0 / (2 * count)
    for c in range(3):
        out[c] = state[MEAN + c]
    for k in range(NBASE):
        out[3 + k] = state[UU + k] * scale


def last_slope_kernel(count, mine1, other1, mine2, other2, dmat, out, state):
    combine_slopes(
        picker(mine1, mine2), picker(other1, other2), count, dmat[...], storer(None, state)
    )
    scale = 1.0 / (2 * count)
    for k in range(6):
        out[k] = state[PG - FIRST + k] * (scale * lead)
        out[6 + k] = state[GG - FIRST + k] * (scale * lead * lead)
    for k in range(5):
        out[12 + k] = state[UG - FIRST + k] * (scale * lead)
    out[17] = state[PG - FIRST + 5] * (scale * lead)


def place_kernel(first, *refs):
    ins, out, sems = refs[:8], refs[-2], refs[-1]
    fields, rows = ins[0].shape[:2]
    zi = lax.axis_index("z")
    zn = lax.axis_size("z")
    core = lax.axis_index(CA)
    copies = []
    for k, ref in enumerate(ins):
        side, step = divmod(k, zn)
        c = core if side == 0 else 1 - core
        at = pl.multiple_of(rows * (zn * c + lax.rem(zi + zn - step, zn)), 8)
        copies.append(
            pltpu.make_async_copy(
                ref, out.at[pl.ds(first, fields), pl.ds(at, rows)], sems.at[k]
            )
        )
    copy_all(copies)


def place(first, pieces, shape, name, base=None):
    hbm = pl.BlockSpec(memory_space=pltpu.HBM)
    extra = [] if base is None else [base]
    return pl.pallas_call(
        functools.partial(place_kernel, first),
        in_specs=[pl.BlockSpec(memory_space=pltpu.VMEM)] * len(pieces) + [hbm] * len(extra),
        out_specs=hbm,
        out_shape=pltpu.HBM(shape, F32),
        input_output_aliases={} if base is None else {len(pieces): 0},
        scratch_shapes=[pltpu.SemaphoreType.DMA((len(pieces),))],
        compiler_params=pltpu.CompilerParams(vmem_limit_bytes=4 * 2**20),
        name=name,
    )(*pieces, *extra)


def small_call(kernel, outs, scratch, name, *args):
    vm = pl.BlockSpec(memory_space=pltpu.VMEM)
    return pl.pallas_call(
        kernel,
        in_specs=[vm] * len(args),
        out_specs=[vm] * len(outs),
        out_shape=[pltpu.VMEM(s, F32) for s in outs],
        scratch_shapes=[pltpu.VMEM(s, F32) for s in scratch],
        compiler_params=pltpu.CompilerParams(vmem_limit_bytes=8 * 2**20),
        cost_estimate=pl.CostEstimate(flops=1000, bytes_accessed=1000, transcendentals=0),
        name=name,
    )(*args)


def send(value, axis, step):
    size = lax.axis_size(axis)
    return lax.ppermute(value, axis, [(i, (i + step) % size) for i in range(size)])


def shards(flow, dy):
    _, lx, lz, ny = flow.shape
    gn = lax.axis_size(GXA)
    zn = lax.axis_size("z")
    up = [(i, i + 1) for i in range(gn - 1)]
    down = [(i + 1, i) for i in range(gn - 1)]
    zs, xs = (3, lx, 4, ny), (4, 4, lz, ny)
    zl, zr, xl, xr = cut(rim_kernel, [zs, zs, xs, xs], 4, "rims", flow)
    with jax.named_scope("rim_exchange"):
        zl = send(zl, ZA, 1)
        zr = send(zr, ZA, -1)
        xl = lax.ppermute(xl, GXA, up)
        xr = lax.ppermute(xr, GXA, down)
    pad, ysl, mean, keep1, give1, dmat = base_moments(flow, dy)
    rows = lx // 2 // zn
    one_piece, two_piece = (FIRST, rows, ny), (STATE - FIRST, rows, ny)

    def along_z(own, up, down, far):
        return [own, send(up, "z", 1), send(far, "z", 2), send(down, "z", -1)]

    def spread(done):
        mine = [done] + [send(done, "z", k) for k in (1, 2, 3)]
        return mine + [send(v, CA, 1) for v in mine]

    with jax.named_scope("base_core"):
        got1 = send(give1, CA, 1)
        parts1 = small_call(
            functools.partial(core_base_kernel, lz), [one_piece] * 4, [], "core_base", keep1, got1
        )
    with jax.named_scope("base_span"):
        pieces1 = along_z(*parts1)
    pad, keep2, give2 = inner_moments(pad, ysl, zl, zr, mean, parts1[0])
    with jax.named_scope("base_span"):
        part1, left1, right1 = small_call(
            functools.partial(span_base_kernel, 2 * lz), [one_piece] * 3, [], "span_base", *pieces1
        )
    with jax.named_scope("base_x"):
        other1 = send(part1, "xh", 1)
        (done1,) = small_call(
            functools.partial(last_base_kernel, 2 * zn * lz),
            [(FIRST - 1, rows, ny)], [one_piece], "last_base", part1, other1,
        )
    with jax.named_scope("base_spread"):
        out1 = place(0, spread(done1), (OUT, lx, ny), "place_base")
    keep2, give2 = edge_moments(pad, keep2, give2, ysl, xl, xr, mean, part1)
    with jax.named_scope("slope_core"):
        got2 = send(give2, CA, 1)
        parts2 = small_call(
            functools.partial(core_slope_kernel, lz), [two_piece] * 4, [], "core_slope",
            keep1, got1, keep2, got2, dmat,
        )
    with jax.named_scope("slope_span"):
        pieces2 = along_z(*parts2)
        (part2,) = small_call(
            functools.partial(span_slope_kernel, 2 * lz), [two_piece], [two_piece] * 2,
            "span_slope", *pieces1, *pieces2, left1, right1, dmat,
        )
    with jax.named_scope("slope_x"):
        other2 = send(part2, "xh", 1)
        (done2,) = small_call(
            functools.partial(last_slope_kernel, 2 * zn * lz),
            [(OUT - FIRST + 1, rows, ny)], [two_piece], "last_slope",
            part1, other1, part2, other2, dmat,
        )
    with jax.named_scope("slope_spread"):
        return place(FIRST - 1, spread(done2), (OUT, lx, ny), "place_slope", out1)


def solution(mesh):
    gx, gz = mesh.shape["gx"], mesh.shape["gz"]
    fine = Mesh(mesh.devices.reshape(gx, 2, gz // 4, 2), (GXA,) + ZA)
    return jax.shard_map(
        shards,
        mesh=fine,
        in_specs=(P(None, GXA, ZA, None), P()),
        out_specs=P(None, GXA, None),
        check_vma=False,
    )
```

```python
import functools

import jax
import jax.numpy as jnp
from jax import lax
from jax.experimental import pallas as pl
from jax.experimental.pallas import tpu as pltpu
from jax.sharding import Mesh, PartitionSpec as P

F32 = jnp.float32
BF16 = jnp.bfloat16
lead = 4.0 / 5.0
ratios = (1.0, -0.25, 1.0 / 21.0, -1.0 / 224.0)
pairs = ((0, 0), (0, 1), (0, 2), (1, 1), (1, 2), (2, 2))
triples = (
    (0, 0, 0), (0, 0, 1), (0, 0, 2), (0, 1, 1), (0, 1, 2),
    (0, 2, 2), (1, 1, 1), (1, 1, 2), (1, 2, 2), (2, 2, 2),
)
MEAN, UU, UUU, PU, DXM, PG, GG, UG = 0, 4, 10, 20, 23, 27, 33, 39
FIRST = 23
STATE = 44
OUT = 40
NBASE = 19
NSLOPE = 22
GXA, ZA, CA = "gx", ("xh", "z", "c"), "c"


def combine_base(left, right, count, put):
    half = [0.5 * (left(MEAN + c) - right(MEAN + c)) for c in range(4)]
    nh = [float(2 * count) * h for h in half]
    for c in range(4):
        put(MEAN + c, 0.5 * (left(MEAN + c) + right(MEAN + c)))
    gap = {}
    for k, (i, j) in enumerate(pairs):
        a, b = left(UU + k), right(UU + k)
        gap[i, j] = gap[j, i] = a - b
        put(UU + k, (a + b) + nh[i] * half[j])
    for k, (i, j, l) in enumerate(triples):
        fix = half[i] * gap[j, l] + half[j] * gap[i, l] + half[l] * gap[i, j]
        put(UUU + k, (left(UUU + k) + right(UUU + k)) + fix)
    for c in range(3):
        put(PU + c, (left(PU + c) + right(PU + c)) + nh[3] * half[c])


def combine_slopes(left, right, count, dmat, put):
    half = [0.5 * (left(MEAN + c) - right(MEAN + c)) for c in range(4)]
    gx = [0.5 * (left(DXM + c) - right(DXM + c)) for c in range(4)]
    rows = half[0].shape[0]
    turned = jnp.dot(
        jnp.concatenate(half, axis=0), dmat,
        precision=lax.Precision.HIGHEST, preferred_element_type=F32,
    )
    gy = [turned[c * rows : (c + 1) * rows] for c in range(4)]
    both = float(2 * count)
    nh = [both * h for h in half]
    for c in range(4):
        put(DXM + c, 0.5 * (left(DXM + c) + right(DXM + c)))
    fixes = (
        2.0 * nh[3] * gx[0],
        nh[3] * (gy[0] + gx[1]),
        nh[3] * gx[2],
        2.0 * nh[3] * gy[1],
        nh[3] * gy[2],
    )
    for k in range(5):
        put(PG + k, (left(PG + k) + right(PG + k)) + fixes[k])
    put(PG + 5, left(PG + 5) + right(PG + 5))
    for k, (i, j) in enumerate(pairs):
        fix = both * (gx[i] * gx[j] + gy[i] * gy[j])
        put(GG + k, (left(GG + k) + right(GG + k)) + fix)
    fixes = (
        2.0 * nh[0] * gx[3],
        nh[0] * gy[3] + nh[1] * gx[3],
        nh[2] * gx[3],
        2.0 * nh[1] * gy[3],
        nh[2] * gy[3],
    )
    for k in range(5):
        put(UG + k, (left(UG + k) + right(UG + k)) - fixes[k])


def copy_all(copies):
    for c in copies:
        c.start()
    for c in copies:
        c.wait()


def rim_kernel(flow, zl, zr, xl, xr, sems):
    _, lx, lz, _ = flow.shape
    copy_all([
        pltpu.make_async_copy(flow.at[pl.ds(0, 3), :, pl.ds(lz - 4, 4)], zl, sems.at[0]),
        pltpu.make_async_copy(flow.at[pl.ds(0, 3), :, pl.ds(0, 4)], zr, sems.at[1]),
        pltpu.make_async_copy(flow.at[:, pl.ds(lx - 4, 4)], xl, sems.at[2]),
        pltpu.make_async_copy(flow.at[:, pl.ds(0, 4)], xr, sems.at[3]),
    ])


def cut(kernel, shapes, copies, name, flow, *after):
    flow = pltpu.with_memory_space_constraint(flow, pltpu.HBM)
    return pl.pallas_call(
        kernel,
        in_specs=[pl.BlockSpec(memory_space=pltpu.HBM)]
        + [pl.BlockSpec(memory_space=pl.ANY)] * len(after),
        out_specs=[pl.BlockSpec(memory_space=pltpu.VMEM)] * len(shapes),
        out_shape=[pltpu.VMEM(s, F32) for s in shapes],
        scratch_shapes=[pltpu.SemaphoreType.DMA((copies,))],
        compiler_params=pltpu.CompilerParams(vmem_limit_bytes=4 * 2**20),
        name=name,
    )(flow, *after)


def base_kernel(flow, pad, mean, keep, send, raw, acc, sems):
    _, lx, ny = mean.shape
    lz = pad.shape[2] - 16
    half = lx // 2
    core = lax.axis_index(CA)
    step = 8
    parts = lx // step

    def fetch(k):
        return pltpu.make_async_copy(
            flow.at[:, pl.ds(step * k, step)],
            raw.at[:, pl.ds(step * k, step)],
            sems.at[k],
        )

    for k in range(parts):
        fetch(k).start()

    def one(x, _):
        centre = []
        for c in range(4):
            m = jnp.sum(raw[c, x], axis=0, keepdims=True) * (1.0 / lz)
            mean[c, pl.ds(x, 1), :] = m
            centre.append(m)
        total = [None] * NBASE

        def add(n, v):
            total[n] = v if total[n] is None else total[n] + v

        for b in range(lz // 8):
            f = [raw[c, x, pl.ds(8 * b, 8), :] - centre[c] for c in range(4)]
            for c in range(4):
                pad[c, x + 4, pl.ds(8 + 8 * b, 8), :] = f[c]
            prod = {}
            for n, (i, j) in enumerate(pairs):
                prod[i, j] = f[i] * f[j]
                add(n, prod[i, j])
            for n, (i, j, l) in enumerate(triples):
                add(6 + n, prod[i, j] * f[l])
            for c in range(3):
                add(16 + c, f[3] * f[c])
        for n in range(NBASE):
            acc[pl.ds(pl.multiple_of(n * 8 * lx + 8 * x, 8), 8), :] = total[n]
        return 0

    def part(k, _):
        fetch(k).wait()
        return lax.fori_loop(0, step, lambda r, _: one(step * k + r, _), 0, unroll=2)

    lax.fori_loop(0, parts, part, 0)
    for out, side in ((send, 1 - core), (keep, core)):
        at = pl.multiple_of(half * side, 8)
        for c in range(4):
            out[MEAN + c] = mean[c, pl.ds(at, half), :]
        for k in range(NBASE):
            out[UU + k] = half_sum(k, acc, lx, at)


def y_kernel(pad, dy, ysl, dmat, weights):
    _, lx, lz, ny = ysl.shape
    step = 8
    d = dy[...].T * (1.0 / lead)
    dmat[...] = d
    dhi = d.astype(BF16)
    dlo = (d - dhi.astype(F32)).astype(BF16)
    weights[pl.ds(0, ny), pl.ds(0, ny)] = dhi
    weights[pl.ds(0, ny), pl.ds(ny, ny)] = dlo
    weights[pl.ds(ny, ny), pl.ds(0, ny)] = dhi
    weights[pl.ds(ny, ny), pl.ds(ny, ny)] = jnp.zeros_like(dlo)

    def part(k, _):
        left = []
        for r in range(step):
            for c in range(4):
                a = pad[c, step * k + r + 4, pl.ds(8, lz), :]
                hi = a.astype(BF16)
                lo = (a - hi.astype(F32)).astype(BF16)
                left.append(jnp.concatenate([hi, lo], axis=1))
        y = jnp.dot(jnp.concatenate(left, axis=0), weights[...], preferred_element_type=F32)
        y = y[:, :ny] + y[:, ny:]
        for r in range(step):
            for c in range(4):
                at = (4 * r + c) * lz
                ysl[c, step * k + r] = y[at : at + lz]
        return 0

    lax.fori_loop(0, lx // step, part, 0)


def row_sum(k, rows, acc):
    return sum(acc[pl.ds(8 * k * rows + s, rows, stride=8), :] for s in range(8))


def half_sum(k, acc, rows, at):
    where = pl.multiple_of(8 * (k * rows + at), 8)
    return sum(acc[pl.ds(where + s, rows // 2, stride=8), :] for s in range(8))


def base_moments(flow):
    _, lx, lz, ny = flow.shape
    vm = pl.BlockSpec(memory_space=pltpu.VMEM)
    half = (FIRST, lx // 2, ny)
    shapes = [(4, lx + 8, lz + 16, ny), (4, lx, ny), half, half]
    return pl.pallas_call(
        base_kernel,
        in_specs=[pl.BlockSpec(memory_space=pltpu.HBM)],
        out_specs=[vm] * 4,
        out_shape=[pltpu.VMEM(s, F32) for s in shapes],
        scratch_shapes=[
            pltpu.VMEM((4, lx, lz, ny), F32),
            pltpu.VMEM((NBASE * 8 * lx, ny), F32),
            pltpu.SemaphoreType.DMA((lx // 8,)),
        ],
        compiler_params=pltpu.CompilerParams(vmem_limit_bytes=16 * 2**20),
        cost_estimate=pl.CostEstimate(flops=1000, bytes_accessed=1000, transcendentals=0),
        name="base_moments",
    )(pltpu.with_memory_space_constraint(flow, pltpu.HBM))


def y_slopes(pad, dy):
    ny = dy.shape[0]
    lx, lz = pad.shape[1] - 8, pad.shape[2] - 16
    vm = pl.BlockSpec(memory_space=pltpu.VMEM)
    return pl.pallas_call(
        y_kernel,
        in_specs=[vm, vm],
        out_specs=[vm, vm],
        out_shape=[pltpu.VMEM((4, lx, lz, ny), F32), pltpu.VMEM((ny, ny), F32)],
        scratch_shapes=[pltpu.VMEM((2 * ny, 2 * ny), BF16)],
        compiler_params=pltpu.CompilerParams(vmem_limit_bytes=16 * 2**20),
        cost_estimate=pl.CostEstimate(flops=1000, bytes_accessed=1000, transcendentals=0),
        name="y_slopes",
    )(pad, dy)


def difference(upper, lower):
    out = None
    for k in range(4):
        diff = upper(k) - lower(k)
        out = diff if out is None else out + ratios[k] * diff
    return out


def slope_row(pad, ysl, x):
    lz, ny = ysl.shape[2:]
    total = [None] * NSLOPE
    row = lax.broadcasted_iota(jnp.int32, (8, ny), 0)
    row = jnp.minimum(row, 7 - row)
    weight = jnp.full((8, ny), sum(ratios), F32)
    for k in range(3):
        weight = jnp.where(row == k, sum(ratios[3 - k :]), weight)
    for c in range(3):
        total[c] = weight * (
            pad[c, x + 4, pl.ds(4 + lz, 8), :] - pad[c, x + 4, pl.ds(4, 8), :]
        )

    def add(k, v):
        total[k] = v if total[k] is None else total[k] + v

    for b in range(lz // 8):
        at = 8 + 8 * b
        u = [pad[c, x + 4, pl.ds(at, 8), :] for c in range(4)]
        p = u[3]
        g = [[None] * 3 for _ in range(4)]
        for c in range(4):
            g[c][0] = difference(
                lambda k: pad[c, x + 5 + k, pl.ds(at, 8), :],
                lambda k: pad[c, x + 3 - k, pl.ds(at, 8), :],
            )
            g[c][1] = ysl[c, x, pl.ds(8 * b, 8), :]
        for c in range(3):
            g[c][2] = difference(
                lambda k: pad[c, x + 4, pl.ds(at + 1 + k, 8), :],
                lambda k: pad[c, x + 4, pl.ds(at - 1 - k, 8), :],
            )
        add(3, p * g[0][0])
        add(4, p * (g[0][1] + g[1][0]))
        add(5, p * g[0][2])
        add(6, p * g[2][0])
        add(7, p * g[1][1])
        add(8, p * g[1][2])
        add(9, p * g[2][1])
        add(10, p * g[2][2])
        for k, (i, j) in enumerate(pairs):
            for dim in range(3):
                add(11 + k, g[i][dim] * g[j][dim])
        add(17, u[0] * g[3][0])
        add(18, u[0] * g[3][1] + u[1] * g[3][0])
        add(19, u[1] * g[3][1])
        add(20, u[2] * g[3][0])
        add(21, u[2] * g[3][1])
    return total


def slope_fields(total, pressure):
    s02, s12, s22 = (total(n) + pressure * total(c) for c, n in enumerate((5, 8, 10)))
    yield PG + 0, 2.0 * total(3)
    yield PG + 1, total(4)
    yield PG + 2, s02 + total(6)
    yield PG + 3, 2.0 * total(7)
    yield PG + 4, s12 + total(9)
    yield PG + 5, 2.0 * s22
    for k in range(6):
        yield GG + k, total(11 + k)
    yield UG + 0, -2.0 * total(17)
    yield UG + 1, -total(18)
    yield UG + 2, s02 - total(20)
    yield UG + 3, -2.0 * total(19)
    yield UG + 4, s12 - total(21)


def inner_kernel(pad_in, ysl, zl, zr, mean, after, pad, keep, send, acc):
    _, lx, lz, ny = ysl.shape
    half = lx // 2
    core = lax.axis_index(CA)

    def rim(x, _):
        for c in range(3):
            m = mean[c, pl.ds(x, 1), :]
            pad[c, x + 4, pl.ds(4, 4), :] = zl[c, x] - m
            pad[c, x + 4, pl.ds(8 + lz, 4), :] = zr[c, x] - m
        return 0

    lax.fori_loop(0, lx, rim, 0, unroll=4)

    def one(x, _):
        total = slope_row(pad, ysl, x)
        for k in range(NSLOPE):
            acc[pl.ds(pl.multiple_of(k * 8 * lx + 8 * x, 8), 8), :] = total[k]
        return 0

    lax.fori_loop(4, lx - 4, one, 0, unroll=4)

    for out, side in ((send, 1 - core), (keep, core)):
        at = pl.multiple_of(half * side, 8)

        fields = slope_fields(
            lambda k, at=at: half_sum(k, acc, lx, at), mean[3, pl.ds(at, half), :]
        )
        for f, v in fields:
            out[f - FIRST] = v


def inner_moments(pad, ysl, zl, zr, mean, after):
    _, lx, lz, ny = ysl.shape
    vm = pl.BlockSpec(memory_space=pltpu.VMEM)
    shape = pltpu.VMEM((STATE - FIRST, lx // 2, ny), F32)
    return pl.pallas_call(
        inner_kernel,
        in_specs=[vm] * 5 + [pl.BlockSpec(memory_space=pl.ANY)],
        out_specs=[vm] * 3,
        out_shape=[pltpu.VMEM(pad.shape, F32), shape, shape],
        input_output_aliases={0: 0},
        scratch_shapes=[pltpu.VMEM((NSLOPE * 8 * lx, ny), F32)],
        compiler_params=pltpu.CompilerParams(vmem_limit_bytes=16 * 2**20),
        cost_estimate=pl.CostEstimate(
            flops=1500000000, bytes_accessed=84_000_000, transcendentals=0
        ),
        name="inner_moments",
    )(pad, ysl, zl, zr, mean, after)


def edge_kernel(
    pad_in, keep_in, send_in, ysl, xl, xr, mean, after, pad, keep, send, acc, mpad, dxm
):
    _, lx, lz, ny = ysl.shape
    half = lx // 2
    core = lax.axis_index(CA)
    gi = lax.axis_index(GXA)
    at_ends = (gi == 0, gi == lax.axis_size(GXA) - 1)

    for c in range(4):
        mpad[c, pl.ds(8, lx), :] = mean[c]
        for j in range(4):
            for halo, at_end, src, dst in (
                (xl, at_ends[0], 3 - j, j), (xr, at_ends[1], lx - 1 - j, lx + 4 + j)
            ):
                own = pad[c, src + 4, pl.ds(8, lz), :]
                m = jnp.sum(halo[c, j], axis=0, keepdims=True) * (1.0 / lz)
                pad[c, dst, pl.ds(8, lz), :] = jnp.where(at_end, own, halo[c, j] - m)
                mpad[c, pl.ds(dst + 4, 1), :] = jnp.where(at_end, mean[c, pl.ds(src, 1), :], m)
        dxm[c] = difference(
            lambda k: mpad[c, pl.ds(9 + k, lx), :], lambda k: mpad[c, pl.ds(7 - k, lx), :]
        )

    for out, side in ((send, 1 - core), (keep, core)):
        for c in range(4):
            out[DXM - FIRST + c] = dxm[c, pl.ds(pl.multiple_of(half * side, 8), half), :]

    def one(i, _):
        x = jnp.where(i < 4, i, lx - 8 + i)
        total = slope_row(pad, ysl, x)
        for k in range(NSLOPE):
            acc[pl.ds(pl.multiple_of(k * 64 + 8 * i, 8), 8), :] = total[k]
        return 0

    lax.fori_loop(0, 8, one, 0)

    pressure = jnp.concatenate([mean[3, pl.ds(0, 4), :], mean[3, pl.ds(lx - 4, 4), :]], axis=0)
    fields = list(slope_fields(lambda k: row_sum(k, 8, acc), pressure))
    for side, rows in ((0, slice(0, 4)), (1, slice(4, 8))):
        at = 0 if side == 0 else half - 4

        @pl.when(core == side)
        def _():
            for f, v in fields:
                keep[f - FIRST, pl.ds(at, 4), :] = v[rows]

        @pl.when(core != side)
        def _():
            for f, v in fields:
                send[f - FIRST, pl.ds(at, 4), :] = v[rows]


def edge_moments(pad, keep, send, ysl, xl, xr, mean, after):
    _, lx, lz, ny = ysl.shape
    vm = pl.BlockSpec(memory_space=pltpu.VMEM)
    out = pl.pallas_call(
        edge_kernel,
        in_specs=[vm] * 7 + [pl.BlockSpec(memory_space=pl.ANY)],
        out_specs=[vm] * 3,
        out_shape=[pltpu.VMEM(v.shape, F32) for v in (pad, keep, send)],
        input_output_aliases={0: 0, 1: 1, 2: 2},
        scratch_shapes=[
            pltpu.VMEM((NSLOPE * 64, ny), F32),
            pltpu.VMEM((4, lx + 16, ny), F32),
            pltpu.VMEM((4, lx, ny), F32),
        ],
        compiler_params=pltpu.CompilerParams(vmem_limit_bytes=16 * 2**20),
        cost_estimate=pl.CostEstimate(
            flops=25 * ysl.size, bytes_accessed=ysl.size // 2, transcendentals=0
        ),
        name="edge_moments",
    )(pad, keep, send, ysl, xl, xr, mean, after)
    return out[1:]


def picker(one, two=None):
    return lambda f: one[f] if f < FIRST else two[f - FIRST]


def storer(one, two=None):
    def put(f, v):
        if f < FIRST:
            one[f] = v
        else:
            two[f - FIRST] = v
    return put


def z_places(rows):
    zi = lax.axis_index("z")
    zn = lax.axis_size("z")
    return [pl.multiple_of(rows * lax.rem(zi + k, zn), 8) for k in (0, 1, zn - 1, 2)]


def core_base_kernel(count, keep, got, *outs):
    rows = outs[0].shape[1]
    for out, at in zip(outs, z_places(rows)):
        combine_base(
            lambda f, at=at: keep[f, pl.ds(at, rows), :],
            lambda f, at=at: got[f, pl.ds(at, rows), :],
            count, storer(out),
        )


def core_slope_kernel(count, keep1, got1, keep2, got2, dmat, *outs):
    rows = outs[0].shape[1]
    places = z_places(rows)

    def pick(one, two):
        def field(f):
            ref, k = (one, f) if f < FIRST else (two, f - FIRST)
            return jnp.concatenate([ref[k, pl.ds(at, rows), :] for at in places], axis=0)
        return field

    def put(f, v):
        for n, ref in enumerate(outs):
            ref[f - FIRST] = v[rows * n : rows * (n + 1)]

    combine_slopes(pick(keep1, keep2), pick(got1, got2), count, dmat[...], put)


def span_base_kernel(count, own, one, two, three, out, left, right):
    combine_base(picker(own), picker(one), count, storer(left))
    combine_base(picker(two), picker(three), count, storer(right))
    combine_base(picker(left), picker(right), 2 * count, storer(out))


def span_slope_kernel(count, *refs):
    base, (own, one, two, three) = refs[:4], refs[4:8]
    left1, right1, dmat, out, left, right = refs[8:]
    d = dmat[...]
    combine_slopes(picker(base[0], own), picker(base[1], one), count, d, storer(None, left))
    combine_slopes(picker(base[2], two), picker(base[3], three), count, d, storer(None, right))
    combine_slopes(
        picker(left1, left), picker(right1, right), 2 * count, d, storer(None, out)
    )


def last_base_kernel(count, mine, other, after, out, state):
    combine_base(picker(mine), picker(other), count, storer(state))
    scale = 1.0 / (2 * count)
    for c in range(3):
        out[c] = state[MEAN + c]
    for k in range(NBASE):
        out[3 + k] = state[UU + k] * scale


def last_slope_kernel(count, mine1, other1, mine2, other2, dmat, out, state):
    combine_slopes(
        picker(mine1, mine2), picker(other1, other2), count, dmat[...], storer(None, state)
    )
    scale = 1.0 / (2 * count)
    for k in range(6):
        out[k] = state[PG - FIRST + k] * (scale * lead)
        out[6 + k] = state[GG - FIRST + k] * (scale * lead * lead)
    for k in range(5):
        out[12 + k] = state[UG - FIRST + k] * (scale * lead)
    out[17] = state[PG - FIRST + 5] * (scale * lead)


def gather_kernel(after, *refs):
    ins, out = refs[:-1], refs[-1]
    rows = ins[0].shape[1]
    zi = lax.axis_index("z")
    zn = lax.axis_size("z")
    for step, ref in enumerate(ins):
        at = pl.multiple_of(rows * lax.rem(zi + zn - step, zn), 8)
        out[:, pl.ds(at, rows), :] = ref[...]


def place_kernel(*refs):
    ins, out, sems = refs[:-2], refs[-2], refs[-1]
    zi = lax.axis_index("z")
    zn = lax.axis_size("z")
    core = lax.axis_index(CA)
    copies = []
    for k, ref in enumerate(ins):
        fields, rows = ref.shape[:2]
        if k < 2:
            first, side, step = 0, k, None
            at = rows * (core if side == 0 else 1 - core)
        else:
            first = OUT - fields
            side, step = divmod(k - 2, zn)
            c = core if side == 0 else 1 - core
            at = rows * (zn * c + lax.rem(zi + zn - step, zn))
        at = pl.multiple_of(at, 8)
        copies.append(
            pltpu.make_async_copy(
                ref, out.at[pl.ds(first, fields), pl.ds(at, rows)], sems.at[k]
            )
        )
    copy_all(copies)


def place(pieces, shape):
    return pl.pallas_call(
        place_kernel,
        in_specs=[pl.BlockSpec(memory_space=pltpu.VMEM)] * len(pieces),
        out_specs=pl.BlockSpec(memory_space=pltpu.HBM),
        out_shape=pltpu.HBM(shape, F32),
        scratch_shapes=[pltpu.SemaphoreType.DMA((len(pieces),))],
        compiler_params=pltpu.CompilerParams(vmem_limit_bytes=4 * 2**20),
        name="place",
    )(*pieces)


def small_call(kernel, outs, scratch, name, *args):
    vm = pl.BlockSpec(memory_space=pltpu.VMEM)
    return pl.pallas_call(
        kernel,
        in_specs=[vm] * len(args),
        out_specs=[vm] * len(outs),
        out_shape=[pltpu.VMEM(s, F32) for s in outs],
        scratch_shapes=[pltpu.VMEM(s, F32) for s in scratch],
        compiler_params=pltpu.CompilerParams(vmem_limit_bytes=8 * 2**20),
        cost_estimate=pl.CostEstimate(flops=1000, bytes_accessed=1000, transcendentals=0),
        name=name,
    )(*args)


def send(value, axis, step):
    size = lax.axis_size(axis)
    return lax.ppermute(value, axis, [(i, (i + step) % size) for i in range(size)])


def shards(flow, dy):
    _, lx, lz, ny = flow.shape
    gn = lax.axis_size(GXA)
    zn = lax.axis_size("z")
    up = [(i, i + 1) for i in range(gn - 1)]
    down = [(i + 1, i) for i in range(gn - 1)]
    zs, xs = (3, lx, 4, ny), (4, 4, lz, ny)
    zl, zr, xl, xr = cut(rim_kernel, [zs, zs, xs, xs], 4, "rims", flow)
    with jax.named_scope("rim_exchange"):
        zl = send(zl, ZA, 1)
        zr = send(zr, ZA, -1)
        xl = lax.ppermute(xl, GXA, up)
        xr = lax.ppermute(xr, GXA, down)
    pad, mean, keep1, give1 = base_moments(flow)
    ysl, dmat = y_slopes(pad, dy)
    rows = lx // 2 // zn
    one_piece, two_piece = (FIRST, rows, ny), (STATE - FIRST, rows, ny)

    def along_z(own, up, down, far):
        return [own, send(up, "z", 1), send(far, "z", 2), send(down, "z", -1)]

    def spread(done):
        return [done] + [send(done, "z", k) for k in (1, 2, 3)]

    with jax.named_scope("base_core"):
        got1 = send(give1, CA, 1)
        parts1 = small_call(
            functools.partial(core_base_kernel, lz), [one_piece] * 4, [], "core_base", keep1, got1
        )
    with jax.named_scope("base_span"):
        pieces1 = along_z(*parts1)
    pad, keep2, give2 = inner_moments(pad, ysl, zl, zr, mean, parts1[0])
    with jax.named_scope("base_span"):
        part1, left1, right1 = small_call(
            functools.partial(span_base_kernel, 2 * lz), [one_piece] * 3, [], "span_base", *pieces1
        )
    with jax.named_scope("base_x"):
        other1 = send(part1, "xh", 1)
    keep2, give2 = edge_moments(pad, keep2, give2, ysl, xl, xr, mean, part1)
    with jax.named_scope("slope_core"):
        got2 = send(give2, CA, 1)
        parts2 = small_call(
            functools.partial(core_slope_kernel, lz), [two_piece] * 4, [], "core_slope",
            keep1, got1, keep2, got2, dmat,
        )
    with jax.named_scope("base_x"):
        (done1,) = small_call(
            functools.partial(last_base_kernel, 2 * zn * lz),
            [(FIRST - 1, rows, ny)], [one_piece], "last_base", part1, other1, parts2[0],
        )
    with jax.named_scope("base_spread"):
        spread1 = spread(done1)
    with jax.named_scope("slope_span"):
        pieces2 = along_z(*parts2)
        (part2,) = small_call(
            functools.partial(span_slope_kernel, 2 * lz), [two_piece], [two_piece] * 2,
            "span_slope", *pieces1, *pieces2, left1, right1, dmat,
        )
    with jax.named_scope("slope_x"):
        other2 = send(part2, "xh", 1)
        (done2,) = small_call(
            functools.partial(last_slope_kernel, 2 * zn * lz),
            [(OUT - FIRST + 1, rows, ny)], [two_piece], "last_slope",
            part1, other1, part2, other2, dmat,
        )
    with jax.named_scope("base_spread"):
        (half1,) = small_call(
            gather_kernel, [(FIRST - 1, lx // 2, ny)], [], "gather", done2, *spread1
        )
        all1 = [half1, send(half1, CA, 1)]
    with jax.named_scope("slope_spread"):
        all2 = spread(done2)
        all2 = all2 + [send(v, CA, 1) for v in all2]
    return place(all1 + all2, (OUT, lx, ny))


def solution(mesh):
    gx, gz = mesh.shape["gx"], mesh.shape["gz"]
    fine = Mesh(mesh.devices.reshape(gx, 2, gz // 4, 2), (GXA,) + ZA)
    return jax.shard_map(
        shards,
        mesh=fine,
        in_specs=(P(None, GXA, ZA, None), P()),
        out_specs=P(None, GXA, None),
        check_vma=False,
    )
```

```python
import functools

import jax
import jax.numpy as jnp
from jax import lax
from jax.experimental import pallas as pl
from jax.experimental.pallas import tpu as pltpu
from jax.sharding import Mesh, PartitionSpec as P

F32 = jnp.float32
BF16 = jnp.bfloat16
lead = 4.0 / 5.0
ratios = (1.0, -0.25, 1.0 / 21.0, -1.0 / 224.0)
pairs = ((0, 0), (0, 1), (0, 2), (1, 1), (1, 2), (2, 2))
triples = (
    (0, 0, 0), (0, 0, 1), (0, 0, 2), (0, 1, 1), (0, 1, 2),
    (0, 2, 2), (1, 1, 1), (1, 1, 2), (1, 2, 2), (2, 2, 2),
)
MEAN, UU, UUU, PU, DXM, PG, GG, UG = 0, 4, 10, 20, 23, 27, 33, 39
FIRST = 23
STATE = 44
OUT = 40
NBASE = 19
NSLOPE = 22
GXA, ZA, CA = "gx", ("xh", "z", "c"), "c"


def combine_base(left, right, count, put):
    half = [0.5 * (left(MEAN + c) - right(MEAN + c)) for c in range(4)]
    nh = [float(2 * count) * h for h in half]
    for c in range(4):
        put(MEAN + c, 0.5 * (left(MEAN + c) + right(MEAN + c)))
    gap = {}
    for k, (i, j) in enumerate(pairs):
        a, b = left(UU + k), right(UU + k)
        gap[i, j] = gap[j, i] = a - b
        put(UU + k, (a + b) + nh[i] * half[j])
    for k, (i, j, l) in enumerate(triples):
        fix = half[i] * gap[j, l] + half[j] * gap[i, l] + half[l] * gap[i, j]
        put(UUU + k, (left(UUU + k) + right(UUU + k)) + fix)
    for c in range(3):
        put(PU + c, (left(PU + c) + right(PU + c)) + nh[3] * half[c])


def combine_slopes(left, right, count, dmat, put):
    half = [0.5 * (left(MEAN + c) - right(MEAN + c)) for c in range(4)]
    gx = [0.5 * (left(DXM + c) - right(DXM + c)) for c in range(4)]
    rows = half[0].shape[0]
    turned = jnp.dot(
        jnp.concatenate(half, axis=0), dmat,
        precision=lax.Precision.HIGHEST, preferred_element_type=F32,
    )
    gy = [turned[c * rows : (c + 1) * rows] for c in range(4)]
    both = float(2 * count)
    nh = [both * h for h in half]
    for c in range(4):
        put(DXM + c, 0.5 * (left(DXM + c) + right(DXM + c)))
    fixes = (
        2.0 * nh[3] * gx[0],
        nh[3] * (gy[0] + gx[1]),
        nh[3] * gx[2],
        2.0 * nh[3] * gy[1],
        nh[3] * gy[2],
    )
    for k in range(5):
        put(PG + k, (left(PG + k) + right(PG + k)) + fixes[k])
    put(PG + 5, left(PG + 5) + right(PG + 5))
    for k, (i, j) in enumerate(pairs):
        fix = both * (gx[i] * gx[j] + gy[i] * gy[j])
        put(GG + k, (left(GG + k) + right(GG + k)) + fix)
    fixes = (
        2.0 * nh[0] * gx[3],
        nh[0] * gy[3] + nh[1] * gx[3],
        nh[2] * gx[3],
        2.0 * nh[1] * gy[3],
        nh[2] * gy[3],
    )
    for k in range(5):
        put(UG + k, (left(UG + k) + right(UG + k)) - fixes[k])


def copy_all(copies):
    for c in copies:
        c.start()
    for c in copies:
        c.wait()


def rim_kernel(flow, zl, zr, xl, xr, sems):
    _, lx, lz, _ = flow.shape
    copy_all([
        pltpu.make_async_copy(flow.at[pl.ds(0, 3), :, pl.ds(lz - 4, 4)], zl, sems.at[0]),
        pltpu.make_async_copy(flow.at[pl.ds(0, 3), :, pl.ds(0, 4)], zr, sems.at[1]),
        pltpu.make_async_copy(flow.at[:, pl.ds(lx - 4, 4)], xl, sems.at[2]),
        pltpu.make_async_copy(flow.at[:, pl.ds(0, 4)], xr, sems.at[3]),
    ])


def cut(kernel, shapes, copies, name, flow, *after):
    flow = pltpu.with_memory_space_constraint(flow, pltpu.HBM)
    return pl.pallas_call(
        kernel,
        in_specs=[pl.BlockSpec(memory_space=pltpu.HBM)]
        + [pl.BlockSpec(memory_space=pl.ANY)] * len(after),
        out_specs=[pl.BlockSpec(memory_space=pltpu.VMEM)] * len(shapes),
        out_shape=[pltpu.VMEM(s, F32) for s in shapes],
        scratch_shapes=[pltpu.SemaphoreType.DMA((copies,))],
        compiler_params=pltpu.CompilerParams(vmem_limit_bytes=4 * 2**20),
        name=name,
    )(flow, *after)


def base_kernel(raw, pad, mean, keep, send, acc):
    _, lx, ny = mean.shape
    lz = pad.shape[2] - 16
    half = lx // 2
    core = lax.axis_index(CA)
    def one(x, _):
        centre = []
        for c in range(4):
            m = jnp.sum(raw[c, x], axis=0, keepdims=True) * (1.0 / lz)
            mean[c, pl.ds(x, 1), :] = m
            centre.append(m)
        total = [None] * NBASE

        def add(n, v):
            total[n] = v if total[n] is None else total[n] + v

        for b in range(lz // 8):
            f = [raw[c, x, pl.ds(8 * b, 8), :] - centre[c] for c in range(4)]
            for c in range(4):
                pad[c, x + 4, pl.ds(8 + 8 * b, 8), :] = f[c]
            prod = {}
            for n, (i, j) in enumerate(pairs):
                prod[i, j] = f[i] * f[j]
                add(n, prod[i, j])
            for n, (i, j, l) in enumerate(triples):
                add(6 + n, prod[i, j] * f[l])
            for c in range(3):
                add(16 + c, f[3] * f[c])
        for n in range(NBASE):
            acc[pl.ds(pl.multiple_of(n * 8 * lx + 8 * x, 8), 8), :] = total[n]
        return 0

    lax.fori_loop(0, lx, one, 0, unroll=2)
    for out, side in ((send, 1 - core), (keep, core)):
        at = pl.multiple_of(half * side, 8)
        for c in range(4):
            out[MEAN + c] = mean[c, pl.ds(at, half), :]
        for k in range(NBASE):
            out[UU + k] = half_sum(k, acc, lx, at)


def y_kernel(pad, dy, ysl, dmat, weights):
    _, lx, lz, ny = ysl.shape
    step = 16
    d = dy[...].T * (1.0 / lead)
    dmat[...] = d
    dhi = d.astype(BF16)
    dlo = (d - dhi.astype(F32)).astype(BF16)
    weights[pl.ds(0, ny), pl.ds(0, ny)] = dhi
    weights[pl.ds(0, ny), pl.ds(ny, ny)] = dlo
    weights[pl.ds(ny, ny), pl.ds(0, ny)] = dhi
    weights[pl.ds(ny, ny), pl.ds(ny, ny)] = jnp.zeros_like(dlo)

    def part(k, _):
        left = []
        for r in range(step):
            for c in range(4):
                a = pad[c, step * k + r + 4, pl.ds(8, lz), :]
                hi = a.astype(BF16)
                lo = (a - hi.astype(F32)).astype(BF16)
                left.append(jnp.concatenate([hi, lo], axis=1))
        y = jnp.dot(jnp.concatenate(left, axis=0), weights[...], preferred_element_type=F32)
        y = y[:, :ny] + y[:, ny:]
        for r in range(step):
            for c in range(4):
                at = (4 * r + c) * lz
                ysl[c, step * k + r] = y[at : at + lz]
        return 0

    lax.fori_loop(0, lx // step, part, 0)


def row_sum(k, rows, acc):
    return sum(acc[pl.ds(8 * k * rows + s, rows, stride=8), :] for s in range(8))


def half_sum(k, acc, rows, at):
    where = pl.multiple_of(8 * (k * rows + at), 8)
    return sum(acc[pl.ds(where + s, rows // 2, stride=8), :] for s in range(8))


def base_moments(flow):
    _, lx, lz, ny = flow.shape
    vm = pl.BlockSpec(memory_space=pltpu.VMEM)
    half = (FIRST, lx // 2, ny)
    shapes = [(4, lx + 8, lz + 16, ny), (4, lx, ny), half, half]
    return pl.pallas_call(
        base_kernel,
        in_specs=[vm],
        out_specs=[vm] * 4,
        out_shape=[pltpu.VMEM(s, F32) for s in shapes],
        scratch_shapes=[
            pltpu.VMEM((NBASE * 8 * lx, ny), F32),
        ],
        compiler_params=pltpu.CompilerParams(vmem_limit_bytes=16 * 2**20),
        cost_estimate=pl.CostEstimate(flops=1000, bytes_accessed=1000, transcendentals=0),
        name="base_moments",
    )(pltpu.with_memory_space_constraint(flow, pltpu.VMEM))


def y_slopes(pad, dy):
    ny = dy.shape[0]
    lx, lz = pad.shape[1] - 8, pad.shape[2] - 16
    vm = pl.BlockSpec(memory_space=pltpu.VMEM)
    return pl.pallas_call(
        y_kernel,
        in_specs=[vm, vm],
        out_specs=[vm, vm],
        out_shape=[pltpu.VMEM((4, lx, lz, ny), F32), pltpu.VMEM((ny, ny), F32)],
        scratch_shapes=[pltpu.VMEM((2 * ny, 2 * ny), BF16)],
        compiler_params=pltpu.CompilerParams(vmem_limit_bytes=16 * 2**20),
        cost_estimate=pl.CostEstimate(flops=1000, bytes_accessed=1000, transcendentals=0),
        name="y_slopes",
    )(pad, dy)


def difference(upper, lower):
    out = None
    for k in range(4):
        diff = upper(k) - lower(k)
        out = diff if out is None else out + ratios[k] * diff
    return out


def slope_row(pad, ysl, x):
    lz, ny = ysl.shape[2:]
    total = [None] * NSLOPE
    row = lax.broadcasted_iota(jnp.int32, (8, ny), 0)
    row = jnp.minimum(row, 7 - row)
    weight = jnp.full((8, ny), sum(ratios), F32)
    for k in range(3):
        weight = jnp.where(row == k, sum(ratios[3 - k :]), weight)
    for c in range(3):
        total[c] = weight * (
            pad[c, x + 4, pl.ds(4 + lz, 8), :] - pad[c, x + 4, pl.ds(4, 8), :]
        )

    def add(k, v):
        total[k] = v if total[k] is None else total[k] + v

    for b in range(lz // 8):
        at = 8 + 8 * b
        u = [pad[c, x + 4, pl.ds(at, 8), :] for c in range(4)]
        p = u[3]
        g = [[None] * 3 for _ in range(4)]
        for c in range(4):
            g[c][0] = difference(
                lambda k: pad[c, x + 5 + k, pl.ds(at, 8), :],
                lambda k: pad[c, x + 3 - k, pl.ds(at, 8), :],
            )
            g[c][1] = ysl[c, x, pl.ds(8 * b, 8), :]
        for c in range(3):
            g[c][2] = difference(
                lambda k: pad[c, x + 4, pl.ds(at + 1 + k, 8), :],
                lambda k: pad[c, x + 4, pl.ds(at - 1 - k, 8), :],
            )
        add(3, p * g[0][0])
        add(4, p * (g[0][1] + g[1][0]))
        add(5, p * g[0][2])
        add(6, p * g[2][0])
        add(7, p * g[1][1])
        add(8, p * g[1][2])
        add(9, p * g[2][1])
        add(10, p * g[2][2])
        for k, (i, j) in enumerate(pairs):
            for dim in range(3):
                add(11 + k, g[i][dim] * g[j][dim])
        add(17, u[0] * g[3][0])
        add(18, u[0] * g[3][1] + u[1] * g[3][0])
        add(19, u[1] * g[3][1])
        add(20, u[2] * g[3][0])
        add(21, u[2] * g[3][1])
    return total


def slope_fields(total, pressure):
    s02, s12, s22 = (total(n) + pressure * total(c) for c, n in enumerate((5, 8, 10)))
    yield PG + 0, 2.0 * total(3)
    yield PG + 1, total(4)
    yield PG + 2, s02 + total(6)
    yield PG + 3, 2.0 * total(7)
    yield PG + 4, s12 + total(9)
    yield PG + 5, 2.0 * s22
    for k in range(6):
        yield GG + k, total(11 + k)
    yield UG + 0, -2.0 * total(17)
    yield UG + 1, -total(18)
    yield UG + 2, s02 - total(20)
    yield UG + 3, -2.0 * total(19)
    yield UG + 4, s12 - total(21)


def inner_kernel(pad_in, ysl, zl, zr, mean, after, pad, keep, send, acc):
    _, lx, lz, ny = ysl.shape
    half = lx // 2
    core = lax.axis_index(CA)

    def rim(x, _):
        for c in range(3):
            m = mean[c, pl.ds(x, 1), :]
            pad[c, x + 4, pl.ds(4, 4), :] = zl[c, x] - m
            pad[c, x + 4, pl.ds(8 + lz, 4), :] = zr[c, x] - m
        return 0

    lax.fori_loop(0, lx, rim, 0, unroll=4)

    def one(x, _):
        total = slope_row(pad, ysl, x)
        for k in range(NSLOPE):
            acc[pl.ds(pl.multiple_of(k * 8 * lx + 8 * x, 8), 8), :] = total[k]
        return 0

    lax.fori_loop(4, lx - 4, one, 0, unroll=4)

    for out, side in ((send, 1 - core), (keep, core)):
        at = pl.multiple_of(half * side, 8)

        fields = slope_fields(
            lambda k, at=at: half_sum(k, acc, lx, at), mean[3, pl.ds(at, half), :]
        )
        for f, v in fields:
            out[f - FIRST] = v


def inner_moments(pad, ysl, zl, zr, mean, after):
    _, lx, lz, ny = ysl.shape
    vm = pl.BlockSpec(memory_space=pltpu.VMEM)
    shape = pltpu.VMEM((STATE - FIRST, lx // 2, ny), F32)
    return pl.pallas_call(
        inner_kernel,
        in_specs=[vm] * 5 + [pl.BlockSpec(memory_space=pl.ANY)],
        out_specs=[vm] * 3,
        out_shape=[pltpu.VMEM(pad.shape, F32), shape, shape],
        input_output_aliases={0: 0},
        scratch_shapes=[pltpu.VMEM((NSLOPE * 8 * lx, ny), F32)],
        compiler_params=pltpu.CompilerParams(vmem_limit_bytes=16 * 2**20),
        cost_estimate=pl.CostEstimate(
            flops=1500000000, bytes_accessed=84_000_000, transcendentals=0
        ),
        name="inner_moments",
    )(pad, ysl, zl, zr, mean, after)


def edge_kernel(
    pad_in, keep_in, send_in, ysl, xl, xr, mean, after, pad, keep, send, acc, mpad, dxm
):
    _, lx, lz, ny = ysl.shape
    half = lx // 2
    core = lax.axis_index(CA)
    gi = lax.axis_index(GXA)
    at_ends = (gi == 0, gi == lax.axis_size(GXA) - 1)

    for c in range(4):
        mpad[c, pl.ds(8, lx), :] = mean[c]
        for j in range(4):
            for halo, at_end, src, dst in (
                (xl, at_ends[0], 3 - j, j), (xr, at_ends[1], lx - 1 - j, lx + 4 + j)
            ):
                own = pad[c, src + 4, pl.ds(8, lz), :]
                m = jnp.sum(halo[c, j], axis=0, keepdims=True) * (1.0 / lz)
                pad[c, dst, pl.ds(8, lz), :] = jnp.where(at_end, own, halo[c, j] - m)
                mpad[c, pl.ds(dst + 4, 1), :] = jnp.where(at_end, mean[c, pl.ds(src, 1), :], m)
        dxm[c] = difference(
            lambda k: mpad[c, pl.ds(9 + k, lx), :], lambda k: mpad[c, pl.ds(7 - k, lx), :]
        )

    for out, side in ((send, 1 - core), (keep, core)):
        for c in range(4):
            out[DXM - FIRST + c] = dxm[c, pl.ds(pl.multiple_of(half * side, 8), half), :]

    def one(i, _):
        x = jnp.where(i < 4, i, lx - 8 + i)
        total = slope_row(pad, ysl, x)
        for k in range(NSLOPE):
            acc[pl.ds(pl.multiple_of(k * 64 + 8 * i, 8), 8), :] = total[k]
        return 0

    lax.fori_loop(0, 8, one, 0, unroll=4)

    pressure = jnp.concatenate([mean[3, pl.ds(0, 4), :], mean[3, pl.ds(lx - 4, 4), :]], axis=0)
    fields = list(slope_fields(lambda k: row_sum(k, 8, acc), pressure))
    for side, rows in ((0, slice(0, 4)), (1, slice(4, 8))):
        at = 0 if side == 0 else half - 4

        @pl.when(core == side)
        def _():
            for f, v in fields:
                keep[f - FIRST, pl.ds(at, 4), :] = v[rows]

        @pl.when(core != side)
        def _():
            for f, v in fields:
                send[f - FIRST, pl.ds(at, 4), :] = v[rows]


def edge_moments(pad, keep, send, ysl, xl, xr, mean, after):
    _, lx, lz, ny = ysl.shape
    vm = pl.BlockSpec(memory_space=pltpu.VMEM)
    out = pl.pallas_call(
        edge_kernel,
        in_specs=[vm] * 7 + [pl.BlockSpec(memory_space=pl.ANY)],
        out_specs=[vm] * 3,
        out_shape=[pltpu.VMEM(v.shape, F32) for v in (pad, keep, send)],
        input_output_aliases={0: 0, 1: 1, 2: 2},
        scratch_shapes=[
            pltpu.VMEM((NSLOPE * 64, ny), F32),
            pltpu.VMEM((4, lx + 16, ny), F32),
            pltpu.VMEM((4, lx, ny), F32),
        ],
        compiler_params=pltpu.CompilerParams(vmem_limit_bytes=16 * 2**20),
        cost_estimate=pl.CostEstimate(
            flops=25 * ysl.size, bytes_accessed=ysl.size // 2, transcendentals=0
        ),
        name="edge_moments",
    )(pad, keep, send, ysl, xl, xr, mean, after)
    return out[1:]


def picker(one, two=None):
    return lambda f: one[f] if f < FIRST else two[f - FIRST]


def storer(one, two=None):
    def put(f, v):
        if f < FIRST:
            one[f] = v
        else:
            two[f - FIRST] = v
    return put


def z_places(rows):
    zi = lax.axis_index("z")
    zn = lax.axis_size("z")
    return [pl.multiple_of(rows * lax.rem(zi + k, zn), 8) for k in (0, 1, zn - 1, 2)]


def core_base_kernel(count, keep, got, *outs):
    rows = outs[0].shape[1]
    for out, at in zip(outs, z_places(rows)):
        combine_base(
            lambda f, at=at: keep[f, pl.ds(at, rows), :],
            lambda f, at=at: got[f, pl.ds(at, rows), :],
            count, storer(out),
        )


def core_slope_kernel(count, keep1, got1, keep2, got2, dmat, *outs):
    rows = outs[0].shape[1]
    places = z_places(rows)

    def pick(one, two):
        def field(f):
            ref, k = (one, f) if f < FIRST else (two, f - FIRST)
            return jnp.concatenate([ref[k, pl.ds(at, rows), :] for at in places], axis=0)
        return field

    def put(f, v):
        for n, ref in enumerate(outs):
            ref[f - FIRST] = v[rows * n : rows * (n + 1)]

    combine_slopes(pick(keep1, keep2), pick(got1, got2), count, dmat[...], put)


def span_base_kernel(count, own, one, two, three, out, left, right):
    combine_base(picker(own), picker(one), count, storer(left))
    combine_base(picker(two), picker(three), count, storer(right))
    combine_base(picker(left), picker(right), 2 * count, storer(out))


def span_slope_kernel(count, *refs):
    base, (own, one, two, three) = refs[:4], refs[4:8]
    left1, right1, dmat, out, left, right = refs[8:]
    d = dmat[...]
    combine_slopes(picker(base[0], own), picker(base[1], one), count, d, storer(None, left))
    combine_slopes(picker(base[2], two), picker(base[3], three), count, d, storer(None, right))
    combine_slopes(
        picker(left1, left), picker(right1, right), 2 * count, d, storer(None, out)
    )


def last_base_kernel(count, mine, other, after, out, state):
    combine_base(picker(mine), picker(other), count, storer(state))
    scale = 1.0 / (2 * count)
    for c in range(3):
        out[c] = state[MEAN + c]
    for k in range(NBASE):
        out[3 + k] = state[UU + k] * scale


def last_slope_kernel(count, mine1, other1, mine2, other2, dmat, out, state):
    combine_slopes(
        picker(mine1, mine2), picker(other1, other2), count, dmat[...], storer(None, state)
    )
    scale = 1.0 / (2 * count)
    for k in range(6):
        out[k] = state[PG - FIRST + k] * (scale * lead)
        out[6 + k] = state[GG - FIRST + k] * (scale * lead * lead)
    for k in range(5):
        out[12 + k] = state[UG - FIRST + k] * (scale * lead)
    out[17] = state[PG - FIRST + 5] * (scale * lead)


def gather_kernel(after, *refs):
    ins, out = refs[:-1], refs[-1]
    rows = ins[0].shape[1]
    zi = lax.axis_index("z")
    zn = lax.axis_size("z")
    for step, ref in enumerate(ins):
        at = pl.multiple_of(rows * lax.rem(zi + zn - step, zn), 8)
        out[:, pl.ds(at, rows), :] = ref[...]


def place_kernel(*refs):
    ins, out, sems = refs[:-2], refs[-2], refs[-1]
    zi = lax.axis_index("z")
    zn = lax.axis_size("z")
    core = lax.axis_index(CA)
    copies = []
    for k, ref in enumerate(ins):
        fields, rows = ref.shape[:2]
        if k < 2:
            first, side, step = 0, k, None
            at = rows * (core if side == 0 else 1 - core)
        else:
            first = OUT - fields
            side, step = divmod(k - 2, zn)
            c = core if side == 0 else 1 - core
            at = rows * (zn * c + lax.rem(zi + zn - step, zn))
        at = pl.multiple_of(at, 8)
        copies.append(
            pltpu.make_async_copy(
                ref, out.at[pl.ds(first, fields), pl.ds(at, rows)], sems.at[k]
            )
        )
    copy_all(copies)


def place(pieces, shape):
    return pl.pallas_call(
        place_kernel,
        in_specs=[pl.BlockSpec(memory_space=pltpu.VMEM)] * len(pieces),
        out_specs=pl.BlockSpec(memory_space=pltpu.HBM),
        out_shape=pltpu.HBM(shape, F32),
        scratch_shapes=[pltpu.SemaphoreType.DMA((len(pieces),))],
        compiler_params=pltpu.CompilerParams(vmem_limit_bytes=4 * 2**20),
        name="place",
    )(*pieces)


def small_call(kernel, outs, scratch, name, *args):
    vm = pl.BlockSpec(memory_space=pltpu.VMEM)
    return pl.pallas_call(
        kernel,
        in_specs=[vm] * len(args),
        out_specs=[vm] * len(outs),
        out_shape=[pltpu.VMEM(s, F32) for s in outs],
        scratch_shapes=[pltpu.VMEM(s, F32) for s in scratch],
        compiler_params=pltpu.CompilerParams(vmem_limit_bytes=8 * 2**20),
        cost_estimate=pl.CostEstimate(flops=1000, bytes_accessed=1000, transcendentals=0),
        name=name,
    )(*args)


def send(value, axis, step):
    size = lax.axis_size(axis)
    return lax.ppermute(value, axis, [(i, (i + step) % size) for i in range(size)])


def shards(flow, dy):
    _, lx, lz, ny = flow.shape
    gn = lax.axis_size(GXA)
    zn = lax.axis_size("z")
    up = [(i, i + 1) for i in range(gn - 1)]
    down = [(i + 1, i) for i in range(gn - 1)]
    zs, xs = (3, lx, 4, ny), (4, 4, lz, ny)
    zl, zr, xl, xr = cut(rim_kernel, [zs, zs, xs, xs], 4, "rims", flow)
    with jax.named_scope("rim_exchange"):
        zl = send(zl, ZA, 1)
        zr = send(zr, ZA, -1)
        xl = lax.ppermute(xl, GXA, up)
        xr = lax.ppermute(xr, GXA, down)
    pad, mean, keep1, give1 = base_moments(flow)
    ysl, dmat = y_slopes(pad, dy)
    rows = lx // 2 // zn
    one_piece, two_piece = (FIRST, rows, ny), (STATE - FIRST, rows, ny)

    def along_z(own, up, down, far):
        return [own, send(up, "z", 1), send(far, "z", 2), send(down, "z", -1)]

    def spread(done):
        return [done] + [send(done, "z", k) for k in (1, 2, 3)]

    with jax.named_scope("base_core"):
        got1 = send(give1, CA, 1)
        parts1 = small_call(
            functools.partial(core_base_kernel, lz), [one_piece] * 4, [], "core_base", keep1, got1
        )
    with jax.named_scope("base_span"):
        pieces1 = along_z(*parts1)
    pad, keep2, give2 = inner_moments(pad, ysl, zl, zr, mean, parts1[0])
    with jax.named_scope("base_span"):
        part1, left1, right1 = small_call(
            functools.partial(span_base_kernel, 2 * lz), [one_piece] * 3, [], "span_base", *pieces1
        )
    with jax.named_scope("base_x"):
        other1 = send(part1, "xh", 1)
    keep2, give2 = edge_moments(pad, keep2, give2, ysl, xl, xr, mean, part1)
    with jax.named_scope("slope_core"):
        got2 = send(give2, CA, 1)
        parts2 = small_call(
            functools.partial(core_slope_kernel, lz), [two_piece] * 4, [], "core_slope",
            keep1, got1, keep2, got2, dmat,
        )
    with jax.named_scope("base_x"):
        (done1,) = small_call(
            functools.partial(last_base_kernel, 2 * zn * lz),
            [(FIRST - 1, rows, ny)], [one_piece], "last_base", part1, other1, parts2[0],
        )
    with jax.named_scope("base_spread"):
        spread1 = spread(done1)
    with jax.named_scope("slope_span"):
        pieces2 = along_z(*parts2)
        (part2,) = small_call(
            functools.partial(span_slope_kernel, 2 * lz), [two_piece], [two_piece] * 2,
            "span_slope", *pieces1, *pieces2, left1, right1, dmat,
        )
    with jax.named_scope("slope_x"):
        other2 = send(part2, "xh", 1)
        (done2,) = small_call(
            functools.partial(last_slope_kernel, 2 * zn * lz),
            [(OUT - FIRST + 1, rows, ny)], [two_piece], "last_slope",
            part1, other1, part2, other2, dmat,
        )
    with jax.named_scope("base_spread"):
        (half1,) = small_call(
            gather_kernel, [(FIRST - 1, lx // 2, ny)], [], "gather", done2, *spread1
        )
        all1 = [half1, send(half1, CA, 1)]
    with jax.named_scope("slope_spread"):
        all2 = spread(done2)
        all2 = all2 + [send(v, CA, 1) for v in all2]
    return place(all1 + all2, (OUT, lx, ny))


def solution(mesh):
    gx, gz = mesh.shape["gx"], mesh.shape["gz"]
    fine = Mesh(mesh.devices.reshape(gx, 2, gz // 4, 2), (GXA,) + ZA)
    return jax.shard_map(
        shards,
        mesh=fine,
        in_specs=(P(None, GXA, ZA, None), P()),
        out_specs=P(None, GXA, None),
        check_vma=False,
    )
```

```python
import functools

import jax
import jax.numpy as jnp
from jax import lax
from jax.experimental import pallas as pl
from jax.experimental.pallas import tpu as pltpu
from jax.sharding import Mesh, PartitionSpec as P

F32 = jnp.float32
BF16 = jnp.bfloat16
lead = 4.0 / 5.0
ratios = (1.0, -0.25, 1.0 / 21.0, -1.0 / 224.0)
pairs = ((0, 0), (0, 1), (0, 2), (1, 1), (1, 2), (2, 2))
triples = (
    (0, 0, 0), (0, 0, 1), (0, 0, 2), (0, 1, 1), (0, 1, 2),
    (0, 2, 2), (1, 1, 1), (1, 1, 2), (1, 2, 2), (2, 2, 2),
)
MEAN, UU, UUU, PU, DXM, PG, GG, UG = 0, 4, 10, 20, 23, 27, 33, 39
FIRST = 23
STATE = 44
OUT = 40
NBASE = 19
NSLOPE = 22
GXA, ZA, CA = "gx", ("xh", "z", "c"), "c"


def combine_base(left, right, count, put):
    half = [0.5 * (left(MEAN + c) - right(MEAN + c)) for c in range(4)]
    nh = [float(2 * count) * h for h in half]
    for c in range(4):
        put(MEAN + c, 0.5 * (left(MEAN + c) + right(MEAN + c)))
    gap = {}
    for k, (i, j) in enumerate(pairs):
        a, b = left(UU + k), right(UU + k)
        gap[i, j] = gap[j, i] = a - b
        put(UU + k, (a + b) + nh[i] * half[j])
    for k, (i, j, l) in enumerate(triples):
        fix = half[i] * gap[j, l] + half[j] * gap[i, l] + half[l] * gap[i, j]
        put(UUU + k, (left(UUU + k) + right(UUU + k)) + fix)
    for c in range(3):
        put(PU + c, (left(PU + c) + right(PU + c)) + nh[3] * half[c])


def combine_slopes(left, right, count, dmat, put):
    half = [0.5 * (left(MEAN + c) - right(MEAN + c)) for c in range(4)]
    gx = [0.5 * (left(DXM + c) - right(DXM + c)) for c in range(4)]
    rows = half[0].shape[0]
    turned = jnp.dot(
        jnp.concatenate(half, axis=0), dmat,
        precision=lax.Precision.HIGHEST, preferred_element_type=F32,
    )
    gy = [turned[c * rows : (c + 1) * rows] for c in range(4)]
    both = float(2 * count)
    nh = [both * h for h in half]
    for c in range(4):
        put(DXM + c, 0.5 * (left(DXM + c) + right(DXM + c)))
    fixes = (
        2.0 * nh[3] * gx[0],
        nh[3] * (gy[0] + gx[1]),
        nh[3] * gx[2],
        2.0 * nh[3] * gy[1],
        nh[3] * gy[2],
    )
    for k in range(5):
        put(PG + k, (left(PG + k) + right(PG + k)) + fixes[k])
    put(PG + 5, left(PG + 5) + right(PG + 5))
    for k, (i, j) in enumerate(pairs):
        fix = both * (gx[i] * gx[j] + gy[i] * gy[j])
        put(GG + k, (left(GG + k) + right(GG + k)) + fix)
    fixes = (
        2.0 * nh[0] * gx[3],
        nh[0] * gy[3] + nh[1] * gx[3],
        nh[2] * gx[3],
        2.0 * nh[1] * gy[3],
        nh[2] * gy[3],
    )
    for k in range(5):
        put(UG + k, (left(UG + k) + right(UG + k)) - fixes[k])


def copy_all(copies):
    for c in copies:
        c.start()
    for c in copies:
        c.wait()


def rim_kernel(flow, zl, zr, xl, xr, sems):
    _, lx, lz, _ = flow.shape
    copy_all([
        pltpu.make_async_copy(flow.at[pl.ds(0, 3), :, pl.ds(lz - 4, 4)], zl, sems.at[0]),
        pltpu.make_async_copy(flow.at[pl.ds(0, 3), :, pl.ds(0, 4)], zr, sems.at[1]),
        pltpu.make_async_copy(flow.at[:, pl.ds(lx - 4, 4)], xl, sems.at[2]),
        pltpu.make_async_copy(flow.at[:, pl.ds(0, 4)], xr, sems.at[3]),
    ])


def cut(kernel, shapes, copies, name, flow, *after):
    flow = pltpu.with_memory_space_constraint(flow, pltpu.HBM)
    return pl.pallas_call(
        kernel,
        in_specs=[pl.BlockSpec(memory_space=pltpu.HBM)]
        + [pl.BlockSpec(memory_space=pl.ANY)] * len(after),
        out_specs=[pl.BlockSpec(memory_space=pltpu.VMEM)] * len(shapes),
        out_shape=[pltpu.VMEM(s, F32) for s in shapes],
        scratch_shapes=[pltpu.SemaphoreType.DMA((copies,))],
        compiler_params=pltpu.CompilerParams(vmem_limit_bytes=4 * 2**20),
        name=name,
    )(flow, *after)


def base_kernel(raw, pad, mean, keep, send, acc):
    _, lx, ny = mean.shape
    lz = pad.shape[2] - 16
    half = lx // 2
    core = lax.axis_index(CA)
    def one(x, _):
        centre = []
        for c in range(4):
            m = jnp.sum(raw[c, x], axis=0, keepdims=True) * (1.0 / lz)
            mean[c, pl.ds(x, 1), :] = m
            centre.append(m)
        total = [None] * NBASE

        def add(n, v):
            total[n] = v if total[n] is None else total[n] + v

        for b in range(lz // 8):
            f = [raw[c, x, pl.ds(8 * b, 8), :] - centre[c] for c in range(4)]
            for c in range(4):
                pad[c, x + 4, pl.ds(8 + 8 * b, 8), :] = f[c]
            prod = {}
            for n, (i, j) in enumerate(pairs):
                prod[i, j] = f[i] * f[j]
                add(n, prod[i, j])
            for n, (i, j, l) in enumerate(triples):
                add(6 + n, prod[i, j] * f[l])
            for c in range(3):
                add(16 + c, f[3] * f[c])
        for n in range(NBASE):
            acc[pl.ds(pl.multiple_of(n * 8 * lx + 8 * x, 8), 8), :] = total[n]
        return 0

    lax.fori_loop(0, lx, one, 0, unroll=2)
    for out, side in ((send, 1 - core), (keep, core)):
        at = pl.multiple_of(half * side, 8)
        for c in range(4):
            out[MEAN + c] = mean[c, pl.ds(at, half), :]
        for k in range(NBASE):
            out[UU + k] = half_sum(k, acc, lx, at)


def y_kernel(pad, dy, ysl, dmat, weights):
    _, lx, lz, ny = ysl.shape
    step = 16
    d = dy[...].T * (1.0 / lead)
    dmat[...] = d
    dhi = d.astype(BF16)
    dlo = (d - dhi.astype(F32)).astype(BF16)
    weights[pl.ds(0, ny), pl.ds(0, ny)] = dhi
    weights[pl.ds(0, ny), pl.ds(ny, ny)] = dlo
    weights[pl.ds(ny, ny), pl.ds(0, ny)] = dhi
    weights[pl.ds(ny, ny), pl.ds(ny, ny)] = jnp.zeros_like(dlo)

    def part(k, _):
        left = []
        for r in range(step):
            for c in range(4):
                a = pad[c, step * k + r + 4, pl.ds(8, lz), :]
                hi = a.astype(BF16)
                lo = (a - hi.astype(F32)).astype(BF16)
                left.append(jnp.concatenate([hi, lo], axis=1))
        y = jnp.dot(jnp.concatenate(left, axis=0), weights[...], preferred_element_type=F32)
        y = y[:, :ny] + y[:, ny:]
        for r in range(step):
            for c in range(4):
                at = (4 * r + c) * lz
                ysl[c, step * k + r] = y[at : at + lz]
        return 0

    lax.fori_loop(0, lx // step, part, 0)


def row_sum(k, rows, acc):
    return sum(acc[pl.ds(8 * k * rows + s, rows, stride=8), :] for s in range(8))


def half_sum(k, acc, rows, at):
    where = pl.multiple_of(8 * (k * rows + at), 8)
    return sum(acc[pl.ds(where + s, rows // 2, stride=8), :] for s in range(8))


def base_moments(flow):
    _, lx, lz, ny = flow.shape
    vm = pl.BlockSpec(memory_space=pltpu.VMEM)
    half = (FIRST, lx // 2, ny)
    shapes = [(4, lx + 8, lz + 16, ny), (4, lx, ny), half, half]
    return pl.pallas_call(
        base_kernel,
        in_specs=[vm],
        out_specs=[vm] * 4,
        out_shape=[pltpu.VMEM(s, F32) for s in shapes],
        scratch_shapes=[
            pltpu.VMEM((NBASE * 8 * lx, ny), F32),
        ],
        compiler_params=pltpu.CompilerParams(vmem_limit_bytes=16 * 2**20),
        cost_estimate=pl.CostEstimate(flops=1000, bytes_accessed=1000, transcendentals=0),
        name="base_moments",
    )(pltpu.with_memory_space_constraint(flow, pltpu.VMEM))


def y_slopes(pad, dy):
    ny = dy.shape[0]
    lx, lz = pad.shape[1] - 8, pad.shape[2] - 16
    vm = pl.BlockSpec(memory_space=pltpu.VMEM)
    return pl.pallas_call(
        y_kernel,
        in_specs=[vm, vm],
        out_specs=[vm, vm],
        out_shape=[pltpu.VMEM((4, lx, lz, ny), F32), pltpu.VMEM((ny, ny), F32)],
        scratch_shapes=[pltpu.VMEM((2 * ny, 2 * ny), BF16)],
        compiler_params=pltpu.CompilerParams(vmem_limit_bytes=16 * 2**20),
        cost_estimate=pl.CostEstimate(flops=1000, bytes_accessed=1000, transcendentals=0),
        name="y_slopes",
    )(pad, dy)


def difference(upper, lower):
    out = None
    for k in range(4):
        diff = upper(k) - lower(k)
        out = diff if out is None else out + ratios[k] * diff
    return out


def slope_row(pad, ysl, x, with_x=True, rest=True):
    lz, ny = ysl.shape[2:]
    total = [None] * NSLOPE

    def add(k, v):
        total[k] = v if total[k] is None else total[k] + v

    if rest:
        row = lax.broadcasted_iota(jnp.int32, (8, ny), 0)
        row = jnp.minimum(row, 7 - row)
        weight = jnp.full((8, ny), sum(ratios), F32)
        for k in range(3):
            weight = jnp.where(row == k, sum(ratios[3 - k :]), weight)
        for c in range(3):
            total[c] = weight * (
                pad[c, x + 4, pl.ds(4 + lz, 8), :] - pad[c, x + 4, pl.ds(4, 8), :]
            )
    for b in range(lz // 8):
        at = 8 + 8 * b
        u = [pad[c, x + 4, pl.ds(at, 8), :] for c in range(4)]
        p = u[3]
        g = [[None] * 3 for _ in range(4)]
        if with_x:
            for c in range(4):
                g[c][0] = difference(
                    lambda k: pad[c, x + 5 + k, pl.ds(at, 8), :],
                    lambda k: pad[c, x + 3 - k, pl.ds(at, 8), :],
                )
        if rest:
            for c in range(4):
                g[c][1] = ysl[c, x, pl.ds(8 * b, 8), :]
            for c in range(3):
                g[c][2] = difference(
                    lambda k: pad[c, x + 4, pl.ds(at + 1 + k, 8), :],
                    lambda k: pad[c, x + 4, pl.ds(at - 1 - k, 8), :],
                )
        if with_x:
            add(3, p * g[0][0])
            add(6, p * g[2][0])
            add(17, u[0] * g[3][0])
            add(20, u[2] * g[3][0])
        if with_x and rest:
            add(4, p * (g[0][1] + g[1][0]))
            add(18, u[0] * g[3][1] + u[1] * g[3][0])
        elif with_x:
            add(4, p * g[1][0])
            add(18, u[1] * g[3][0])
        else:
            add(4, p * g[0][1])
            add(18, u[0] * g[3][1])
        if rest:
            add(5, p * g[0][2])
            add(7, p * g[1][1])
            add(8, p * g[1][2])
            add(9, p * g[2][1])
            add(10, p * g[2][2])
            add(19, u[1] * g[3][1])
            add(21, u[2] * g[3][1])
        dims = ((0,) if with_x else ()) + ((1, 2) if rest else ())
        for k, (i, j) in enumerate(pairs):
            for dim in dims:
                add(11 + k, g[i][dim] * g[j][dim])
    return total


def end_row(i, lx):
    return jnp.where(i < 4, i, lx - 8 + i)


def slope_fields(total, pressure):
    s02, s12, s22 = (total(n) + pressure * total(c) for c, n in enumerate((5, 8, 10)))
    yield PG + 0, 2.0 * total(3)
    yield PG + 1, total(4)
    yield PG + 2, s02 + total(6)
    yield PG + 3, 2.0 * total(7)
    yield PG + 4, s12 + total(9)
    yield PG + 5, 2.0 * s22
    for k in range(6):
        yield GG + k, total(11 + k)
    yield UG + 0, -2.0 * total(17)
    yield UG + 1, -total(18)
    yield UG + 2, s02 - total(20)
    yield UG + 3, -2.0 * total(19)
    yield UG + 4, s12 - total(21)


def inner_kernel(pad_in, ysl, zl, zr, mean, after, pad, keep, send, acc):
    _, lx, lz, ny = ysl.shape
    half = lx // 2
    core = lax.axis_index(CA)

    def rim(x, _):
        for c in range(3):
            m = mean[c, pl.ds(x, 1), :]
            pad[c, x + 4, pl.ds(4, 4), :] = zl[c, x] - m
            pad[c, x + 4, pl.ds(8 + lz, 4), :] = zr[c, x] - m
        return 0

    lax.fori_loop(0, lx, rim, 0, unroll=4)

    def one(x, _):
        total = slope_row(pad, ysl, x)
        for k in range(NSLOPE):
            acc[pl.ds(pl.multiple_of(k * 8 * lx + 8 * x, 8), 8), :] = total[k]
        return 0

    lax.fori_loop(4, lx - 4, one, 0, unroll=4)

    def end(i, _):
        x = end_row(i, lx)
        total = slope_row(pad, ysl, x, with_x=False)
        for k in range(NSLOPE):
            v = jnp.zeros((8, ny), F32) if total[k] is None else total[k]
            acc[pl.ds(pl.multiple_of(k * 8 * lx + 8 * x, 8), 8), :] = v
        return 0

    lax.fori_loop(0, 8, end, 0, unroll=4)

    for out, side in ((send, 1 - core), (keep, core)):
        at = pl.multiple_of(half * side, 8)

        fields = slope_fields(
            lambda k, at=at: half_sum(k, acc, lx, at), mean[3, pl.ds(at, half), :]
        )
        for f, v in fields:
            out[f - FIRST] = v


def inner_moments(pad, ysl, zl, zr, mean, after):
    _, lx, lz, ny = ysl.shape
    vm = pl.BlockSpec(memory_space=pltpu.VMEM)
    shape = pltpu.VMEM((STATE - FIRST, lx // 2, ny), F32)
    return pl.pallas_call(
        inner_kernel,
        in_specs=[vm] * 5 + [pl.BlockSpec(memory_space=pl.ANY)],
        out_specs=[vm] * 3,
        out_shape=[pltpu.VMEM(pad.shape, F32), shape, shape],
        input_output_aliases={0: 0},
        scratch_shapes=[pltpu.VMEM((NSLOPE * 8 * lx, ny), F32)],
        compiler_params=pltpu.CompilerParams(vmem_limit_bytes=16 * 2**20),
        cost_estimate=pl.CostEstimate(
            flops=1500000000, bytes_accessed=84_000_000, transcendentals=0
        ),
        name="inner_moments",
    )(pad, ysl, zl, zr, mean, after)


def edge_kernel(
    pad_in, keep_in, send_in, ysl, xl, xr, mean, after, pad, keep, send, acc, mpad, dxm
):
    _, lx, lz, ny = ysl.shape
    half = lx // 2
    core = lax.axis_index(CA)
    gi = lax.axis_index(GXA)
    at_ends = (gi == 0, gi == lax.axis_size(GXA) - 1)

    for c in range(4):
        mpad[c, pl.ds(8, lx), :] = mean[c]
        for j in range(4):
            for halo, at_end, src, dst in (
                (xl, at_ends[0], 3 - j, j), (xr, at_ends[1], lx - 1 - j, lx + 4 + j)
            ):
                own = pad[c, src + 4, pl.ds(8, lz), :]
                m = jnp.sum(halo[c, j], axis=0, keepdims=True) * (1.0 / lz)
                pad[c, dst, pl.ds(8, lz), :] = jnp.where(at_end, own, halo[c, j] - m)
                mpad[c, pl.ds(dst + 4, 1), :] = jnp.where(at_end, mean[c, pl.ds(src, 1), :], m)
        dxm[c] = difference(
            lambda k: mpad[c, pl.ds(9 + k, lx), :], lambda k: mpad[c, pl.ds(7 - k, lx), :]
        )

    for out, side in ((send, 1 - core), (keep, core)):
        for c in range(4):
            out[DXM - FIRST + c] = dxm[c, pl.ds(pl.multiple_of(half * side, 8), half), :]

    def one(i, _):
        total = slope_row(pad, ysl, end_row(i, lx), rest=False)
        for k in used:
            acc[pl.ds(pl.multiple_of(k * 64 + 8 * i, 8), 8), :] = total[k]
        return 0

    used = (3, 4, 6, 11, 12, 13, 14, 15, 16, 17, 18, 20)
    lax.fori_loop(0, 8, one, 0, unroll=4)

    def total(k):
        return row_sum(k, 8, acc)

    fields = [(PG + 0, 2.0 * total(3)), (PG + 1, total(4)), (PG + 2, total(6))]
    fields += [(GG + k, total(11 + k)) for k in range(6)]
    fields += [(UG + 0, -2.0 * total(17)), (UG + 1, -total(18)), (UG + 2, -total(20))]
    for side, rows in ((0, slice(0, 4)), (1, slice(4, 8))):
        at = pl.ds(0 if side == 0 else half - 4, 4)

        @pl.when(core == side)
        def _():
            for f, v in fields:
                keep[f - FIRST, at, :] = keep[f - FIRST, at, :] + v[rows]

        @pl.when(core != side)
        def _():
            for f, v in fields:
                send[f - FIRST, at, :] = send[f - FIRST, at, :] + v[rows]


def edge_moments(pad, keep, send, ysl, xl, xr, mean, after):
    _, lx, lz, ny = ysl.shape
    vm = pl.BlockSpec(memory_space=pltpu.VMEM)
    out = pl.pallas_call(
        edge_kernel,
        in_specs=[vm] * 7 + [pl.BlockSpec(memory_space=pl.ANY)],
        out_specs=[vm] * 3,
        out_shape=[pltpu.VMEM(v.shape, F32) for v in (pad, keep, send)],
        input_output_aliases={0: 0, 1: 1, 2: 2},
        scratch_shapes=[
            pltpu.VMEM((NSLOPE * 64, ny), F32),
            pltpu.VMEM((4, lx + 16, ny), F32),
            pltpu.VMEM((4, lx, ny), F32),
        ],
        compiler_params=pltpu.CompilerParams(vmem_limit_bytes=16 * 2**20),
        cost_estimate=pl.CostEstimate(
            flops=25 * ysl.size, bytes_accessed=ysl.size // 2, transcendentals=0
        ),
        name="edge_moments",
    )(pad, keep, send, ysl, xl, xr, mean, after)
    return out[1:]


def picker(one, two=None):
    return lambda f: one[f] if f < FIRST else two[f - FIRST]


def storer(one, two=None):
    def put(f, v):
        if f < FIRST:
            one[f] = v
        else:
            two[f - FIRST] = v
    return put


def z_places(rows):
    zi = lax.axis_index("z")
    zn = lax.axis_size("z")
    return [pl.multiple_of(rows * lax.rem(zi + k, zn), 8) for k in (0, 1, zn - 1, 2)]


def core_base_kernel(count, keep, got, *outs):
    rows = outs[0].shape[1]
    for out, at in zip(outs, z_places(rows)):
        combine_base(
            lambda f, at=at: keep[f, pl.ds(at, rows), :],
            lambda f, at=at: got[f, pl.ds(at, rows), :],
            count, storer(out),
        )


def core_slope_kernel(count, keep1, got1, keep2, got2, dmat, *outs):
    rows = outs[0].shape[1]
    places = z_places(rows)

    def pick(one, two):
        def field(f):
            ref, k = (one, f) if f < FIRST else (two, f - FIRST)
            return jnp.concatenate([ref[k, pl.ds(at, rows), :] for at in places], axis=0)
        return field

    def put(f, v):
        for n, ref in enumerate(outs):
            ref[f - FIRST] = v[rows * n : rows * (n + 1)]

    combine_slopes(pick(keep1, keep2), pick(got1, got2), count, dmat[...], put)


def span_base_kernel(count, own, one, two, three, out, left, right):
    combine_base(picker(own), picker(one), count, storer(left))
    combine_base(picker(two), picker(three), count, storer(right))
    combine_base(picker(left), picker(right), 2 * count, storer(out))


def span_slope_kernel(count, *refs):
    base, (own, one, two, three) = refs[:4], refs[4:8]
    left1, right1, dmat, out, left, right = refs[8:]
    d = dmat[...]
    combine_slopes(picker(base[0], own), picker(base[1], one), count, d, storer(None, left))
    combine_slopes(picker(base[2], two), picker(base[3], three), count, d, storer(None, right))
    combine_slopes(
        picker(left1, left), picker(right1, right), 2 * count, d, storer(None, out)
    )


def last_base_kernel(count, mine, other, after, out, state):
    combine_base(picker(mine), picker(other), count, storer(state))
    scale = 1.0 / (2 * count)
    for c in range(3):
        out[c] = state[MEAN + c]
    for k in range(NBASE):
        out[3 + k] = state[UU + k] * scale


def last_slope_kernel(count, mine1, other1, mine2, other2, dmat, out, state):
    combine_slopes(
        picker(mine1, mine2), picker(other1, other2), count, dmat[...], storer(None, state)
    )
    scale = 1.0 / (2 * count)
    for k in range(6):
        out[k] = state[PG - FIRST + k] * (scale * lead)
        out[6 + k] = state[GG - FIRST + k] * (scale * lead * lead)
    for k in range(5):
        out[12 + k] = state[UG - FIRST + k] * (scale * lead)
    out[17] = state[PG - FIRST + 5] * (scale * lead)


def gather_kernel(after, *refs):
    ins, out = refs[:-1], refs[-1]
    rows = ins[0].shape[1]
    zi = lax.axis_index("z")
    zn = lax.axis_size("z")
    for step, ref in enumerate(ins):
        at = pl.multiple_of(rows * lax.rem(zi + zn - step, zn), 8)
        out[:, pl.ds(at, rows), :] = ref[...]


def place_kernel(*refs):
    ins, out, sems = refs[:-2], refs[-2], refs[-1]
    zi = lax.axis_index("z")
    zn = lax.axis_size("z")
    core = lax.axis_index(CA)
    copies = []
    for k, ref in enumerate(ins):
        fields, rows = ref.shape[:2]
        if k < 2:
            first, side, step = 0, k, None
            at = rows * (core if side == 0 else 1 - core)
        else:
            first = OUT - fields
            side, step = divmod(k - 2, zn)
            c = core if side == 0 else 1 - core
            at = rows * (zn * c + lax.rem(zi + zn - step, zn))
        at = pl.multiple_of(at, 8)
        copies.append(
            pltpu.make_async_copy(
                ref, out.at[pl.ds(first, fields), pl.ds(at, rows)], sems.at[k]
            )
        )
    copy_all(copies)


def place(pieces, shape):
    return pl.pallas_call(
        place_kernel,
        in_specs=[pl.BlockSpec(memory_space=pltpu.VMEM)] * len(pieces),
        out_specs=pl.BlockSpec(memory_space=pltpu.HBM),
        out_shape=pltpu.HBM(shape, F32),
        scratch_shapes=[pltpu.SemaphoreType.DMA((len(pieces),))],
        compiler_params=pltpu.CompilerParams(vmem_limit_bytes=4 * 2**20),
        name="place",
    )(*pieces)


def small_call(kernel, outs, scratch, name, *args):
    vm = pl.BlockSpec(memory_space=pltpu.VMEM)
    return pl.pallas_call(
        kernel,
        in_specs=[vm] * len(args),
        out_specs=[vm] * len(outs),
        out_shape=[pltpu.VMEM(s, F32) for s in outs],
        scratch_shapes=[pltpu.VMEM(s, F32) for s in scratch],
        compiler_params=pltpu.CompilerParams(vmem_limit_bytes=8 * 2**20),
        cost_estimate=pl.CostEstimate(flops=1000, bytes_accessed=1000, transcendentals=0),
        name=name,
    )(*args)


def send(value, axis, step):
    size = lax.axis_size(axis)
    return lax.ppermute(value, axis, [(i, (i + step) % size) for i in range(size)])


def shards(flow, dy):
    _, lx, lz, ny = flow.shape
    gn = lax.axis_size(GXA)
    zn = lax.axis_size("z")
    up = [(i, i + 1) for i in range(gn - 1)]
    down = [(i + 1, i) for i in range(gn - 1)]
    zs, xs = (3, lx, 4, ny), (4, 4, lz, ny)
    zl, zr, xl, xr = cut(rim_kernel, [zs, zs, xs, xs], 4, "rims", flow)
    with jax.named_scope("rim_exchange"):
        zl = send(zl, ZA, 1)
        zr = send(zr, ZA, -1)
        xl = lax.ppermute(xl, GXA, up)
        xr = lax.ppermute(xr, GXA, down)
    pad, mean, keep1, give1 = base_moments(flow)
    ysl, dmat = y_slopes(pad, dy)
    rows = lx // 2 // zn
    one_piece, two_piece = (FIRST, rows, ny), (STATE - FIRST, rows, ny)

    def along_z(own, up, down, far):
        return [own, send(up, "z", 1), send(far, "z", 2), send(down, "z", -1)]

    def spread(done):
        return [done] + [send(done, "z", k) for k in (1, 2, 3)]

    with jax.named_scope("base_core"):
        got1 = send(give1, CA, 1)
        parts1 = small_call(
            functools.partial(core_base_kernel, lz), [one_piece] * 4, [], "core_base", keep1, got1
        )
    with jax.named_scope("base_span"):
        pieces1 = along_z(*parts1)
    pad, keep2, give2 = inner_moments(pad, ysl, zl, zr, mean, parts1[0])
    with jax.named_scope("base_span"):
        part1, left1, right1 = small_call(
            functools.partial(span_base_kernel, 2 * lz), [one_piece] * 3, [], "span_base", *pieces1
        )
    with jax.named_scope("base_x"):
        other1 = send(part1, "xh", 1)
    keep2, give2 = edge_moments(pad, keep2, give2, ysl, xl, xr, mean, part1)
    with jax.named_scope("slope_core"):
        got2 = send(give2, CA, 1)
        parts2 = small_call(
            functools.partial(core_slope_kernel, lz), [two_piece] * 4, [], "core_slope",
            keep1, got1, keep2, got2, dmat,
        )
    with jax.named_scope("base_x"):
        (done1,) = small_call(
            functools.partial(last_base_kernel, 2 * zn * lz),
            [(FIRST - 1, rows, ny)], [one_piece], "last_base", part1, other1, parts2[0],
        )
    with jax.named_scope("base_spread"):
        spread1 = spread(done1)
    with jax.named_scope("slope_span"):
        pieces2 = along_z(*parts2)
        (part2,) = small_call(
            functools.partial(span_slope_kernel, 2 * lz), [two_piece], [two_piece] * 2,
            "span_slope", *pieces1, *pieces2, left1, right1, dmat,
        )
    with jax.named_scope("slope_x"):
        other2 = send(part2, "xh", 1)
        (done2,) = small_call(
            functools.partial(last_slope_kernel, 2 * zn * lz),
            [(OUT - FIRST + 1, rows, ny)], [two_piece], "last_slope",
            part1, other1, part2, other2, dmat,
        )
    with jax.named_scope("base_spread"):
        (half1,) = small_call(
            gather_kernel, [(FIRST - 1, lx // 2, ny)], [], "gather", done2, *spread1
        )
        all1 = [half1, send(half1, CA, 1)]
    with jax.named_scope("slope_spread"):
        all2 = spread(done2)
        all2 = all2 + [send(v, CA, 1) for v in all2]
    return place(all1 + all2, (OUT, lx, ny))


def solution(mesh):
    gx, gz = mesh.shape["gx"], mesh.shape["gz"]
    fine = Mesh(mesh.devices.reshape(gx, 2, gz // 4, 2), (GXA,) + ZA)
    return jax.shard_map(
        shards,
        mesh=fine,
        in_specs=(P(None, GXA, ZA, None), P()),
        out_specs=P(None, GXA, None),
        check_vma=False,
    )
```

```python
import functools

import jax
import jax.numpy as jnp
from jax import lax
from jax.experimental import pallas as pl
from jax.experimental.pallas import tpu as pltpu
from jax.sharding import Mesh, PartitionSpec as P

F32 = jnp.float32
BF16 = jnp.bfloat16
lead = 4.0 / 5.0
ratios = (1.0, -0.25, 1.0 / 21.0, -1.0 / 224.0)
pairs = ((0, 0), (0, 1), (0, 2), (1, 1), (1, 2), (2, 2))
triples = (
    (0, 0, 0), (0, 0, 1), (0, 0, 2), (0, 1, 1), (0, 1, 2),
    (0, 2, 2), (1, 1, 1), (1, 1, 2), (1, 2, 2), (2, 2, 2),
)
MEAN, UU, UUU, PU, DXM, PG, GG, UG = 0, 4, 10, 20, 23, 27, 33, 39
FIRST = 23
STATE = 44
OUT = 40
NBASE = 19
z_order = (0, 2, 1, 3)
NSLOPE = 22
GXA, ZA, CA = "gx", ("xh", "z", "c"), "c"


def combine_base(left, right, count, put):
    half = [0.5 * (left(MEAN + c) - right(MEAN + c)) for c in range(4)]
    nh = [float(2 * count) * h for h in half]
    for c in range(4):
        put(MEAN + c, 0.5 * (left(MEAN + c) + right(MEAN + c)))
    gap = {}
    for k, (i, j) in enumerate(pairs):
        a, b = left(UU + k), right(UU + k)
        gap[i, j] = gap[j, i] = a - b
        put(UU + k, (a + b) + nh[i] * half[j])
    for k, (i, j, l) in enumerate(triples):
        fix = half[i] * gap[j, l] + half[j] * gap[i, l] + half[l] * gap[i, j]
        put(UUU + k, (left(UUU + k) + right(UUU + k)) + fix)
    for c in range(3):
        put(PU + c, (left(PU + c) + right(PU + c)) + nh[3] * half[c])


def combine_slopes(left, right, count, dmat, put):
    half = [0.5 * (left(MEAN + c) - right(MEAN + c)) for c in range(4)]
    gx = [0.5 * (left(DXM + c) - right(DXM + c)) for c in range(4)]
    rows = half[0].shape[0]
    turned = jnp.dot(
        jnp.concatenate(half, axis=0), dmat,
        precision=lax.Precision.HIGHEST, preferred_element_type=F32,
    )
    gy = [turned[c * rows : (c + 1) * rows] for c in range(4)]
    both = float(2 * count)
    nh = [both * h for h in half]
    for c in range(4):
        put(DXM + c, 0.5 * (left(DXM + c) + right(DXM + c)))
    fixes = (
        2.0 * nh[3] * gx[0],
        nh[3] * (gy[0] + gx[1]),
        nh[3] * gx[2],
        2.0 * nh[3] * gy[1],
        nh[3] * gy[2],
    )
    for k in range(5):
        put(PG + k, (left(PG + k) + right(PG + k)) + fixes[k])
    put(PG + 5, left(PG + 5) + right(PG + 5))
    for k, (i, j) in enumerate(pairs):
        fix = both * (gx[i] * gx[j] + gy[i] * gy[j])
        put(GG + k, (left(GG + k) + right(GG + k)) + fix)
    fixes = (
        2.0 * nh[0] * gx[3],
        nh[0] * gy[3] + nh[1] * gx[3],
        nh[2] * gx[3],
        2.0 * nh[1] * gy[3],
        nh[2] * gy[3],
    )
    for k in range(5):
        put(UG + k, (left(UG + k) + right(UG + k)) - fixes[k])


def copy_all(copies):
    for c in copies:
        c.start()
    for c in copies:
        c.wait()


def rim_kernel(flow, zl, zr, xl, xr, sems):
    _, lx, lz, _ = flow.shape
    copy_all([
        pltpu.make_async_copy(flow.at[pl.ds(0, 3), :, pl.ds(lz - 4, 4)], zl, sems.at[0]),
        pltpu.make_async_copy(flow.at[pl.ds(0, 3), :, pl.ds(0, 4)], zr, sems.at[1]),
        pltpu.make_async_copy(flow.at[:, pl.ds(lx - 4, 4)], xl, sems.at[2]),
        pltpu.make_async_copy(flow.at[:, pl.ds(0, 4)], xr, sems.at[3]),
    ])


def cut(kernel, shapes, copies, name, flow, *after):
    flow = pltpu.with_memory_space_constraint(flow, pltpu.HBM)
    return pl.pallas_call(
        kernel,
        in_specs=[pl.BlockSpec(memory_space=pltpu.HBM)]
        + [pl.BlockSpec(memory_space=pl.ANY)] * len(after),
        out_specs=[pl.BlockSpec(memory_space=pltpu.VMEM)] * len(shapes),
        out_shape=[pltpu.VMEM(s, F32) for s in shapes],
        scratch_shapes=[pltpu.SemaphoreType.DMA((copies,))],
        compiler_params=pltpu.CompilerParams(vmem_limit_bytes=4 * 2**20),
        name=name,
    )(flow, *after)


def base_kernel(raw, pad, mean, keep, send, acc):
    _, lx, ny = mean.shape
    lz = pad.shape[2] - 16
    half = lx // 2
    core = lax.axis_index(CA)
    def one(x, _):
        centre = []
        for c in range(4):
            m = jnp.sum(raw[c, x], axis=0, keepdims=True) * (1.0 / lz)
            mean[c, pl.ds(x, 1), :] = m
            centre.append(m)
        total = [None] * NBASE

        def add(n, v):
            total[n] = v if total[n] is None else total[n] + v

        for b in range(lz // 8):
            f = [raw[c, x, pl.ds(8 * b, 8), :] - centre[c] for c in range(4)]
            for c in range(4):
                pad[c, x + 4, pl.ds(8 + 8 * b, 8), :] = f[c]
            prod = {}
            for n, (i, j) in enumerate(pairs):
                prod[i, j] = f[i] * f[j]
                add(n, prod[i, j])
            for n, (i, j, l) in enumerate(triples):
                add(6 + n, prod[i, j] * f[l])
            for c in range(3):
                add(16 + c, f[3] * f[c])
        for n in range(NBASE):
            acc[pl.ds(pl.multiple_of(n * 8 * lx + 8 * x, 8), 8), :] = total[n]
        return 0

    lax.fori_loop(0, lx, one, 0, unroll=2)
    for out, side in ((send, 1 - core), (keep, core)):
        at = pl.multiple_of(half * side, 8)
        for c in range(4):
            out[MEAN + c] = mean[c, pl.ds(at, half), :]
        for k in range(NBASE):
            out[UU + k] = half_sum(k, acc, lx, at)


def y_kernel(pad, dy, ysl, dmat, weights):
    _, lx, lz, ny = ysl.shape
    step = 16
    d = dy[...].T * (1.0 / lead)
    dmat[...] = d
    dhi = d.astype(BF16)
    dlo = (d - dhi.astype(F32)).astype(BF16)
    weights[pl.ds(0, ny), pl.ds(0, ny)] = dhi
    weights[pl.ds(0, ny), pl.ds(ny, ny)] = dlo
    weights[pl.ds(ny, ny), pl.ds(0, ny)] = dhi
    weights[pl.ds(ny, ny), pl.ds(ny, ny)] = jnp.zeros_like(dlo)

    def part(k, _):
        left = []
        for r in range(step):
            for c in range(4):
                a = pad[c, step * k + r + 4, pl.ds(8, lz), :]
                hi = a.astype(BF16)
                lo = (a - hi.astype(F32)).astype(BF16)
                left.append(jnp.concatenate([hi, lo], axis=1))
        y = jnp.dot(jnp.concatenate(left, axis=0), weights[...], preferred_element_type=F32)
        y = y[:, :ny] + y[:, ny:]
        for r in range(step):
            for c in range(4):
                at = (4 * r + c) * lz
                ysl[c, step * k + r] = y[at : at + lz]
        return 0

    lax.fori_loop(0, lx // step, part, 0)


def row_sum(k, rows, acc):
    return sum(acc[pl.ds(8 * k * rows + s, rows, stride=8), :] for s in range(8))


def half_sum(k, acc, rows, at):
    where = pl.multiple_of(8 * (k * rows + at), 8)
    return sum(acc[pl.ds(where + s, rows // 2, stride=8), :] for s in range(8))


def base_moments(flow):
    _, lx, lz, ny = flow.shape
    vm = pl.BlockSpec(memory_space=pltpu.VMEM)
    half = (FIRST, lx // 2, ny)
    shapes = [(4, lx + 8, lz + 16, ny), (4, lx, ny), half, half]
    return pl.pallas_call(
        base_kernel,
        in_specs=[vm],
        out_specs=[vm] * 4,
        out_shape=[pltpu.VMEM(s, F32) for s in shapes],
        scratch_shapes=[
            pltpu.VMEM((NBASE * 8 * lx, ny), F32),
        ],
        compiler_params=pltpu.CompilerParams(vmem_limit_bytes=16 * 2**20),
        cost_estimate=pl.CostEstimate(flops=1000, bytes_accessed=1000, transcendentals=0),
        name="base_moments",
    )(pltpu.with_memory_space_constraint(flow, pltpu.VMEM))


def y_slopes(pad, dy):
    ny = dy.shape[0]
    lx, lz = pad.shape[1] - 8, pad.shape[2] - 16
    vm = pl.BlockSpec(memory_space=pltpu.VMEM)
    return pl.pallas_call(
        y_kernel,
        in_specs=[vm, vm],
        out_specs=[vm, vm],
        out_shape=[pltpu.VMEM((4, lx, lz, ny), F32), pltpu.VMEM((ny, ny), F32)],
        scratch_shapes=[pltpu.VMEM((2 * ny, 2 * ny), BF16)],
        compiler_params=pltpu.CompilerParams(vmem_limit_bytes=16 * 2**20),
        cost_estimate=pl.CostEstimate(flops=1000, bytes_accessed=1000, transcendentals=0),
        name="y_slopes",
    )(pad, dy)


def difference(upper, lower):
    out = None
    for k in range(4):
        diff = upper(k) - lower(k)
        out = diff if out is None else out + ratios[k] * diff
    return out


def slope_row(pad, ysl, x, with_x=True, rest=True):
    lz, ny = ysl.shape[2:]
    total = [None] * NSLOPE

    def add(k, v):
        total[k] = v if total[k] is None else total[k] + v

    if rest:
        row = lax.broadcasted_iota(jnp.int32, (8, ny), 0)
        row = jnp.minimum(row, 7 - row)
        weight = jnp.full((8, ny), sum(ratios), F32)
        for k in range(3):
            weight = jnp.where(row == k, sum(ratios[3 - k :]), weight)
        for c in range(3):
            total[c] = weight * (
                pad[c, x + 4, pl.ds(4 + lz, 8), :] - pad[c, x + 4, pl.ds(4, 8), :]
            )
    for b in range(lz // 8):
        at = 8 + 8 * b
        u = [pad[c, x + 4, pl.ds(at, 8), :] for c in range(4)]
        p = u[3]
        g = [[None] * 3 for _ in range(4)]
        if with_x:
            for c in range(4):
                g[c][0] = difference(
                    lambda k: pad[c, x + 5 + k, pl.ds(at, 8), :],
                    lambda k: pad[c, x + 3 - k, pl.ds(at, 8), :],
                )
        if rest:
            for c in range(4):
                g[c][1] = ysl[c, x, pl.ds(8 * b, 8), :]
            for c in range(3):
                g[c][2] = difference(
                    lambda k: pad[c, x + 4, pl.ds(at + 1 + k, 8), :],
                    lambda k: pad[c, x + 4, pl.ds(at - 1 - k, 8), :],
                )
        if with_x:
            add(3, p * g[0][0])
            add(6, p * g[2][0])
            add(17, u[0] * g[3][0])
            add(20, u[2] * g[3][0])
        if with_x and rest:
            add(4, p * (g[0][1] + g[1][0]))
            add(18, u[0] * g[3][1] + u[1] * g[3][0])
        elif with_x:
            add(4, p * g[1][0])
            add(18, u[1] * g[3][0])
        else:
            add(4, p * g[0][1])
            add(18, u[0] * g[3][1])
        if rest:
            add(5, p * g[0][2])
            add(7, p * g[1][1])
            add(8, p * g[1][2])
            add(9, p * g[2][1])
            add(10, p * g[2][2])
            add(19, u[1] * g[3][1])
            add(21, u[2] * g[3][1])
        dims = ((0,) if with_x else ()) + ((1, 2) if rest else ())
        for k, (i, j) in enumerate(pairs):
            for dim in dims:
                add(11 + k, g[i][dim] * g[j][dim])
    return total


def end_row(i, lx):
    return jnp.where(i < 4, i, lx - 8 + i)


def slope_fields(total, pressure):
    s02, s12, s22 = (total(n) + pressure * total(c) for c, n in enumerate((5, 8, 10)))
    yield PG + 0, 2.0 * total(3)
    yield PG + 1, total(4)
    yield PG + 2, s02 + total(6)
    yield PG + 3, 2.0 * total(7)
    yield PG + 4, s12 + total(9)
    yield PG + 5, 2.0 * s22
    for k in range(6):
        yield GG + k, total(11 + k)
    yield UG + 0, -2.0 * total(17)
    yield UG + 1, -total(18)
    yield UG + 2, s02 - total(20)
    yield UG + 3, -2.0 * total(19)
    yield UG + 4, s12 - total(21)


def inner_kernel(pad_in, ysl, zl, zr, mean, after, pad, keep, send, acc):
    _, lx, lz, ny = ysl.shape
    half = lx // 2
    core = lax.axis_index(CA)

    def rim(x, _):
        for c in range(3):
            m = mean[c, pl.ds(x, 1), :]
            pad[c, x + 4, pl.ds(4, 4), :] = zl[c, x] - m
            pad[c, x + 4, pl.ds(8 + lz, 4), :] = zr[c, x] - m
        return 0

    lax.fori_loop(0, lx, rim, 0, unroll=4)

    def one(x, _):
        total = slope_row(pad, ysl, x)
        for k in range(NSLOPE):
            acc[pl.ds(pl.multiple_of(k * 8 * lx + 8 * x, 8), 8), :] = total[k]
        return 0

    lax.fori_loop(4, lx - 4, one, 0, unroll=4)

    def end(i, _):
        x = end_row(i, lx)
        total = slope_row(pad, ysl, x, with_x=False)
        for k in range(NSLOPE):
            v = jnp.zeros((8, ny), F32) if total[k] is None else total[k]
            acc[pl.ds(pl.multiple_of(k * 8 * lx + 8 * x, 8), 8), :] = v
        return 0

    lax.fori_loop(0, 8, end, 0, unroll=4)

    for out, side in ((send, 1 - core), (keep, core)):
        at = pl.multiple_of(half * side, 8)

        fields = slope_fields(
            lambda k, at=at: half_sum(k, acc, lx, at), mean[3, pl.ds(at, half), :]
        )
        for f, v in fields:
            out[f - FIRST] = v


def inner_moments(pad, ysl, zl, zr, mean, after):
    _, lx, lz, ny = ysl.shape
    vm = pl.BlockSpec(memory_space=pltpu.VMEM)
    shape = pltpu.VMEM((STATE - FIRST, lx // 2, ny), F32)
    return pl.pallas_call(
        inner_kernel,
        in_specs=[vm] * 5 + [pl.BlockSpec(memory_space=pl.ANY)],
        out_specs=[vm] * 3,
        out_shape=[pltpu.VMEM(pad.shape, F32), shape, shape],
        input_output_aliases={0: 0},
        scratch_shapes=[pltpu.VMEM((NSLOPE * 8 * lx, ny), F32)],
        compiler_params=pltpu.CompilerParams(vmem_limit_bytes=16 * 2**20),
        cost_estimate=pl.CostEstimate(
            flops=1500000000, bytes_accessed=84_000_000, transcendentals=0
        ),
        name="inner_moments",
    )(pad, ysl, zl, zr, mean, after)


def edge_kernel(
    pad_in, keep_in, send_in, ysl, xl, xr, mean, after, pad, keep, send, acc, mpad, dxm
):
    _, lx, lz, ny = ysl.shape
    half = lx // 2
    core = lax.axis_index(CA)
    gi = lax.axis_index(GXA)
    at_ends = (gi == 0, gi == lax.axis_size(GXA) - 1)

    for c in range(4):
        mpad[c, pl.ds(8, lx), :] = mean[c]
        for j in range(4):
            for halo, at_end, src, dst in (
                (xl, at_ends[0], 3 - j, j), (xr, at_ends[1], lx - 1 - j, lx + 4 + j)
            ):
                own = pad[c, src + 4, pl.ds(8, lz), :]
                m = jnp.sum(halo[c, j], axis=0, keepdims=True) * (1.0 / lz)
                pad[c, dst, pl.ds(8, lz), :] = jnp.where(at_end, own, halo[c, j] - m)
                mpad[c, pl.ds(dst + 4, 1), :] = jnp.where(at_end, mean[c, pl.ds(src, 1), :], m)
        dxm[c] = difference(
            lambda k: mpad[c, pl.ds(9 + k, lx), :], lambda k: mpad[c, pl.ds(7 - k, lx), :]
        )

    for out, side in ((send, 1 - core), (keep, core)):
        for c in range(4):
            out[DXM - FIRST + c] = dxm[c, pl.ds(pl.multiple_of(half * side, 8), half), :]

    def one(i, _):
        total = slope_row(pad, ysl, end_row(i, lx), rest=False)
        for k in used:
            acc[pl.ds(pl.multiple_of(k * 64 + 8 * i, 8), 8), :] = total[k]
        return 0

    used = (3, 4, 6, 11, 12, 13, 14, 15, 16, 17, 18, 20)
    lax.fori_loop(0, 8, one, 0, unroll=4)

    def total(k):
        return row_sum(k, 8, acc)

    fields = [(PG + 0, 2.0 * total(3)), (PG + 1, total(4)), (PG + 2, total(6))]
    fields += [(GG + k, total(11 + k)) for k in range(6)]
    fields += [(UG + 0, -2.0 * total(17)), (UG + 1, -total(18)), (UG + 2, -total(20))]
    for side, rows in ((0, slice(0, 4)), (1, slice(4, 8))):
        at = pl.ds(0 if side == 0 else half - 4, 4)

        @pl.when(core == side)
        def _():
            for f, v in fields:
                keep[f - FIRST, at, :] = keep[f - FIRST, at, :] + v[rows]

        @pl.when(core != side)
        def _():
            for f, v in fields:
                send[f - FIRST, at, :] = send[f - FIRST, at, :] + v[rows]


def edge_moments(pad, keep, send, ysl, xl, xr, mean, after):
    _, lx, lz, ny = ysl.shape
    vm = pl.BlockSpec(memory_space=pltpu.VMEM)
    out = pl.pallas_call(
        edge_kernel,
        in_specs=[vm] * 7 + [pl.BlockSpec(memory_space=pl.ANY)],
        out_specs=[vm] * 3,
        out_shape=[pltpu.VMEM(v.shape, F32) for v in (pad, keep, send)],
        input_output_aliases={0: 0, 1: 1, 2: 2},
        scratch_shapes=[
            pltpu.VMEM((NSLOPE * 64, ny), F32),
            pltpu.VMEM((4, lx + 16, ny), F32),
            pltpu.VMEM((4, lx, ny), F32),
        ],
        compiler_params=pltpu.CompilerParams(vmem_limit_bytes=16 * 2**20),
        cost_estimate=pl.CostEstimate(
            flops=25 * ysl.size, bytes_accessed=ysl.size // 2, transcendentals=0
        ),
        name="edge_moments",
    )(pad, keep, send, ysl, xl, xr, mean, after)
    return out[1:]


def picker(one, two=None):
    return lambda f: one[f] if f < FIRST else two[f - FIRST]


def storer(one, two=None):
    def put(f, v):
        if f < FIRST:
            one[f] = v
        else:
            two[f - FIRST] = v
    return put


def z_places(rows):
    zi = lax.axis_index("z")
    zn = lax.axis_size("z")
    return [pl.multiple_of(rows * lax.rem(zi + k, zn), 8) for k in (0, 1, zn - 1, 2)]


def core_base_kernel(count, keep, got, *outs):
    rows = outs[0].shape[1]
    for out, at in zip(outs, z_places(rows)):
        combine_base(
            lambda f, at=at: keep[f, pl.ds(at, rows), :],
            lambda f, at=at: got[f, pl.ds(at, rows), :],
            count, storer(out),
        )


def core_slope_kernel(count, keep1, got1, keep2, got2, dmat, *outs):
    rows = outs[0].shape[1]
    places = z_places(rows)

    def pick(one, two):
        def field(f):
            ref, k = (one, f) if f < FIRST else (two, f - FIRST)
            return jnp.concatenate([ref[k, pl.ds(at, rows), :] for at in places], axis=0)
        return field

    def put(f, v):
        for n, ref in enumerate(outs):
            ref[f - FIRST] = v[rows * n : rows * (n + 1)]

    combine_slopes(pick(keep1, keep2), pick(got1, got2), count, dmat[...], put)


def span_base_kernel(count, own, one, two, three, out, left, right):
    combine_base(picker(own), picker(one), count, storer(left))
    combine_base(picker(two), picker(three), count, storer(right))
    combine_base(picker(left), picker(right), 2 * count, storer(out))


def span_slope_kernel(count, *refs):
    base, (own, one, two, three) = refs[:4], refs[4:8]
    left1, right1, dmat, out, left, right = refs[8:]
    d = dmat[...]
    combine_slopes(picker(base[0], own), picker(base[1], one), count, d, storer(None, left))
    combine_slopes(picker(base[2], two), picker(base[3], three), count, d, storer(None, right))
    combine_slopes(
        picker(left1, left), picker(right1, right), 2 * count, d, storer(None, out)
    )


def last_base_kernel(count, mine, other, after, out, state):
    combine_base(picker(mine), picker(other), count, storer(state))
    scale = 1.0 / (2 * count)
    for c in range(3):
        out[c] = state[MEAN + c]
    for k in range(NBASE):
        out[3 + k] = state[UU + k] * scale


def last_slope_kernel(count, mine1, other1, mine2, other2, dmat, out, state):
    combine_slopes(
        picker(mine1, mine2), picker(other1, other2), count, dmat[...], storer(None, state)
    )
    scale = 1.0 / (2 * count)
    for k in range(6):
        out[k] = state[PG - FIRST + k] * (scale * lead)
        out[6 + k] = state[GG - FIRST + k] * (scale * lead * lead)
    for k in range(5):
        out[12 + k] = state[UG - FIRST + k] * (scale * lead)
    out[17] = state[PG - FIRST + 5] * (scale * lead)


def gather_kernel(after, *refs):
    ins, out = refs[:-1], refs[-1]
    rows = ins[0].shape[1]
    zi = lax.axis_index("z")
    zn = lax.axis_size("z")
    for step, ref in enumerate(ins):
        at = pl.multiple_of(rows * lax.rem(zi + zn - step, zn), 8)
        out[:, pl.ds(at, rows), :] = ref[...]


def place_kernel(*refs):
    ins, out, sems = refs[:-2], refs[-2], refs[-1]
    zi = lax.axis_index("z")
    zn = lax.axis_size("z")
    core = lax.axis_index(CA)
    copies = []
    for k, ref in enumerate(ins):
        fields, rows = ref.shape[:2]
        if k < 2:
            first, side, step = 0, k, None
            at = rows * (core if side == 0 else 1 - core)
        else:
            first = OUT - fields
            side, step = divmod(k - 2, zn)
            c = core if side == 0 else 1 - core
            at = rows * (zn * c + lax.rem(zi + zn - z_order[step], zn))
        at = pl.multiple_of(at, 8)
        copies.append(
            pltpu.make_async_copy(
                ref, out.at[pl.ds(first, fields), pl.ds(at, rows)], sems.at[k]
            )
        )
    copy_all(copies)


def place(pieces, shape):
    return pl.pallas_call(
        place_kernel,
        in_specs=[pl.BlockSpec(memory_space=pltpu.VMEM)] * len(pieces),
        out_specs=pl.BlockSpec(memory_space=pltpu.HBM),
        out_shape=pltpu.HBM(shape, F32),
        scratch_shapes=[pltpu.SemaphoreType.DMA((len(pieces),))],
        compiler_params=pltpu.CompilerParams(vmem_limit_bytes=4 * 2**20),
        name="place",
    )(*pieces)


def small_call(kernel, outs, scratch, name, *args):
    vm = pl.BlockSpec(memory_space=pltpu.VMEM)
    return pl.pallas_call(
        kernel,
        in_specs=[vm] * len(args),
        out_specs=[vm] * len(outs),
        out_shape=[pltpu.VMEM(s, F32) for s in outs],
        scratch_shapes=[pltpu.VMEM(s, F32) for s in scratch],
        compiler_params=pltpu.CompilerParams(vmem_limit_bytes=8 * 2**20),
        cost_estimate=pl.CostEstimate(flops=1000, bytes_accessed=1000, transcendentals=0),
        name=name,
    )(*args)


def send(value, axis, step):
    size = lax.axis_size(axis)
    return lax.ppermute(value, axis, [(i, (i + step) % size) for i in range(size)])


def shards(flow, dy):
    _, lx, lz, ny = flow.shape
    gn = lax.axis_size(GXA)
    zn = lax.axis_size("z")
    up = [(i, i + 1) for i in range(gn - 1)]
    down = [(i + 1, i) for i in range(gn - 1)]
    zs, xs = (3, lx, 4, ny), (4, 4, lz, ny)
    zl, zr, xl, xr = cut(rim_kernel, [zs, zs, xs, xs], 4, "rims", flow)
    with jax.named_scope("rim_exchange"):
        zl = send(zl, ZA, 1)
        zr = send(zr, ZA, -1)
        xl = lax.ppermute(xl, GXA, up)
        xr = lax.ppermute(xr, GXA, down)
    pad, mean, keep1, give1 = base_moments(flow)
    ysl, dmat = y_slopes(pad, dy)
    rows = lx // 2 // zn
    one_piece, two_piece = (FIRST, rows, ny), (STATE - FIRST, rows, ny)

    def along_z(own, up, down, far):
        return [own, send(up, "z", 1), send(far, "z", 2), send(down, "z", -1)]

    def spread(done):
        return [done] + [send(done, "z", k) for k in (1, 2, 3)]

    with jax.named_scope("base_core"):
        got1 = send(give1, CA, 1)
        parts1 = small_call(
            functools.partial(core_base_kernel, lz), [one_piece] * 4, [], "core_base", keep1, got1
        )
    with jax.named_scope("base_span"):
        pieces1 = along_z(*parts1)
    pad, keep2, give2 = inner_moments(pad, ysl, zl, zr, mean, parts1[0])
    with jax.named_scope("base_span"):
        part1, left1, right1 = small_call(
            functools.partial(span_base_kernel, 2 * lz), [one_piece] * 3, [], "span_base", *pieces1
        )
    with jax.named_scope("base_x"):
        other1 = send(part1, "xh", 1)
    keep2, give2 = edge_moments(pad, keep2, give2, ysl, xl, xr, mean, part1)
    with jax.named_scope("slope_core"):
        got2 = send(give2, CA, 1)
        parts2 = small_call(
            functools.partial(core_slope_kernel, lz), [two_piece] * 4, [], "core_slope",
            keep1, got1, keep2, got2, dmat,
        )
    with jax.named_scope("base_x"):
        (done1,) = small_call(
            functools.partial(last_base_kernel, 2 * zn * lz),
            [(FIRST - 1, rows, ny)], [one_piece], "last_base", part1, other1, parts2[0],
        )
    with jax.named_scope("base_spread"):
        spread1 = spread(done1)
    with jax.named_scope("slope_span"):
        pieces2 = along_z(*parts2)
        (part2,) = small_call(
            functools.partial(span_slope_kernel, 2 * lz), [two_piece], [two_piece] * 2,
            "span_slope", *pieces1, *pieces2, left1, right1, dmat,
        )
    with jax.named_scope("slope_x"):
        other2 = send(part2, "xh", 1)
        (done2,) = small_call(
            functools.partial(last_slope_kernel, 2 * zn * lz),
            [(OUT - FIRST + 1, rows, ny)], [two_piece], "last_slope",
            part1, other1, part2, other2, dmat,
        )
    with jax.named_scope("base_spread"):
        (half1,) = small_call(
            gather_kernel, [(FIRST - 1, lx // 2, ny)], [], "gather", done2, *spread1
        )
        all1 = [half1, send(half1, CA, 1)]
    with jax.named_scope("slope_spread"):
        all2 = [done2] + [send(done2, "z", k) for k in z_order[1:]]
        all2 = all2 + [send(v, CA, 1) for v in all2]
    return place(all1 + all2, (OUT, lx, ny))


def solution(mesh):
    gx, gz = mesh.shape["gx"], mesh.shape["gz"]
    fine = Mesh(mesh.devices.reshape(gx, 2, gz // 4, 2), (GXA,) + ZA)
    return jax.shard_map(
        shards,
        mesh=fine,
        in_specs=(P(None, GXA, ZA, None), P()),
        out_specs=P(None, GXA, None),
        check_vma=False,
    )
```

```python
import functools

import jax
import jax.numpy as jnp
from jax import lax
from jax.experimental import pallas as pl
from jax.experimental.pallas import tpu as pltpu
from jax.sharding import Mesh, PartitionSpec as P

F32 = jnp.float32
BF16 = jnp.bfloat16
lead = 4.0 / 5.0
ratios = (1.0, -0.25, 1.0 / 21.0, -1.0 / 224.0)
pairs = ((0, 0), (0, 1), (0, 2), (1, 1), (1, 2), (2, 2))
triples = (
    (0, 0, 0), (0, 0, 1), (0, 0, 2), (0, 1, 1), (0, 1, 2),
    (0, 2, 2), (1, 1, 1), (1, 1, 2), (1, 2, 2), (2, 2, 2),
)
MEAN, UU, UUU, PU, DXM, PG, GG, UG = 0, 4, 10, 20, 23, 27, 33, 39
FIRST = 23
STATE = 44
OUT = 40
NBASE = 19
z_order = (0, 2, 1, 3)
NSLOPE = 22
GXA, ZA, CA = "gx", ("xh", "z", "c"), "c"


def combine_base(left, right, count, put):
    half = [0.5 * (left(MEAN + c) - right(MEAN + c)) for c in range(4)]
    nh = [float(2 * count) * h for h in half]
    for c in range(4):
        put(MEAN + c, 0.5 * (left(MEAN + c) + right(MEAN + c)))
    gap = {}
    for k, (i, j) in enumerate(pairs):
        a, b = left(UU + k), right(UU + k)
        gap[i, j] = gap[j, i] = a - b
        put(UU + k, (a + b) + nh[i] * half[j])
    for k, (i, j, l) in enumerate(triples):
        fix = half[i] * gap[j, l] + half[j] * gap[i, l] + half[l] * gap[i, j]
        put(UUU + k, (left(UUU + k) + right(UUU + k)) + fix)
    for c in range(3):
        put(PU + c, (left(PU + c) + right(PU + c)) + nh[3] * half[c])


def combine_slopes(left, right, count, dmat, put):
    half = [0.5 * (left(MEAN + c) - right(MEAN + c)) for c in range(4)]
    gx = [0.5 * (left(DXM + c) - right(DXM + c)) for c in range(4)]
    rows = half[0].shape[0]
    turned = jnp.dot(
        jnp.concatenate(half, axis=0), dmat,
        precision=lax.Precision.HIGHEST, preferred_element_type=F32,
    )
    gy = [turned[c * rows : (c + 1) * rows] for c in range(4)]
    both = float(2 * count)
    nh = [both * h for h in half]
    for c in range(4):
        put(DXM + c, 0.5 * (left(DXM + c) + right(DXM + c)))
    fixes = (
        2.0 * nh[3] * gx[0],
        nh[3] * (gy[0] + gx[1]),
        nh[3] * gx[2],
        2.0 * nh[3] * gy[1],
        nh[3] * gy[2],
    )
    for k in range(5):
        put(PG + k, (left(PG + k) + right(PG + k)) + fixes[k])
    put(PG + 5, left(PG + 5) + right(PG + 5))
    for k, (i, j) in enumerate(pairs):
        fix = both * (gx[i] * gx[j] + gy[i] * gy[j])
        put(GG + k, (left(GG + k) + right(GG + k)) + fix)
    fixes = (
        2.0 * nh[0] * gx[3],
        nh[0] * gy[3] + nh[1] * gx[3],
        nh[2] * gx[3],
        2.0 * nh[1] * gy[3],
        nh[2] * gy[3],
    )
    for k in range(5):
        put(UG + k, (left(UG + k) + right(UG + k)) - fixes[k])


def copy_all(copies):
    for c in copies:
        c.start()
    for c in copies:
        c.wait()


def rim_kernel(flow, zl, zr, xl, xr, sems):
    _, lx, lz, _ = flow.shape
    copy_all([
        pltpu.make_async_copy(flow.at[pl.ds(0, 3), :, pl.ds(lz - 4, 4)], zl, sems.at[0]),
        pltpu.make_async_copy(flow.at[pl.ds(0, 3), :, pl.ds(0, 4)], zr, sems.at[1]),
        pltpu.make_async_copy(flow.at[:, pl.ds(lx - 4, 4)], xl, sems.at[2]),
        pltpu.make_async_copy(flow.at[:, pl.ds(0, 4)], xr, sems.at[3]),
    ])


def cut(kernel, shapes, copies, name, flow, *after):
    flow = pltpu.with_memory_space_constraint(flow, pltpu.HBM)
    return pl.pallas_call(
        kernel,
        in_specs=[pl.BlockSpec(memory_space=pltpu.HBM)]
        + [pl.BlockSpec(memory_space=pl.ANY)] * len(after),
        out_specs=[pl.BlockSpec(memory_space=pltpu.VMEM)] * len(shapes),
        out_shape=[pltpu.VMEM(s, F32) for s in shapes],
        scratch_shapes=[pltpu.SemaphoreType.DMA((copies,))],
        compiler_params=pltpu.CompilerParams(vmem_limit_bytes=4 * 2**20),
        name=name,
    )(flow, *after)


def base_kernel(raw, pad, mean, keep, send, acc):
    _, lx, ny = mean.shape
    lz = pad.shape[2] - 16
    half = lx // 2
    core = lax.axis_index(CA)
    def one(x, _):
        centre = []
        for c in range(4):
            m = jnp.sum(raw[c, x], axis=0, keepdims=True) * (1.0 / lz)
            mean[c, pl.ds(x, 1), :] = m
            centre.append(m)
        total = [None] * NBASE

        def add(n, v):
            total[n] = v if total[n] is None else total[n] + v

        for b in range(lz // 8):
            f = [raw[c, x, pl.ds(8 * b, 8), :] - centre[c] for c in range(4)]
            for c in range(4):
                pad[c, x + 4, pl.ds(8 + 8 * b, 8), :] = f[c]
            prod = {}
            for n, (i, j) in enumerate(pairs):
                prod[i, j] = f[i] * f[j]
                add(n, prod[i, j])
            for n, (i, j, l) in enumerate(triples):
                add(6 + n, prod[i, j] * f[l])
            for c in range(3):
                add(16 + c, f[3] * f[c])
        for n in range(NBASE):
            acc[pl.ds(pl.multiple_of(n * 8 * lx + 8 * x, 8), 8), :] = total[n]
        return 0

    lax.fori_loop(0, lx, one, 0, unroll=2)
    for out, side in ((send, 1 - core), (keep, core)):
        at = pl.multiple_of(half * side, 8)
        for c in range(4):
            out[MEAN + c] = mean[c, pl.ds(at, half), :]
        for k in range(NBASE):
            out[UU + k] = half_sum(k, acc, lx, at)


def y_kernel(pad, dy, ysl, dmat, weights):
    _, lx, lz, ny = ysl.shape
    step = 16
    d = dy[...].T * (1.0 / lead)
    dmat[...] = d
    dhi = d.astype(BF16)
    dlo = (d - dhi.astype(F32)).astype(BF16)
    weights[pl.ds(0, ny), pl.ds(0, ny)] = dhi
    weights[pl.ds(0, ny), pl.ds(ny, ny)] = dlo
    weights[pl.ds(ny, ny), pl.ds(0, ny)] = dhi
    weights[pl.ds(ny, ny), pl.ds(ny, ny)] = jnp.zeros_like(dlo)

    def part(k, _):
        left = []
        for r in range(step):
            for c in range(4):
                a = pad[c, step * k + r + 4, pl.ds(8, lz), :]
                hi = a.astype(BF16)
                lo = (a - hi.astype(F32)).astype(BF16)
                left.append(jnp.concatenate([hi, lo], axis=1))
        y = jnp.dot(jnp.concatenate(left, axis=0), weights[...], preferred_element_type=F32)
        y = y[:, :ny] + y[:, ny:]
        for r in range(step):
            for c in range(4):
                at = (4 * r + c) * lz
                ysl[c, step * k + r] = y[at : at + lz]
        return 0

    lax.fori_loop(0, lx // step, part, 0)


def row_sum(k, rows, acc):
    return sum(acc[pl.ds(8 * k * rows + s, rows, stride=8), :] for s in range(8))


def half_sum(k, acc, rows, at):
    where = pl.multiple_of(8 * (k * rows + at), 8)
    return sum(acc[pl.ds(where + s, rows // 2, stride=8), :] for s in range(8))


def base_moments(flow):
    _, lx, lz, ny = flow.shape
    vm = pl.BlockSpec(memory_space=pltpu.VMEM)
    half = (FIRST, lx // 2, ny)
    shapes = [(4, lx + 8, lz + 16, ny), (4, lx, ny), half, half]
    return pl.pallas_call(
        base_kernel,
        in_specs=[vm],
        out_specs=[vm] * 4,
        out_shape=[pltpu.VMEM(s, F32) for s in shapes],
        scratch_shapes=[
            pltpu.VMEM((NBASE * 8 * lx, ny), F32),
        ],
        compiler_params=pltpu.CompilerParams(vmem_limit_bytes=16 * 2**20),
        cost_estimate=pl.CostEstimate(flops=1000, bytes_accessed=1000, transcendentals=0),
        name="base_moments",
    )(pltpu.with_memory_space_constraint(flow, pltpu.VMEM))


def y_slopes(pad, dy):
    ny = dy.shape[0]
    lx, lz = pad.shape[1] - 8, pad.shape[2] - 16
    vm = pl.BlockSpec(memory_space=pltpu.VMEM)
    return pl.pallas_call(
        y_kernel,
        in_specs=[vm, vm],
        out_specs=[vm, vm],
        out_shape=[pltpu.VMEM((4, lx, lz, ny), F32), pltpu.VMEM((ny, ny), F32)],
        scratch_shapes=[pltpu.VMEM((2 * ny, 2 * ny), BF16)],
        compiler_params=pltpu.CompilerParams(vmem_limit_bytes=16 * 2**20),
        cost_estimate=pl.CostEstimate(flops=1000, bytes_accessed=1000, transcendentals=0),
        name="y_slopes",
    )(pad, dy)


def difference(upper, lower):
    out = None
    for k in range(4):
        diff = upper(k) - lower(k)
        out = diff if out is None else out + ratios[k] * diff
    return out


def slope_row(pad, ysl, x, with_x=True, rest=True):
    lz, ny = ysl.shape[2:]
    total = [None] * NSLOPE

    def add(k, v):
        total[k] = v if total[k] is None else total[k] + v

    if rest:
        row = lax.broadcasted_iota(jnp.int32, (8, ny), 0)
        row = jnp.minimum(row, 7 - row)
        weight = jnp.full((8, ny), sum(ratios), F32)
        for k in range(3):
            weight = jnp.where(row == k, sum(ratios[3 - k :]), weight)
        for c in range(3):
            total[c] = weight * (
                pad[c, x + 4, pl.ds(4 + lz, 8), :] - pad[c, x + 4, pl.ds(4, 8), :]
            )
    for b in range(lz // 8):
        at = 8 + 8 * b
        u = [pad[c, x + 4, pl.ds(at, 8), :] for c in range(4)]
        p = u[3]
        g = [[None] * 3 for _ in range(4)]
        if with_x:
            for c in range(4):
                g[c][0] = difference(
                    lambda k: pad[c, x + 5 + k, pl.ds(at, 8), :],
                    lambda k: pad[c, x + 3 - k, pl.ds(at, 8), :],
                )
        if rest:
            for c in range(4):
                g[c][1] = ysl[c, x, pl.ds(8 * b, 8), :]
            for c in range(3):
                g[c][2] = difference(
                    lambda k: pad[c, x + 4, pl.ds(at + 1 + k, 8), :],
                    lambda k: pad[c, x + 4, pl.ds(at - 1 - k, 8), :],
                )
        if with_x:
            add(3, p * g[0][0])
            add(6, p * g[2][0])
            add(17, u[0] * g[3][0])
            add(20, u[2] * g[3][0])
        if with_x and rest:
            add(4, p * (g[0][1] + g[1][0]))
            add(18, u[0] * g[3][1] + u[1] * g[3][0])
        elif with_x:
            add(4, p * g[1][0])
            add(18, u[1] * g[3][0])
        else:
            add(4, p * g[0][1])
            add(18, u[0] * g[3][1])
        if rest:
            add(5, p * g[0][2])
            add(7, p * g[1][1])
            add(8, p * g[1][2])
            add(9, p * g[2][1])
            add(10, p * g[2][2])
            add(19, u[1] * g[3][1])
            add(21, u[2] * g[3][1])
        dims = ((0,) if with_x else ()) + ((1, 2) if rest else ())
        for k, (i, j) in enumerate(pairs):
            for dim in dims:
                add(11 + k, g[i][dim] * g[j][dim])
    return total


def end_row(i, lx):
    return jnp.where(i < 4, i, lx - 8 + i)


def slope_fields(total, pressure):
    s02, s12, s22 = (total(n) + pressure * total(c) for c, n in enumerate((5, 8, 10)))
    yield PG + 0, 2.0 * total(3)
    yield PG + 1, total(4)
    yield PG + 2, s02 + total(6)
    yield PG + 3, 2.0 * total(7)
    yield PG + 4, s12 + total(9)
    yield PG + 5, 2.0 * s22
    for k in range(6):
        yield GG + k, total(11 + k)
    yield UG + 0, -2.0 * total(17)
    yield UG + 1, -total(18)
    yield UG + 2, s02 - total(20)
    yield UG + 3, -2.0 * total(19)
    yield UG + 4, s12 - total(21)


def inner_kernel(pad_in, ysl, zl, zr, mean, after, pad, keep, send, acc):
    _, lx, lz, ny = ysl.shape
    half = lx // 2
    core = lax.axis_index(CA)

    def rim(x, _):
        for c in range(3):
            m = mean[c, pl.ds(x, 1), :]
            pad[c, x + 4, pl.ds(4, 4), :] = zl[c, x] - m
            pad[c, x + 4, pl.ds(8 + lz, 4), :] = zr[c, x] - m
        return 0

    lax.fori_loop(0, lx, rim, 0, unroll=4)

    def one(x, _):
        total = slope_row(pad, ysl, x)
        for k in range(NSLOPE):
            acc[pl.ds(pl.multiple_of(k * 8 * lx + 8 * x, 8), 8), :] = total[k]
        return 0

    lax.fori_loop(4, lx - 4, one, 0, unroll=4)

    def end(i, _):
        x = end_row(i, lx)
        total = slope_row(pad, ysl, x, with_x=False)
        for k in range(NSLOPE):
            v = jnp.zeros((8, ny), F32) if total[k] is None else total[k]
            acc[pl.ds(pl.multiple_of(k * 8 * lx + 8 * x, 8), 8), :] = v
        return 0

    lax.fori_loop(0, 8, end, 0, unroll=4)

    for out, side in ((send, 1 - core), (keep, core)):
        at = pl.multiple_of(half * side, 8)

        fields = slope_fields(
            lambda k, at=at: half_sum(k, acc, lx, at), mean[3, pl.ds(at, half), :]
        )
        for f, v in fields:
            out[f - FIRST] = v


def inner_moments(pad, ysl, zl, zr, mean, after):
    _, lx, lz, ny = ysl.shape
    vm = pl.BlockSpec(memory_space=pltpu.VMEM)
    shape = pltpu.VMEM((STATE - FIRST, lx // 2, ny), F32)
    return pl.pallas_call(
        inner_kernel,
        in_specs=[vm] * 5 + [pl.BlockSpec(memory_space=pl.ANY)],
        out_specs=[vm] * 3,
        out_shape=[pltpu.VMEM(pad.shape, F32), shape, shape],
        input_output_aliases={0: 0},
        scratch_shapes=[pltpu.VMEM((NSLOPE * 8 * lx, ny), F32)],
        compiler_params=pltpu.CompilerParams(vmem_limit_bytes=16 * 2**20),
        cost_estimate=pl.CostEstimate(
            flops=1500000000, bytes_accessed=84_000_000, transcendentals=0
        ),
        name="inner_moments",
    )(pad, ysl, zl, zr, mean, after)


def edge_kernel(
    pad_in, keep_in, send_in, ysl, xl, xr, mean, after, pad, keep, send, acc, mpad, dxm
):
    _, lx, lz, ny = ysl.shape
    half = lx // 2
    core = lax.axis_index(CA)
    gi = lax.axis_index(GXA)
    at_ends = (gi == 0, gi == lax.axis_size(GXA) - 1)

    for c in range(4):
        mpad[c, pl.ds(8, lx), :] = mean[c]
        for j in range(4):
            for halo, at_end, src, dst in (
                (xl, at_ends[0], 3 - j, j), (xr, at_ends[1], lx - 1 - j, lx + 4 + j)
            ):
                own = pad[c, src + 4, pl.ds(8, lz), :]
                m = jnp.sum(halo[c, j], axis=0, keepdims=True) * (1.0 / lz)
                pad[c, dst, pl.ds(8, lz), :] = jnp.where(at_end, own, halo[c, j] - m)
                mpad[c, pl.ds(dst + 4, 1), :] = jnp.where(at_end, mean[c, pl.ds(src, 1), :], m)
        dxm[c] = difference(
            lambda k: mpad[c, pl.ds(9 + k, lx), :], lambda k: mpad[c, pl.ds(7 - k, lx), :]
        )

    for out, side in ((send, 1 - core), (keep, core)):
        for c in range(4):
            out[DXM - FIRST + c] = dxm[c, pl.ds(pl.multiple_of(half * side, 8), half), :]

    def one(i, _):
        total = slope_row(pad, ysl, end_row(i, lx), rest=False)
        for k in used:
            acc[pl.ds(pl.multiple_of(k * 64 + 8 * i, 8), 8), :] = total[k]
        return 0

    used = (3, 4, 6, 11, 12, 13, 14, 15, 16, 17, 18, 20)
    lax.fori_loop(0, 8, one, 0, unroll=4)

    def total(k):
        return row_sum(k, 8, acc)

    fields = [(PG + 0, 2.0 * total(3)), (PG + 1, total(4)), (PG + 2, total(6))]
    fields += [(GG + k, total(11 + k)) for k in range(6)]
    fields += [(UG + 0, -2.0 * total(17)), (UG + 1, -total(18)), (UG + 2, -total(20))]
    for side, rows in ((0, slice(0, 4)), (1, slice(4, 8))):
        at = pl.ds(0 if side == 0 else half - 4, 4)

        @pl.when(core == side)
        def _():
            for f, v in fields:
                keep[f - FIRST, at, :] = keep[f - FIRST, at, :] + v[rows]

        @pl.when(core != side)
        def _():
            for f, v in fields:
                send[f - FIRST, at, :] = send[f - FIRST, at, :] + v[rows]


def edge_moments(pad, keep, send, ysl, xl, xr, mean, after):
    _, lx, lz, ny = ysl.shape
    vm = pl.BlockSpec(memory_space=pltpu.VMEM)
    out = pl.pallas_call(
        edge_kernel,
        in_specs=[vm] * 7 + [pl.BlockSpec(memory_space=pl.ANY)],
        out_specs=[vm] * 3,
        out_shape=[pltpu.VMEM(v.shape, F32) for v in (pad, keep, send)],
        input_output_aliases={0: 0, 1: 1, 2: 2},
        scratch_shapes=[
            pltpu.VMEM((NSLOPE * 64, ny), F32),
            pltpu.VMEM((4, lx + 16, ny), F32),
            pltpu.VMEM((4, lx, ny), F32),
        ],
        compiler_params=pltpu.CompilerParams(vmem_limit_bytes=16 * 2**20),
        cost_estimate=pl.CostEstimate(
            flops=25 * ysl.size, bytes_accessed=ysl.size // 2, transcendentals=0
        ),
        name="edge_moments",
    )(pad, keep, send, ysl, xl, xr, mean, after)
    return out[1:]


def picker(one, two=None):
    return lambda f: one[f] if f < FIRST else two[f - FIRST]


def storer(one, two=None):
    def put(f, v):
        if f < FIRST:
            one[f] = v
        else:
            two[f - FIRST] = v
    return put


def z_places(rows):
    zi = lax.axis_index("z")
    zn = lax.axis_size("z")
    return [pl.multiple_of(rows * lax.rem(zi + k, zn), 8) for k in (0, 1, zn - 1, 2)]


def core_base_kernel(count, keep, got, *outs):
    rows = outs[0].shape[1]
    for out, at in zip(outs, z_places(rows)):
        combine_base(
            lambda f, at=at: keep[f, pl.ds(at, rows), :],
            lambda f, at=at: got[f, pl.ds(at, rows), :],
            count, storer(out),
        )


def core_slope_kernel(count, keep1, got1, keep2, got2, dmat, *outs):
    rows = outs[0].shape[1]
    places = z_places(rows)

    def pick(one, two):
        def field(f):
            ref, k = (one, f) if f < FIRST else (two, f - FIRST)
            return jnp.concatenate([ref[k, pl.ds(at, rows), :] for at in places], axis=0)
        return field

    def put(f, v):
        for n, ref in enumerate(outs):
            ref[f - FIRST] = v[rows * n : rows * (n + 1)]

    combine_slopes(pick(keep1, keep2), pick(got1, got2), count, dmat[...], put)


def span_base_kernel(count, own, one, two, three, out, left, right):
    combine_base(picker(own), picker(one), count, storer(left))
    combine_base(picker(two), picker(three), count, storer(right))
    combine_base(picker(left), picker(right), 2 * count, storer(out))


def span_slope_kernel(count, *refs):
    base, (own, one, two, three) = refs[:4], refs[4:8]
    left1, right1, dmat, out, left, right = refs[8:]
    d = dmat[...]
    combine_slopes(picker(base[0], own), picker(base[1], one), count, d, storer(None, left))
    combine_slopes(picker(base[2], two), picker(base[3], three), count, d, storer(None, right))
    combine_slopes(
        picker(left1, left), picker(right1, right), 2 * count, d, storer(None, out)
    )


def last_base_kernel(count, mine, other, after, out, state):
    combine_base(picker(mine), picker(other), count, storer(state))
    scale = 1.0 / (2 * count)
    for c in range(3):
        out[c] = state[MEAN + c]
    for k in range(NBASE):
        out[3 + k] = state[UU + k] * scale


def last_slope_kernel(count, mine1, other1, mine2, other2, dmat, out, state):
    combine_slopes(
        picker(mine1, mine2), picker(other1, other2), count, dmat[...], storer(None, state)
    )
    scale = 1.0 / (2 * count)
    for k in range(6):
        out[k] = state[PG - FIRST + k] * (scale * lead)
        out[6 + k] = state[GG - FIRST + k] * (scale * lead * lead)
    for k in range(5):
        out[12 + k] = state[UG - FIRST + k] * (scale * lead)
    out[17] = state[PG - FIRST + 5] * (scale * lead)


def gather_kernel(after, *refs):
    ins, out = refs[:-1], refs[-1]
    rows = ins[0].shape[1]
    zi = lax.axis_index("z")
    zn = lax.axis_size("z")
    for step, ref in enumerate(ins):
        at = pl.multiple_of(rows * lax.rem(zi + zn - step, zn), 8)
        out[:, pl.ds(at, rows), :] = ref[...]


def place_kernel(*refs):
    ins, out, sems = refs[:-2], refs[-2], refs[-1]
    zi = lax.axis_index("z")
    zn = lax.axis_size("z")
    core = lax.axis_index(CA)
    copies = []
    for k, ref in enumerate(ins):
        fields, rows = ref.shape[:2]
        if k < 2:
            first, side, step = 0, k, None
            at = rows * (core if side == 0 else 1 - core)
        else:
            first = OUT - fields
            side, step = divmod(k - 2, zn)
            c = core if side == 0 else 1 - core
            at = rows * (zn * c + lax.rem(zi + zn - z_order[step], zn))
        at = pl.multiple_of(at, 8)
        copies.append(
            pltpu.make_async_copy(
                ref, out.at[pl.ds(first, fields), pl.ds(at, rows)], sems.at[k]
            )
        )
    copy_all(copies)


def place(pieces, shape):
    return pl.pallas_call(
        place_kernel,
        in_specs=[pl.BlockSpec(memory_space=pltpu.VMEM)] * len(pieces),
        out_specs=pl.BlockSpec(memory_space=pltpu.HBM),
        out_shape=pltpu.HBM(shape, F32),
        scratch_shapes=[pltpu.SemaphoreType.DMA((len(pieces),))],
        compiler_params=pltpu.CompilerParams(vmem_limit_bytes=4 * 2**20),
        name="place",
    )(*pieces)


def small_call(kernel, outs, scratch, name, *args):
    vm = pl.BlockSpec(memory_space=pltpu.VMEM)
    return pl.pallas_call(
        kernel,
        in_specs=[vm] * len(args),
        out_specs=[vm] * len(outs),
        out_shape=[pltpu.VMEM(s, F32) for s in outs],
        scratch_shapes=[pltpu.VMEM(s, F32) for s in scratch],
        compiler_params=pltpu.CompilerParams(vmem_limit_bytes=8 * 2**20),
        cost_estimate=pl.CostEstimate(flops=1000, bytes_accessed=1000, transcendentals=0),
        name=name,
    )(*args)


def send(value, axis, step):
    size = lax.axis_size(axis)
    return lax.ppermute(value, axis, [(i, (i + step) % size) for i in range(size)])


def shards(flow, dy):
    _, lx, lz, ny = flow.shape
    gn = lax.axis_size(GXA)
    zn = lax.axis_size("z")
    up = [(i, i + 1) for i in range(gn - 1)]
    down = [(i + 1, i) for i in range(gn - 1)]
    zs, xs = (3, lx, 4, ny), (4, 4, lz, ny)
    zl, zr, xl, xr = cut(rim_kernel, [zs, zs, xs, xs], 4, "rims", flow)
    with jax.named_scope("rim_exchange"):
        zl = send(zl, ZA, 1)
        zr = send(zr, ZA, -1)
        xl = lax.ppermute(xl, GXA, up)
        xr = lax.ppermute(xr, GXA, down)
    pad, mean, keep1, give1 = base_moments(flow)
    ysl, dmat = y_slopes(pad, dy)
    rows = lx // 2 // zn
    one_piece, two_piece = (FIRST, rows, ny), (STATE - FIRST, rows, ny)

    def along_z(own, up, down, far):
        return [own, send(far, "z", 2), send(up, "z", 1), send(down, "z", -1)]

    def spread(done):
        return [done] + [send(done, "z", k) for k in (1, 2, 3)]

    with jax.named_scope("base_core"):
        got1 = send(give1, CA, 1)
        parts1 = small_call(
            functools.partial(core_base_kernel, lz), [one_piece] * 4, [], "core_base", keep1, got1
        )
    with jax.named_scope("base_span"):
        pieces1 = along_z(*parts1)
    pad, keep2, give2 = inner_moments(pad, ysl, zl, zr, mean, parts1[0])
    with jax.named_scope("base_span"):
        part1, left1, right1 = small_call(
            functools.partial(span_base_kernel, 2 * lz), [one_piece] * 3, [], "span_base", *pieces1
        )
    with jax.named_scope("base_x"):
        other1 = send(part1, "xh", 1)
    keep2, give2 = edge_moments(pad, keep2, give2, ysl, xl, xr, mean, part1)
    with jax.named_scope("slope_core"):
        got2 = send(give2, CA, 1)
        parts2 = small_call(
            functools.partial(core_slope_kernel, lz), [two_piece] * 4, [], "core_slope",
            keep1, got1, keep2, got2, dmat,
        )
    with jax.named_scope("base_x"):
        (done1,) = small_call(
            functools.partial(last_base_kernel, 2 * zn * lz),
            [(FIRST - 1, rows, ny)], [one_piece], "last_base", part1, other1, parts2[0],
        )
    with jax.named_scope("base_spread"):
        spread1 = spread(done1)
    with jax.named_scope("slope_span"):
        pieces2 = along_z(*parts2)
        (part2,) = small_call(
            functools.partial(span_slope_kernel, 2 * lz), [two_piece], [two_piece] * 2,
            "span_slope", *pieces1, *pieces2, left1, right1, dmat,
        )
    with jax.named_scope("slope_x"):
        other2 = send(part2, "xh", 1)
        (done2,) = small_call(
            functools.partial(last_slope_kernel, 2 * zn * lz),
            [(OUT - FIRST + 1, rows, ny)], [two_piece], "last_slope",
            part1, other1, part2, other2, dmat,
        )
    with jax.named_scope("base_spread"):
        (half1,) = small_call(
            gather_kernel, [(FIRST - 1, lx // 2, ny)], [], "gather", done2, *spread1
        )
        all1 = [half1, send(half1, CA, 1)]
    with jax.named_scope("slope_spread"):
        all2 = [done2] + [send(done2, "z", k) for k in z_order[1:]]
        all2 = all2 + [send(v, CA, 1) for v in all2]
    return place(all1 + all2, (OUT, lx, ny))


def solution(mesh):
    gx, gz = mesh.shape["gx"], mesh.shape["gz"]
    fine = Mesh(mesh.devices.reshape(gx, 2, gz // 4, 2), (GXA,) + ZA)
    return jax.shard_map(
        shards,
        mesh=fine,
        in_specs=(P(None, GXA, ZA, None), P()),
        out_specs=P(None, GXA, None),
        check_vma=False,
    )
```
